32 devices in a mesh: section: 2 (over x), dp: 16 (over z, y, core).
Axes of the slice: x: 2, y: 2, z: 4, core: 2. Of those that a mesh axis runs over, the one named last changes fastest.
Arguments:
- patches: bfloat16 [32, 128, 768], P('dp'), may hold values from -6 to 6
- masks: int32 [32, 48, 128], P('dp'), may hold values from 0 to 1, as said below
- lead_times: int32 [32], P('dp'), may hold values from 6 to 168
- cotangent: bfloat16 [32, 128, 1024], P('dp'), may hold values from -6 to 6
- patch_weight: bfloat16 [768, 1024], replicated, may hold values from -1.5 to 1.5
- var_embed: bfloat16 [48, 1024], replicated, may hold values from -6 to 6
- attention: bfloat16 [2, 4, 1024, 1024], P('section')
- attn_vectors: bfloat16 [2, 4, 1024], P('section'), may hold values from -5 to 5
- norm_gains: bfloat16 [2, 1024], replicated, may hold values from 0.5 to 1.5
- trunk_shifts: bfloat16 [3, 1024], replicated, may hold values from -5 to 5
- mlp_in: bfloat16 [1024, 4096], replicated, may hold values from -0.1875 to 0.1875
- mlp_in_bias: bfloat16 [4096], replicated, may hold values from -3 to 3
- mlp_out: bfloat16 [4096, 1024], replicated, may hold values from -0.09375 to 0.09375
Outputs:
- activations: bfloat16 [2, 32, 128, 1024], P('section', 'dp')
- input_grad: float32 [32, 128, 768], P('dp', None, 'section')
- patch_weight_grad: float32 [768, 1024], P(('section', 'dp'))
- var_embed_grad: float32 [48, 1024], replicated
- attention_grad: float32 [2, 4096, 1024], P('section', 'dp')
- attn_vectors_grad: float32 [2, 4096], P('section', 'dp')
- norm_gains_grad: float32 [2, 1024], replicated
- trunk_shifts_grad: float32 [3, 1024], replicated
- mlp_in_grad: float32 [1024, 4096], P(None, ('section', 'dp'))
- mlp_in_bias_grad: float32 [4096], P(('section', 'dp'))
- mlp_out_grad: float32 [4096, 1024], P(('section', 'dp'))
The draws below stay inside these ranges and needn't reach their ends.
Inputs may be any that keep to these rules, and one draw needn't show every extreme that they name: `masks`: every cell of every sample has at least one present variable; the share of present variables differs from sample to sample.
All inputs are finite; a program needn't handle non-finite values.
Results may differ from the reference program's by a relative error of at most 0.015.
Values may be sent and summed in bfloat16 or wider, within the bound.
A program may use at most 384 MiB of HBM per device.

```python
import jax
import jax.numpy as jnp
from jax import lax

D = 1024
HEADS = 16
HEAD = 64
FF = 4096
V = 48
PIX = 16
SEQ = 128
SAMPLES = 32


def draw_attention(key, part):
    key = jax.random.fold_in(key, 11)
    base_draw = jax.random.normal(key, (2, 4, D, D), jnp.float32) * D ** (-0.5)
    boost = jnp.ones((2, 4, 1, 1), jnp.float32).at[1, 3].set(2.5)
    return (base_draw * boost).astype(jnp.bfloat16)


def draw_masks(key, part):
    key = jax.random.fold_in(key, 23)
    rate_key, roll_key, pick_key = jax.random.split(key, 3)
    keep_rate = jax.random.randint(rate_key, (SAMPLES, 1, 1), 15, 96)
    rolled = jax.random.randint(roll_key, (SAMPLES, V, SEQ), 0, 100)
    forced = jax.random.randint(pick_key, (SAMPLES, 1, SEQ), 0, V)
    variable_ids = jnp.arange(V, dtype=jnp.int32)[None, :, None]
    return jnp.where((rolled < keep_rate) | (variable_ids == forced), 1, 0).astype(jnp.int32)


def with_ends(entries, own_key, least, high):
    longest = entries.shape.index(max(entries.shape))
    spots = []
    for shift in (0, 1):
        where = [jax.random.randint(jax.random.fold_in(own_key, axis), (), 0, length) for axis, length in enumerate(entries.shape)]
        where[longest] = (where[longest] + shift) % entries.shape[longest]
        spots.append(tuple(where))
    return entries.at[spots[0]].set(least).at[spots[1]].set(high)


def steps_of(rng, extent, shards, least, high):
    level = 1.0
    for dim, shards_of in shards:
        steps = jax.random.uniform(jax.random.fold_in(jax.random.fold_in(rng, 6), dim), (shards_of,), jnp.float32, least / len(shards), high / len(shards))
        level = level * jnp.repeat(jnp.exp(steps), extent[dim] // shards_of).reshape((-1,) + (1,) * (len(extent) - 1 - dim))
    return level


def gaussian(own_key, extent, scale, most, shards=(), held_as=jnp.bfloat16):
    factor_of = steps_of(own_key, extent, shards, -0.22, 0.18) if shards else 1.0
    entries = jax.random.normal(own_key, extent, jnp.float32) * scale * factor_of
    return jnp.minimum(jnp.maximum(entries, -most), most).astype(held_as)


def setup_inputs(seed: int = 0) -> dict:
    streams_of = jax.random.split(jax.random.key(seed), 14)
    return {
        "patches": gaussian(streams_of[0], (SAMPLES, SEQ, V * PIX), 1.0, 6.0, ((0, 16),)),
        "masks": draw_masks(jax.random.fold_in(streams_of[13], 71), 0),
        "lead_times": with_ends(jax.random.randint(streams_of[2], (SAMPLES,), 6, 169), jax.random.fold_in(streams_of[2], 1), 6, 168).astype(jnp.int32),
        "cotangent": gaussian(streams_of[3], (SAMPLES, SEQ, D), 1.0, 6.0, ((0, 16),)),
        "patch_weight": gaussian(streams_of[4], (V * PIX, D), PIX ** -0.5, 1.5),
        "var_embed": gaussian(streams_of[5], (V, D), 1.0, 6.0),
        "attention": draw_attention(jax.random.fold_in(streams_of[13], 71), 0),
        "attn_vectors": gaussian(streams_of[7], (2, 4, D), 0.8, 5.0, ((0, 2),)),
        "norm_gains": jnp.clip(1.0 + 0.1 * jax.random.normal(streams_of[8], (2, D), jnp.float32), 0.5, 1.5).astype(jnp.bfloat16),
        "trunk_shifts": gaussian(streams_of[9], (3, D), 0.7, 5.0),
        "mlp_in": gaussian(streams_of[10], (D, FF), D ** -0.5, 0.1875),
        "mlp_in_bias": gaussian(streams_of[11], (FF,), 0.3, 3.0),
        "mlp_out": gaussian(streams_of[12], (FF, D), FF ** -0.5, 0.09375),
    }


EPSILON = 1e-05
MASKED = -1e+30
HIGHEST = lax.Precision.HIGHEST

@jax.custom_vjp
def low(v):
    return lax.optimization_barrier(v.astype(jnp.bfloat16)).astype(jnp.float32)

@jax.custom_vjp
def low_back(v):
    return v

def low_keep(v):
    return (low(v), None)

def low_pass(kept, grad):
    return (grad,)

def back_keep(v):
    return (v, None)

def back_low(kept, grad):
    return (low(grad),)
low.defvjp(low_keep, low_pass)
low_back.defvjp(back_keep, back_low)

def layer_norm(features, gain_row, shift_row):
    row_mean = lax.optimization_barrier(jnp.mean(features, axis=-1, keepdims=True))
    centred = features - row_mean
    spread = lax.optimization_barrier(jnp.mean(centred * centred, axis=-1, keepdims=True))
    return centred * lax.rsqrt(spread + EPSILON) * gain_row + shift_row

def layer_one(pixel_rows, valid_cells, patch_weight, var_embed, layer_weights, layer_vectors):
    score_scale = HEAD ** (-0.5)
    shaped = pixel_rows.reshape(SEQ, V, PIX)
    pieces = jnp.einsum('tvp,vpd->tvd', shaped, patch_weight.reshape(V, PIX, D), precision=HIGHEST)
    embedded = low(low_back(pieces) + var_embed[None])
    query_vec = jnp.dot(layer_vectors[0], layer_weights[0], precision=HIGHEST) + layer_vectors[1]
    folded = low(jnp.einsum('dhk,hk->dh', layer_weights[1].reshape(D, HEADS, HEAD), query_vec.reshape(HEADS, HEAD), precision=HIGHEST))
    scores = low_back(jnp.einsum('tvd,dh->tvh', embedded, folded, precision=HIGHEST) * score_scale)
    scores = jnp.where(valid_cells.T[:, :, None] > 0, scores, MASKED)
    weights = low(jax.nn.softmax(scores, axis=1))
    pooled = low(low_back(jnp.einsum('tvh,tvd->thd', weights, embedded, precision=HIGHEST)))
    projected = jnp.einsum('thd,dhk->thk', pooled, layer_weights[2].reshape(D, HEADS, HEAD), precision=HIGHEST).reshape(SEQ, D)
    values = low(low_back(projected) + layer_vectors[2])
    return low(low_back(jnp.dot(values, layer_weights[3], precision=HIGHEST) + layer_vectors[3]))

def layer_two(front_rows, lead_hours, layer_weights, layer_vectors, norm_gains, trunk_shifts, mlp_in, mlp_in_bias, mlp_out):
    score_scale = HEAD ** (-0.5)
    resid_in = front_rows + lead_hours.astype(jnp.float32) / 100.0 * trunk_shifts[2]
    normed = low(layer_norm(resid_in, norm_gains[0], trunk_shifts[0]))
    queries = low(low_back(jnp.dot(normed, layer_weights[0], precision=HIGHEST)) + layer_vectors[0]).reshape(SEQ, HEADS, HEAD)
    key_rows = low(low_back(jnp.dot(normed, layer_weights[1], precision=HIGHEST))).reshape(SEQ, HEADS, HEAD)
    value_rows = low(low_back(jnp.dot(normed, layer_weights[2], precision=HIGHEST)) + layer_vectors[1]).reshape(SEQ, HEADS, HEAD)
    scores = low_back(jnp.einsum('qhd,khd->hqk', queries, key_rows, precision=HIGHEST) * score_scale)
    attn_probs = low(jax.nn.softmax(scores, axis=-1))
    mixed_heads = low(low_back(jnp.einsum('hqk,khd->qhd', attn_probs, value_rows, precision=HIGHEST).reshape(SEQ, D)))
    resid_mid = resid_in + low_back(jnp.dot(mixed_heads, layer_weights[3], precision=HIGHEST)) + layer_vectors[2]
    normed_two = low(layer_norm(resid_mid, norm_gains[1], trunk_shifts[1]))
    hidden_pre = low_back(jnp.dot(normed_two, mlp_in, precision=HIGHEST)) + mlp_in_bias
    hidden_low = low(jax.nn.gelu(hidden_pre, approximate=False))
    return resid_mid + low_back(jnp.dot(hidden_low, mlp_out, precision=HIGHEST)) + layer_vectors[3]

def reference(patches, masks, lead_times, cotangent, patch_weight, var_embed, attention, attn_vectors, norm_gains, trunk_shifts, mlp_in, mlp_in_bias, mlp_out):

    def forward(pixels, p_weight, v_embed, attn_all, vec_all, gains, shifts, w_in, b_in, w_out):

        def one_sample(sample_items):
            pixel_rows, valid_cells, lead_hours = sample_items
            front_rows = layer_one(pixel_rows, valid_cells, p_weight, v_embed, attn_all[0], vec_all[0])
            final_rows = layer_two(front_rows, lead_hours, attn_all[1], vec_all[1], gains, shifts, w_in, b_in, w_out)
            return (front_rows, final_rows)
        return lax.map(jax.checkpoint(one_sample), (pixels, masks, lead_times))
    (fronts, finals), backward = jax.vjp(forward, patches.astype(jnp.float32), patch_weight.astype(jnp.float32), var_embed.astype(jnp.float32), attention.astype(jnp.float32), attn_vectors.astype(jnp.float32), norm_gains.astype(jnp.float32), trunk_shifts.astype(jnp.float32), mlp_in.astype(jnp.float32), mlp_in_bias.astype(jnp.float32), mlp_out.astype(jnp.float32))
    grads_all = backward((jnp.zeros_like(fronts), cotangent.astype(jnp.float32)))
    activations = jnp.stack([fronts, finals]).astype(jnp.bfloat16)
    return (activations, grads_all[0], grads_all[1], grads_all[2], grads_all[3].reshape(2, 4 * D, D), grads_all[4].reshape(2, 4 * D), grads_all[5], grads_all[6], grads_all[7], grads_all[8], grads_all[9])
```

```python
import functools

import jax
import jax.numpy as jnp
from jax import lax
from jax.experimental import pallas as pl
from jax.experimental.pallas import tpu as pltpu
from jax.sharding import PartitionSpec as P

D = 1024
HEADS = 16
HEAD = 64
FF = 4096
V = 48
PIX = 16


EPSILON = 1e-05
MASKED = -1e30
HIGHEST = lax.Precision.HIGHEST


def shortened(array):
    return jax.tree.map(lambda a: a.astype(jnp.bfloat16) if a.dtype == jnp.float32 else a, array)


def from_behind(value, axis, steps):
    count = lax.axis_size(axis)
    leading, last = (max(0, -steps), min(count, count - steps))
    return lax.ppermute(value, axis, [(source, source + steps) for source in range(leading, last)])


def layer_norm(features, gain_row, shift_row):
    row_mean = jnp.mean(features, axis=-1, keepdims=True)
    centred = features - row_mean
    spread = jnp.mean(centred * centred, axis=-1, keepdims=True)
    return centred * lax.rsqrt(spread + EPSILON) * gain_row + shift_row


def exact_gelu(inputs):
    return jax.nn.gelu(inputs, approximate=False)


def matmul(left_side, right_side):
    return jnp.dot(left_side, right_side, preferred_element_type=jnp.float32)


def matmul_tn(left_side, right_side):
    return lax.dot_general(
        left_side, right_side, (((0,), (0,)), ((), ())), preferred_element_type=jnp.float32
    )


def matmul_nt(left_side, right_side):
    return lax.dot_general(
        left_side, right_side, (((1,), (1,)), ((), ())), preferred_element_type=jnp.float32
    )


def updated(carried, changes):
    merged = dict(carried)
    merged.update(changes)
    return merged


def query_terms(layer_weights, layer_vectors):
    query_vec = matmul(layer_vectors[0][None, :], layer_weights[0])[0] + layer_vectors[1].astype(
        jnp.float32
    )
    key_wide = layer_weights[1].astype(jnp.float32).reshape(D, HEADS, HEAD)
    folded = jnp.einsum("dhk,hk->dh", key_wide, query_vec.reshape(HEADS, HEAD), precision=HIGHEST)
    return (query_vec, key_wide, folded)


def embed_block(pixel_rows, valid_cells, patch_weight, var_embed, folded_low, score_scale):
    cell_count = pixel_rows.shape[0]
    shaped = pixel_rows.reshape(cell_count, V, PIX)
    pieces = jnp.einsum(
        "tvp,vpd->tvd", shaped, patch_weight.reshape(V, PIX, D), preferred_element_type=jnp.float32
    )
    embedded = (pieces + var_embed.astype(jnp.float32)[None]).astype(jnp.bfloat16)
    scores = (
        jnp.einsum("tvd,dh->tvh", embedded, folded_low, preferred_element_type=jnp.float32)
        * score_scale
    )
    scores = jnp.where(valid_cells[:, :, None] > 0, scores, MASKED)
    weights = jax.nn.softmax(scores, axis=1)
    weights_low = weights.astype(jnp.bfloat16)
    pooled = jnp.einsum(
        "tvh,tvd->thd", weights_low, embedded, preferred_element_type=jnp.float32
    ).astype(jnp.bfloat16)
    return (shaped, embedded, weights, weights_low, pooled)


def pool_values(pooled, layer_weights, layer_vectors):
    cell_count = pooled.shape[0]
    projected = jnp.einsum(
        "thd,dhk->thk",
        pooled,
        layer_weights[2].reshape(D, HEADS, HEAD),
        preferred_element_type=jnp.float32,
    )
    return (projected.reshape(cell_count, D) + layer_vectors[2].astype(jnp.float32)).astype(
        jnp.bfloat16
    )


def front_block_back(
    pixel_rows,
    valid_cells,
    d_out,
    patch_weight,
    var_embed,
    layer_weights,
    layer_vectors,
    folded_low,
    score_scale,
):
    shaped, embedded, weights, weights_low, pooled = embed_block(
        pixel_rows, valid_cells, patch_weight, var_embed, folded_low, score_scale
    )
    values_low = pool_values(pooled, layer_weights, layer_vectors)
    cell_count = pixel_rows.shape[0]
    g_bo = jnp.sum(d_out.astype(jnp.float32), axis=0)
    g_wo = matmul_tn(values_low, d_out)
    d_values = matmul_nt(d_out, layer_weights[3])
    g_bv = jnp.sum(d_values, axis=0)
    d_values_low = d_values.astype(jnp.bfloat16).reshape(cell_count, HEADS, HEAD)
    g_wv = jnp.einsum(
        "thd,thk->dhk", pooled, d_values_low, preferred_element_type=jnp.float32
    ).reshape(D, D)
    d_pooled = jnp.einsum(
        "thk,dhk->thd",
        d_values_low,
        layer_weights[2].reshape(D, HEADS, HEAD),
        preferred_element_type=jnp.float32,
    ).astype(jnp.bfloat16)
    d_weights = jnp.einsum("thd,tvd->tvh", d_pooled, embedded, preferred_element_type=jnp.float32)
    d_embedded = jnp.einsum(
        "tvh,thd->tvd", weights_low, d_pooled, preferred_element_type=jnp.float32
    )
    d_scores = (weights * (d_weights - jnp.sum(weights * d_weights, axis=1, keepdims=True))).astype(
        jnp.bfloat16
    )
    g_folded = (
        jnp.einsum("tvd,tvh->dh", embedded, d_scores, preferred_element_type=jnp.float32)
        * score_scale
    )
    d_embedded = (
        d_embedded
        + jnp.einsum("tvh,dh->tvd", d_scores, folded_low, preferred_element_type=jnp.float32)
        * score_scale
    )
    g_var = jnp.sum(d_embedded, axis=0)
    d_embedded_low = d_embedded.astype(jnp.bfloat16)
    g_patch = jnp.einsum(
        "tvp,tvd->vpd", shaped, d_embedded_low, preferred_element_type=jnp.float32
    ).reshape(V * PIX, D)
    d_pixels = jnp.einsum(
        "tvd,vpd->tvp",
        d_embedded_low,
        patch_weight.reshape(V, PIX, D),
        preferred_element_type=jnp.float32,
    ).reshape(cell_count, V * PIX)
    return (g_wv, g_wo, g_bv, g_bo, g_folded, g_var, g_patch, d_pixels)


def layer_two(
    x_in,
    lead_hours,
    d_out,
    layer_weights,
    layer_vectors,
    norm_gains,
    trunk_shifts,
    mlp_in,
    mlp_in_bias,
    mlp_out,
):
    seq_len = x_in.shape[0]
    score_scale = HEAD ** (-0.5)
    gain_rows = norm_gains.astype(jnp.float32)
    shift_rows = trunk_shifts.astype(jnp.float32)
    vec_rows = layer_vectors.astype(jnp.float32)
    lead_scale = lead_hours.astype(jnp.float32) / 100.0
    resid_in = x_in.astype(jnp.float32) + lead_scale * shift_rows[2]
    normed, first_back = jax.vjp(layer_norm, resid_in, gain_rows[0], shift_rows[0])
    normed_low = normed.astype(jnp.bfloat16)
    queries = (
        (matmul(normed_low, layer_weights[0]) + vec_rows[0])
        .astype(jnp.bfloat16)
        .reshape(seq_len, HEADS, HEAD)
    )
    key_rows = (
        matmul(normed_low, layer_weights[1]).astype(jnp.bfloat16).reshape(seq_len, HEADS, HEAD)
    )
    value_rows = (
        (matmul(normed_low, layer_weights[2]) + vec_rows[1])
        .astype(jnp.bfloat16)
        .reshape(seq_len, HEADS, HEAD)
    )
    scores = (
        jnp.einsum("qhd,khd->hqk", queries, key_rows, preferred_element_type=jnp.float32)
        * score_scale
    )
    attn_probs = jax.nn.softmax(scores, axis=-1)
    probs_low = attn_probs.astype(jnp.bfloat16)
    mixed_heads = (
        jnp.einsum("hqk,khd->qhd", probs_low, value_rows, preferred_element_type=jnp.float32)
        .reshape(seq_len, D)
        .astype(jnp.bfloat16)
    )
    resid_mid = resid_in + matmul(mixed_heads, layer_weights[3]) + vec_rows[2]
    normed_two, second_back = jax.vjp(layer_norm, resid_mid, gain_rows[1], shift_rows[1])
    normed_two_low = normed_two.astype(jnp.bfloat16)
    hidden_pre = matmul(normed_two_low, mlp_in) + mlp_in_bias.astype(jnp.float32)
    hidden, gelu_back = jax.vjp(exact_gelu, hidden_pre)
    hidden_low = hidden.astype(jnp.bfloat16)
    produced = (resid_mid + matmul(hidden_low, mlp_out) + vec_rows[3]).astype(jnp.bfloat16)
    d_final = d_out.astype(jnp.float32)
    g_b2 = jnp.sum(d_final, axis=0)
    g_wout = matmul_tn(hidden_low, d_out)
    d_hidden = matmul_nt(d_out, mlp_out)
    d_pre = gelu_back(d_hidden)[0]
    g_bin = jnp.sum(d_pre, axis=0)
    d_pre_low = d_pre.astype(jnp.bfloat16)
    g_win = matmul_tn(normed_two_low, d_pre_low)
    d_mid_norm, g_gain_two, g_shift_two = second_back(matmul_nt(d_pre_low, mlp_in))
    d_mid = d_final + d_mid_norm
    g_bo = jnp.sum(d_mid, axis=0)
    d_mid_low = d_mid.astype(jnp.bfloat16)
    g_wo = matmul_tn(mixed_heads, d_mid_low)
    d_mixed = (
        matmul_nt(d_mid_low, layer_weights[3]).astype(jnp.bfloat16).reshape(seq_len, HEADS, HEAD)
    )
    d_probs = jnp.einsum("qhd,khd->hqk", d_mixed, value_rows, preferred_element_type=jnp.float32)
    d_values = jnp.einsum(
        "hqk,qhd->khd", probs_low, d_mixed, preferred_element_type=jnp.float32
    ).reshape(seq_len, D)
    d_scores = (
        attn_probs * (d_probs - jnp.sum(attn_probs * d_probs, axis=-1, keepdims=True))
    ).astype(jnp.bfloat16)
    d_queries = (
        jnp.einsum("hqk,khd->qhd", d_scores, key_rows, preferred_element_type=jnp.float32).reshape(
            seq_len, D
        )
        * score_scale
    )
    d_keys = (
        jnp.einsum("hqk,qhd->khd", d_scores, queries, preferred_element_type=jnp.float32).reshape(
            seq_len, D
        )
        * score_scale
    )
    g_bq = jnp.sum(d_queries, axis=0)
    g_bv = jnp.sum(d_values, axis=0)
    d_queries_low = d_queries.astype(jnp.bfloat16)
    d_keys_low = d_keys.astype(jnp.bfloat16)
    d_values_low = d_values.astype(jnp.bfloat16)
    g_wq = matmul_tn(normed_low, d_queries_low)
    g_wk = matmul_tn(normed_low, d_keys_low)
    g_wv = matmul_tn(normed_low, d_values_low)
    d_normed = (
        matmul_nt(d_queries_low, layer_weights[0])
        + matmul_nt(d_keys_low, layer_weights[1])
        + matmul_nt(d_values_low, layer_weights[2])
    )
    d_in_norm, g_gain_one, g_shift_one = first_back(d_normed)
    d_in = d_mid + d_in_norm
    g_lead = lead_scale * jnp.sum(d_in, axis=0)
    return (
        produced,
        d_in.astype(jnp.bfloat16),
        jnp.stack([g_wq, g_wk, g_wv, g_wo]),
        jnp.stack([g_bq, g_bv, g_bo, g_b2]),
        jnp.stack([g_gain_one, g_gain_two]),
        jnp.stack([g_shift_one, g_shift_two, g_lead]),
        g_win,
        g_bin,
        g_wout,
    )


def send_forward(sent_rows):
    return from_behind(shortened(sent_rows), "section", 1).astype(sent_rows.dtype)


def shards(
    patches,
    masks,
    lead_times,
    cotangent,
    patch_weight,
    var_embed,
    attention,
    attn_vectors,
    norm_gains,
    trunk_shifts,
    mlp_in,
    mlp_in_bias,
    mlp_out,
):
    micro_count, seq_len, pixel_width = patches.shape
    block_rows = min(128, seq_len)
    score_scale = HEAD ** (-0.5)
    layer_weights = attention[0]
    layer_vectors = attn_vectors[0]
    on_front = lax.axis_index("section") == 0
    empty_rows = jnp.zeros((seq_len, D), jnp.bfloat16)
    carried = {
        "attn": jnp.zeros((4, D, D), jnp.float32),
        "vec": jnp.zeros((4, D), jnp.float32),
        "u_sum": jnp.zeros((D, HEADS), jnp.float32),
        "patch": jnp.zeros((V * PIX, D), jnp.float32),
        "var": jnp.zeros((V, D), jnp.float32),
        "gains": jnp.zeros((2, D), jnp.float32),
        "shifts": jnp.zeros((3, D), jnp.float32),
        "w_in": jnp.zeros((D, FF), jnp.float32),
        "b_in": jnp.zeros((FF,), jnp.float32),
        "w_out": jnp.zeros((FF, D), jnp.float32),
        "outputs": jnp.zeros((micro_count, seq_len, D), jnp.bfloat16),
        "pixels": jnp.zeros((micro_count, seq_len, pixel_width), jnp.float32),
        "returned": jnp.zeros((micro_count, seq_len, D), jnp.bfloat16),
    }

    def front_forward(carried, mb_index):
        query_vec, key_wide, folded = query_terms(layer_weights, layer_vectors)
        folded_low = folded.astype(jnp.bfloat16)
        valid_cells = masks[mb_index, :, 0:block_rows].T
        block_parts = embed_block(
            patches[mb_index, 0:block_rows],
            valid_cells,
            patch_weight,
            var_embed,
            folded_low,
            score_scale,
        )
        values_low = pool_values(block_parts[4], layer_weights, layer_vectors)
        pieces = [
            (matmul(values_low, layer_weights[3]) + layer_vectors[3].astype(jnp.float32)).astype(
                jnp.bfloat16
            )
        ]
        produced = jnp.concatenate(pieces, axis=0)
        return (
            updated(carried, {"outputs": carried["outputs"].at[mb_index].set(produced)}),
            produced,
        )

    def front_backward(carried, mb_index, d_front):
        query_vec, key_wide, folded = query_terms(layer_weights, layer_vectors)
        folded_low = folded.astype(jnp.bfloat16)
        attn_sum = carried["attn"]
        vec_sum = carried["vec"]
        u_total = carried["u_sum"]
        var_total = carried["var"]
        patch_total = carried["patch"]
        valid_cells = masks[mb_index, :, 0:block_rows].T
        block_grads = front_block_back(
            patches[mb_index, 0:block_rows],
            valid_cells,
            d_front[0:block_rows],
            patch_weight,
            var_embed,
            layer_weights,
            layer_vectors,
            folded_low,
            score_scale,
        )
        attn_sum = attn_sum.at[2].add(block_grads[0]).at[3].add(block_grads[1])
        vec_sum = vec_sum.at[2].add(block_grads[2]).at[3].add(block_grads[3])
        u_total = u_total + block_grads[4]
        var_total = var_total + block_grads[5]
        patch_total = patch_total + block_grads[6]
        pixel_pieces = [block_grads[7]]
        pixel_grads = carried["pixels"].at[mb_index].set(jnp.concatenate(pixel_pieces, axis=0))
        return updated(
            carried,
            {
                "attn": attn_sum,
                "vec": vec_sum,
                "u_sum": u_total,
                "var": var_total,
                "patch": patch_total,
                "pixels": pixel_grads,
            },
        )

    def back_step(carried, mb_index, arriving):
        produced, d_front, attn_part, vec_part, gain_part, shift_part, g_win, g_bin, g_wout = (
            layer_two(
                arriving,
                lead_times[mb_index],
                cotangent[mb_index],
                layer_weights,
                layer_vectors,
                norm_gains,
                trunk_shifts,
                mlp_in,
                mlp_in_bias,
                mlp_out,
            )
        )
        changes = {
            "attn": carried["attn"] + attn_part,
            "vec": carried["vec"] + vec_part,
            "gains": carried["gains"] + gain_part,
            "shifts": carried["shifts"] + shift_part,
            "w_in": carried["w_in"] + g_win,
            "b_in": carried["b_in"] + g_bin,
            "w_out": carried["w_out"] + g_wout,
            "outputs": carried["outputs"].at[mb_index].set(produced),
            "returned": carried["returned"].at[mb_index].set(d_front),
        }
        return (updated(carried, changes), d_front)

    def finish_front(carried):
        query_vec, key_wide, folded = query_terms(layer_weights, layer_vectors)
        u_total = carried["u_sum"]
        d_key = (u_total[:, :, None] * query_vec.reshape(HEADS, HEAD)[None]).reshape(D, D)
        d_query_vec = jnp.einsum("dh,dhk->hk", u_total, key_wide, precision=HIGHEST).reshape(D)
        d_query_weight = layer_vectors[0].astype(jnp.float32)[:, None] * d_query_vec[None, :]
        d_query = jnp.dot(layer_weights[0].astype(jnp.float32), d_query_vec, precision=HIGHEST)
        attn_sum = carried["attn"].at[0].set(d_query_weight).at[1].set(d_key)
        vec_sum = carried["vec"].at[0].set(d_query).at[1].set(d_query_vec)
        return updated(carried, {"attn": attn_sum, "vec": vec_sum})

    arriving_act = empty_rows
    for step_number in range(micro_count + 1):

        def front_turn(inputs, step_number=step_number):
            carried, act_in = inputs
            sent_rows = empty_rows
            if step_number < micro_count:
                carried, sent_rows = front_forward(carried, step_number)
            return (carried, sent_rows)

        def back_turn(inputs, step_number=step_number):
            carried, act_in = inputs
            if step_number >= 1:
                carried, returned_rows = back_step(carried, step_number - 1, act_in)
            return (carried, empty_rows)

        carried, sent_act = lax.cond(on_front, front_turn, back_turn, (carried, arriving_act))
        if step_number < micro_count:
            arriving_act = send_forward(sent_act)
    gradients_back = from_behind(shortened(carried["returned"]), "section", -1)

    def front_all(kept_state):
        for mb_index in range(micro_count):
            kept_state = front_backward(kept_state, mb_index, gradients_back[mb_index])
        return kept_state

    carried = lax.cond(on_front, front_all, lambda kept_state: kept_state, carried)
    carried = lax.cond(on_front, finish_front, lambda kept_state: kept_state, carried)
    attn_grads, vec_grads = (
        lax.psum_scatter(
            carried["attn"].reshape(1, 4 * D, D), "dp", scatter_dimension=1, tiled=True
        ),
        lax.psum_scatter(carried["vec"].reshape(1, 4 * D), "dp", scatter_dimension=1, tiled=True),
    )
    win_grads, bin_grads, wout_grads, patch_grads = (
        lax.psum_scatter(carried["w_in"], ("section", "dp"), scatter_dimension=1, tiled=True),
        lax.psum_scatter(carried["b_in"], ("section", "dp"), scatter_dimension=0, tiled=True),
        lax.psum_scatter(carried["w_out"], ("section", "dp"), scatter_dimension=0, tiled=True),
        lax.psum_scatter(carried["patch"], ("section", "dp"), scatter_dimension=0, tiled=True),
    )
    var_grads, gain_grads, shift_grads = lax.psum(
        (carried["var"], carried["gains"], carried["shifts"]), ("section", "dp")
    )
    pixel_half = pixel_width // 2
    moved = from_behind(shortened(carried["pixels"][:, :, pixel_half:]), "section", 1)
    input_grads = jnp.where(on_front, carried["pixels"][:, :, :pixel_half], moved)
    activations = carried["outputs"][None]
    return (
        activations,
        input_grads,
        patch_grads,
        var_grads,
        attn_grads,
        vec_grads,
        gain_grads,
        shift_grads,
        win_grads,
        bin_grads,
        wout_grads,
    )


F32 = jnp.float32
BF = jnp.bfloat16
I32 = jnp.int32
MESH = pl.DeviceIdType.MESH
CELLS = 256
SLOT = 64
WIDE = 1152
LANES = 128
SCALE = 0.125
ROOT_HALF = 0.7071067811865476
ROOT_TAU = 0.3989422804014327


def nn(a, b):
    return jnp.dot(a, b, preferred_element_type=F32)


def nt(a, b):
    return lax.dot_general(a, b, (((1,), (1,)), ((), ())), preferred_element_type=F32)


def tn(a, b):
    return lax.dot_general(a, b, (((0,), (0,)), ((), ())), preferred_element_type=F32)


def at(start, size):
    if isinstance(start, int):
        return pl.ds(start, size)
    return pl.ds(pl.multiple_of(start, size), size)


def each(count, body):
    def step(index, carry):
        body(index)
        return carry

    lax.fori_loop(0, count, step, 0)


def iota(shape, dim):
    return lax.broadcasted_iota(I32, shape, dim)


def halves(value):
    high = value.astype(BF)
    return high, (value - high.astype(F32)).astype(BF)


def pixel_column(slot):
    return ((slot & (SLOT - 1)) << 4) + (slot >> 6)


def slot_tile(index, rows, columns):
    match = pixel_column(iota((rows, 1), 0) + index * rows)
    return jnp.where(iota((rows, columns), 1) == match, 1.0, 0.0).astype(BF)


def spread(tile):
    return jnp.concatenate([tile] * (WIDE // LANES), axis=1)


def front_tables(r):
    def place(index):
        tile = slot_tile(index, 256, V * PIX)
        r.table[at(index * 256, 256), :] = nn(tile, r.raw[...]).astype(BF)
        r.pat[:, at(index * 256, 256)] = nt(r.pix[...], tile).astype(BF)

    each(4, place)
    r.table[1024:1072, :] = r.embed[...]
    r.table[1072:WIDE, :] = jnp.zeros((WIDE - 1072, D), BF)
    lane = iota((CELLS, LANES), 1)
    r.pat[:, 1024:WIDE] = jnp.where(lane < V, 1.0, 0.0).astype(BF)
    twice = jnp.where(iota((V, LANES), 1) & (SLOT - 1) == iota((V, LANES), 0), 1.0, 0.0).astype(BF)
    for sample in range(2):
        present = tn(r.masks[sample].astype(F32).astype(BF), twice)
        r.keep[sample * 128 : sample * 128 + 128, :] = present


def front_query(r):
    first = jnp.broadcast_to(r.vecs[0:1, :], (16, D))
    query = nn(first, r.attn[0])[0:1, :] + r.vecs[1:2, :].astype(F32)
    own = iota((HEADS, D), 1) >> 6 == iota((HEADS, D), 0)
    high, low = halves(jnp.where(own, jnp.broadcast_to(query, (HEADS, D)), 0.0))
    r.qhead[0:HEADS, :] = high
    r.qhead[HEADS : 2 * HEADS, :] = low
    both = nt(r.qhead[...], r.attn[1])
    folded = (both[0:HEADS] + both[HEADS : 2 * HEADS]).astype(BF)
    r.fold[...] = folded
    r.score[...] = nt(folded, r.table[...]) * SCALE


def front_values(r):
    def tile(index):
        lanes = at(index * 256, 256)
        r.mid[:, lanes] = nn(r.table[...], r.attn[2, :, lanes]).astype(BF)

    each(4, tile)


def front_scores(r, head):
    row = r.score[pl.ds(head, 1), :]
    total = None
    for k in range(WIDE // LANES):
        part = r.pat[:, k * LANES : (k + 1) * LANES].astype(F32) * row[:, k * LANES : (k + 1) * LANES]
        total = part if total is None else total + part
    total = total + pltpu.roll(total, SLOT, 1)
    total = jnp.where(r.keep[...] > 0.5, total, MASKED)
    top = jnp.max(total, axis=1, keepdims=True)
    grown = jnp.exp(total - top)
    return grown / (0.5 * jnp.sum(grown, axis=1, keepdims=True))


def front_forward(r, out):
    first_half = iota((CELLS, LANES), 1) < HEAD

    def pair(index):
        lanes = at(index * LANES, LANES)
        found = []
        for part in range(2):
            head = index * 2 + part
            weights = front_scores(r, head)
            r.probs[at(head * 2, 2)] = weights.reshape(2, 128, LANES)
            pooled = r.pat[...] * spread(weights.astype(BF))
            found.append(nn(pooled, r.mid[:, lanes]))
        values = jnp.where(first_half, found[0], found[1]) + r.vecs[2:3, lanes].astype(F32)
        r.agg[:, lanes] = values.astype(BF)

    each(HEADS // 2, pair)

    def tile(index):
        lanes = at(index * 256, 256)
        out[:, lanes] = (nn(r.agg[...], r.attn[3, :, lanes]) + r.vecs[3:4, lanes].astype(F32)).astype(BF)

    each(4, tile)


def front_back_values(r, d_out):
    def tile(index):
        rows = at(index * 256, 256)
        grad = nt(d_out[...], r.attn[3, rows, :])
        r.small[64:65, rows] = jnp.sum(grad, axis=0, keepdims=True)
        r.small[65:66, rows] = jnp.sum(d_out[:, rows].astype(F32), axis=0, keepdims=True)
        r.dlow[:, rows] = grad.astype(BF)

    each(4, tile)
    r.turn_a[...] = r.dlow[...].T


def front_back_heads(r):
    first_half = iota((CELLS, LANES), 1) < HEAD
    r.input_sum[...] = jnp.zeros((CELLS, D), F32)

    def pair(index):
        lanes = at(index * LANES, LANES)
        grads = r.dlow[:, lanes]
        mid = r.mid[:, lanes]
        for part in range(2):
            head = index * 2 + part
            mine = first_half if part == 0 else jnp.logical_not(first_half)
            own = jnp.where(mine, grads, jnp.zeros_like(grads))
            weights = r.probs[at(head * 2, 2)].reshape(CELLS, LANES)
            low = weights.astype(BF)
            lowf = low.astype(F32)
            total = None
            for k in range(WIDE // 384):
                wide = nt(own, mid[k * 384 : (k + 1) * 384, :])
                for j in range(3):
                    n = k * 3 + j
                    cols = slice(n * LANES, (n + 1) * LANES)
                    piece = wide[:, j * LANES : (j + 1) * LANES]
                    term = piece * r.pat[:, cols].astype(F32)
                    total = term if total is None else total + term
                    if n < 8:
                        r.input_sum[:, cols] = r.input_sum[:, cols] + lowf * piece
            total = total + pltpu.roll(total, SLOT, 1)
            inner = 0.5 * jnp.sum(weights * total, axis=1, keepdims=True)
            d_score = (weights * (total - inner)).astype(BF).astype(F32)
            row = r.score[pl.ds(head, 1), :]
            for n in range(9):
                cols = slice(n * LANES, (n + 1) * LANES)
                if n < 8:
                    r.input_sum[:, cols] = r.input_sum[:, cols] + d_score * row[:, cols]
                r.uses[head, :, cols] = SCALE * jnp.sum(
                    d_score * r.pat[:, cols].astype(F32), axis=0, keepdims=True
                )
            pooled = r.pat[...] * spread(low)
            r.turned[at(head * HEAD, HEAD), :] = nn(r.turn_a[at(head * HEAD, HEAD), :], pooled).astype(BF)

    each(HEADS // 2, pair)


def put_front(r, which, quarter, value):
    y, c = quarter // 2, quarter % 2
    for j in range(2):
        r.grads[which * 2 + j, at((c * 2 + y) * 128, 128), :] = value[j * 128 : (j + 1) * 128].astype(BF)


def front_back_out(r, d_out):
    r.turn_b[...] = r.agg[...].T

    def tile(index):
        put_front(r, 1, index, nn(r.turn_b[at(index * 256, 256), :], d_out[...]))

    each(4, tile)


def front_back_table(r):
    uses = jnp.concatenate([r.uses[h] for h in range(HEADS)], axis=0).astype(BF)
    r.small[48:64, :] = nn(uses, r.table[...])
    r.mid[...] = r.turned[...].T


def front_back_projection(r):
    def values(index):
        rows = at(index * 256, 256)
        put_front(r, 0, index, tn(r.table[:, rows], r.mid[...]))

    each(4, values)


def front_back_pixels(r):
    uses = jnp.concatenate([r.uses[h] for h in range(HEADS)], axis=0).astype(BF)

    def pixels(index):
        lanes = at(index * 256, 256)
        full = nt(r.mid[...], r.attn[2, lanes, :]) + tn(uses, r.fold[:, lanes])
        r.turned[:, lanes] = full[0:1024].astype(BF)
        r.small[0:48, lanes] = full[1024:1072]

    each(4, pixels)


def front_back_order(r):
    def order(index):
        row = iota((256, 1), 0) + index * 256
        piece, k = row // 48, row % 48
        owner = ((piece & 1) * 2 + ((piece >> 1) & 1)) * 4 + ((piece >> 2) & 1) * 2 + (piece >> 3)
        natural = owner * 24 + jnp.where(k < 24, k, k + 360)
        slot = (natural & (PIX - 1)) * SLOT + (natural >> 4)
        pick = jnp.where(iota((256, D), 1) == slot, 1.0, 0.0).astype(BF)
        r.patch_sum[at(index * 256, 256), :] = nn(pick, r.turned[:, 0:1024]).astype(BF)

    each(3, order)


def front_back_inputs(r, own_half, other_half):
    low = r.input_sum[...].astype(BF)
    r.dlow[...] = low
    for half, out in ((0, own_half), (1, other_half)):
        column = pixel_column(iota((D, 1), 0)) - half * 384
        pick = jnp.where(iota((D, 384), 1) == column, 1.0, 0.0).astype(BF)
        out[...] = nn(r.dlow[...], pick).astype(out.dtype)


def row_mean(x):
    return jnp.mean(x, axis=1, keepdims=True)


def col_sum(x):
    return jnp.sum(x, axis=0, keepdims=True)


def trunk_ahead(r):
    def tile(index):
        n, k = index // 4, index % 4
        rows = at(k * 256, 256)
        r.grads[n, 0:256, rows] = nt(r.cot[...], r.bufs[1, n, rows, :]).astype(BF)

    each(16, tile)
    r.small[3:4, :] = col_sum(r.cot[...].astype(F32))


def normalise(r, source, spread_rows, unit, gain, shift, out):
    def rows_of(index):
        rows = at(index * 64, 64)
        x = source[rows, :]
        centred = x - row_mean(x)
        rstd = lax.rsqrt(row_mean(centred * centred) + EPSILON)
        scaled = centred * rstd
        unit[rows, :] = scaled
        spread_rows[rows, :] = jnp.broadcast_to(rstd, (64, LANES))
        out[rows, :] = (scaled * gain + shift).astype(BF)

    each(4, rows_of)


def trunk_attention(r, front):
    shift_rows = r.shifts[...].astype(F32)
    gain_rows = r.gains[...].astype(F32)

    def enter(index):
        rows = at(index * 128, 128)
        lead = r.leads[index].astype(F32) / 100.0
        r.resid[rows, :] = front[rows, :].astype(F32) + lead * shift_rows[2:3]

    each(2, enter)
    normalise(r, r.resid, r.rstd_one, r.unit_one, gain_rows[0:1], shift_rows[0:1], r.normed)

    def project(index):
        lanes = at(index * 256, 256)
        x = r.normed[...]
        r.q[:, lanes] = (nn(x, r.attn[0, :, lanes]) + r.vecs[0:1, lanes].astype(F32)).astype(BF)
        r.k[:, lanes] = nn(x, r.attn[1, :, lanes]).astype(BF)
        r.v[:, lanes] = (nn(x, r.attn[2, :, lanes]) + r.vecs[1:2, lanes].astype(F32)).astype(BF)

    each(4, project)
    first = iota((128, LANES), 1) < HEAD

    def pair(index):
        sample, hp = index // 8, index % 8
        rows, lanes = at(sample * 128, 128), at(hp * LANES, LANES)
        q, k, v = r.q[rows, lanes], r.k[rows, lanes], r.v[rows, lanes]
        none = jnp.zeros_like(q)
        mixed = None
        for part in range(2):
            mine = first if part == 0 else jnp.logical_not(first)
            scores = nt(jnp.where(mine, q, none), k) * SCALE
            grown = jnp.exp(scores - jnp.max(scores, axis=1, keepdims=True))
            probs = grown / jnp.sum(grown, axis=1, keepdims=True)
            r.probs[index * 2 + part] = probs
            term = nn(probs.astype(BF), jnp.where(mine, v, none))
            mixed = term if mixed is None else mixed + term
        r.mixed[rows, lanes] = mixed.astype(BF)

    each(16, pair)

    def leave(index):
        lanes = at(index * 256, 256)
        grown = nn(r.mixed[...], r.attn[3, :, lanes]) + r.vecs[2:3, lanes].astype(F32)
        r.resid[:, lanes] = r.resid[:, lanes] + grown

    each(4, leave)
    normalise(r, r.resid, r.rstd_two, r.unit_two, gain_rows[1:2], shift_rows[1:2], r.second)


def curve(x):
    area = 0.5 + 0.5 * lax.erf(x * ROOT_HALF)
    return x * area, area + x * (ROOT_TAU * jnp.exp(-0.5 * x * x))


def trunk_hidden(r):
    def tile(index):
        n, k = index // 4, index % 4
        lanes = at(k * 256, 256)
        pre = nn(r.second[...], r.bufs[0, n, :, lanes]) + r.bias[n, :, lanes].astype(F32)
        value, slope = curve(pre)
        r.grads[n, 256:512, lanes] = value.astype(BF)
        r.grads[n, 0:256, lanes] = (r.grads[n, 0:256, lanes].astype(F32) * slope).astype(BF)

    each(16, tile)

    def back(index):
        rows = at(index * 256, 256)
        total = None
        for n in range(4):
            term = nt(r.grads[n, 0:256, :], r.bufs[0, n, rows, :])
            total = term if total is None else total + term
        r.d_mid[:, rows] = total

    each(4, back)


def norm_back(grad, unit, rstd, gain):
    scaled = grad * gain
    along = row_mean(scaled * unit)
    return rstd * (scaled - row_mean(scaled) - unit * along)


def trunk_back(r, d_in):
    gain_rows = r.gains[...].astype(F32)
    shift_rows = r.shifts[...].astype(F32)
    r.small[2:3, :] = jnp.zeros((1, D), F32)
    r.small[4:9, :] = jnp.zeros((5, D), F32)

    def second(index):
        rows = at(index * 64, 64)
        grad, unit = r.d_mid[rows, :], r.unit_two[rows, :]
        mid = r.cot[rows, :].astype(F32) + norm_back(grad, unit, r.rstd_two[rows, 0:1], gain_rows[1:2])
        r.d_mid[rows, :] = mid
        r.d_low[rows, :] = mid.astype(BF)
        r.small[2:3, :] += col_sum(mid)
        r.small[5:6, :] += col_sum(grad * unit)
        r.small[7:8, :] += col_sum(grad)

    each(4, second)

    def mix(index):
        rows = at(index * 256, 256)
        r.second[:, rows] = nt(r.d_low[...], r.attn[3, rows, :]).astype(BF)

    each(4, mix)
    first = iota((128, LANES), 1) < HEAD
    r.small[0:2, :] = jnp.zeros((2, D), F32)

    def pair(index):
        sample, hp = index // 8, index % 8
        rows, lanes = at(sample * 128, 128), at(hp * LANES, LANES)
        q, k, v = r.q[rows, lanes], r.k[rows, lanes], r.v[rows, lanes]
        d_mixed = r.second[rows, lanes]
        none = jnp.zeros_like(q)
        d_q = d_k = d_v = None
        for part in range(2):
            mine = first if part == 0 else jnp.logical_not(first)
            own = jnp.where(mine, d_mixed, none)
            probs = r.probs[index * 2 + part]
            d_probs = nt(own, v)
            inner = jnp.sum(probs * d_probs, axis=1, keepdims=True)
            d_scores = (probs * (d_probs - inner)).astype(BF)
            terms = (
                nn(d_scores, jnp.where(mine, k, none)),
                tn(d_scores, jnp.where(mine, q, none)),
                tn(probs.astype(BF), own),
            )
            d_q = terms[0] if d_q is None else d_q + terms[0]
            d_k = terms[1] if d_k is None else d_k + terms[1]
            d_v = terms[2] if d_v is None else d_v + terms[2]
        d_q = d_q * SCALE
        r.q[rows, lanes] = d_q.astype(BF)
        r.k[rows, lanes] = (d_k * SCALE).astype(BF)
        r.v[rows, lanes] = d_v.astype(BF)
        r.small[0:1, lanes] += col_sum(d_q)
        r.small[1:2, lanes] += col_sum(d_v)

    each(16, pair)

    def inward(index):
        rows = at(index * 256, 256)
        total = nt(r.q[...], r.attn[0, rows, :]) + nt(r.k[...], r.attn[1, rows, :])
        r.unit_two[:, rows] = total + nt(r.v[...], r.attn[2, rows, :])

    each(4, inward)

    def start(index):
        rows = at(index * 64, 64)
        grad, unit = r.unit_two[rows, :], r.unit_one[rows, :]
        whole = r.d_mid[rows, :] + norm_back(grad, unit, r.rstd_one[rows, 0:1], gain_rows[0:1])
        d_in[rows, :] = whole.astype(BF)
        lead = r.leads[index // 2].astype(F32) / 100.0
        r.small[4:5, :] += col_sum(grad * unit)
        r.small[6:7, :] += col_sum(grad)
        r.small[8:9, :] += lead * col_sum(whole)

    each(4, start)


def trunk_out(r, out):
    def tile(index):
        lanes = at(index * 256, 256)
        total = r.resid[:, lanes] + r.vecs[3:4, lanes].astype(F32)
        for n in range(4):
            total = total + nn(r.grads[n, 256:512, :], r.bufs[1, n, :, lanes])
        out[:, lanes] = total.astype(BF)

    each(4, tile)


def trunk_weights(r):
    r.turn_a[...] = r.normed[...].T
    r.turn_b[...] = r.mixed[...].T

    def quarter(index):
        y, c = index // 2, index % 2
        rows = at(index * 256, 256)
        for m, (left, right) in enumerate(
            ((r.turn_a, r.q), (r.turn_a, r.k), (r.turn_a, r.v), (r.turn_b, r.d_low))
        ):
            value = nn(left[rows, :], right[...])
            for j in range(4):
                spot = ((c * 2 + y) * 4 + (m % 2) * 2 + m // 2) * 64
                r.bufs[0, j, at(spot, 64), :] = value[j * 64 : (j + 1) * 64].astype(BF)

    each(4, quarter)


def hidden_tables(r):
    r.win_t[...] = r.win[...].T
    r.units[...] = jnp.broadcast_to(r.unit_bias[0:1, :].astype(F32), (256, 256)).T
    r.unit_two[...] = jnp.zeros((256, D), F32)
    r.d_mid[...] = jnp.zeros((256, D), F32)
    r.bias_sum[...] = jnp.zeros((256, 256), F32)


def hidden_plane(r, plane):
    def tile(index):
        rows = at(index * 256, 256)
        x, cot = r.bufs[0, plane, rows, :], r.bufs[1, plane, rows, :]
        value, slope = curve(nt(r.win_t[...], x) + r.units[...])
        grad = nt(r.wout[...], cot) * slope
        r.bias_sum[...] += grad
        r.unit_two[...] += nn(grad.astype(BF), x)
        r.d_mid[...] += nn(value.astype(BF), cot)

    each(4, tile)


def remote(source, target, sent, arrived, device):
    return pltpu.make_async_remote_copy(
        src_ref=source,
        dst_ref=target,
        send_sem=sent,
        recv_sem=arrived,
        device_id=device,
        device_id_type=MESH,
    )


class Place:
    def __init__(self):
        self.section = lax.axis_index("section")
        self.me = lax.axis_index("dp")
        self.c = self.me % 2
        self.y = (self.me // 2) % 2
        self.low = (self.me // 4) % 2
        self.high = self.me // 8
        self.across = {"section": 1 - self.section}
        self.core = {"dp": self.me + 1 - 2 * self.c}
        self.beside = {"dp": self.me + 2 - 4 * self.y}
        self.near = {"dp": self.me + 4 - 8 * self.low}
        self.far = {"dp": self.me + 8 - 16 * self.high}
        self.both = {"dp": self.me + 12 - 8 * self.low - 16 * self.high}

    def plane(self, step):
        low = (self.low + step % 2) % 2
        high = (self.high + step // 2) % 2
        return high * 2 + low

    def levels(self):
        return (self.core, self.beside, self.near, self.far)


class Share:
    def __init__(self, r, place, which, sent, arrived):
        self.place, self.sent, self.arrived = place, sent, arrived
        self.buf = r.bufs.at[which]
        self.pair = place.y * 2 + place.c
        self.other = (1 - place.y) * 2 + place.c
        self.mine = place.high * 2 + place.low

    def copy(self, plane, spot, number, device):
        block = self.buf.at[plane, at(spot * 256, 256)]
        return remote(block, block, self.sent.at[number], self.arrived.at[plane * 4 + spot], device)

    def wait(self, plane, spot):
        self.copy(plane, spot, 0, self.place.core).wait_recv()

    def along(self, plane, number, to_upper):
        step = 4 if to_upper else -4
        device = {"dp": self.place.me + step}
        pl.when(self.mine < 3 if to_upper else self.mine > 0)(
            lambda: self.copy(plane, self.pair, number, device).start()
        )

    def open(self):
        self.along(self.mine, 0, True)
        self.along(self.mine, 1, False)
        self.copy(self.mine, self.pair, 2 + self.mine, self.place.beside).start()
        self.copy(self.mine, self.pair, 6 + self.mine, self.place.core).start()

    def pass_on(self, distance):
        for below in (True, False):
            plane = self.mine - distance if below else self.mine + distance

            @pl.when(plane >= 0 if below else plane < 4)
            def _():
                self.wait(plane, self.pair)
                self.along(plane, 14 + plane, below)
                self.copy(plane, self.pair, 2 + plane, self.place.beside).start()
                self.copy(plane, self.pair, 6 + plane, self.place.core).start()

            if distance == 1 and not below:
                continue
            before = plane + 1 if below else plane - 1

            @pl.when(before >= 0 if below else before < 4)
            def _():
                self.wait(before, self.other)
                self.copy(before, self.other, 10 + before, self.place.core).start()

    def settle(self, plane):
        self.wait(plane, self.place.y * 2 + 1 - self.place.c)
        self.wait(plane, (1 - self.place.y) * 2 + 1 - self.place.c)

    def close(self):
        def done(number):
            self.copy(0, 0, number, self.place.core).wait_send()

        pl.when(self.mine < 3)(lambda: done(0))
        pl.when(self.mine > 0)(lambda: done(1))
        for number in range(2, 14):
            done(number)
        for plane in range(4):
            gone = ((plane < self.mine) & (self.mine < 3)) | ((plane > self.mine) & (self.mine > 0))
            pl.when(gone)(functools.partial(done, 14 + plane))


class Halving:
    def __init__(self, place, source, room, sizes, sent, arrived, done, target=None):
        self.place, self.source, self.room, self.sizes = place, source, room, sizes
        self.sent, self.arrived, self.done, self.target = sent, arrived, done, target
        self.bits = (place.c, place.y, place.low, place.high)

    def takes(self, level):
        if self.target is None or level < 2:
            return None
        on_low = self.place.low == self.target[0]
        return on_low if level == 2 else on_low & (self.place.high == self.target[1])

    def gives(self, level):
        if self.target is None or level < 2:
            return None
        on_low = self.place.low == self.target[0]
        return jnp.logical_not(on_low) if level == 2 else on_low & (self.place.high != self.target[1])

    def when(self, condition, action):
        if condition is None:
            action()
        else:
            pl.when(condition)(action)

    def part(self, j, level, side):
        rows = self.sizes[level]
        start = 0 if self.target is not None and level >= 2 else side * rows
        return self.source(j, start, rows) if level == 0 else self.room(j, level - 1, start, rows)

    def copy(self, j, level):
        give = self.part(j, level, 1 - self.bits[level])
        target = self.room(j, level, 0, self.sizes[level])
        device = self.place.levels()[level]
        return remote(give, target, self.sent.at[j, level], self.arrived.at[j, level], device)

    def begin(self, j, level):
        self.when(self.gives(level), lambda: self.copy(j, level).start())

    def finish(self, j, level):
        self.when(self.takes(level), lambda: self.take(j, level))
        if level < 3:
            self.begin(j, level + 1)

    def take(self, j, level):
        self.copy(j, level).wait_recv()
        mine = self.part(j, level, self.bits[level])
        room = self.room(j, level, 0, self.sizes[level])
        total = mine[...].astype(F32) + room[...].astype(F32)
        if level == 3:
            self.done(j, total)
        else:
            room[...] = total.astype(BF)

    def close(self, j):
        for level in range(4):
            self.when(self.gives(level), lambda: self.copy(j, level).wait_send())


class Doubling:
    def __init__(self, r, place, rows, sent, arrived):
        self.r, self.place, self.rows, self.sent, self.arrived = r, place, rows, sent, arrived

    def before(self, level):
        return self.r.small.at[0 : self.rows] if level == 0 else self.r.small_in.at[level - 1, 0 : self.rows]

    def copy(self, level):
        target = self.r.small_in.at[level, 0 : self.rows]
        device = self.place.levels()[level]
        return remote(self.before(level), target, self.sent.at[level], self.arrived.at[level], device)

    def begin(self):
        self.copy(0).start()

    def finish(self, level):
        self.copy(level).wait_recv()
        rows = slice(0, self.rows)
        self.r.small_in[level, rows] = self.before(level)[...] + self.r.small_in[level, rows]
        if level < 3:
            self.copy(level + 1).start()

    def close(self):
        for level in range(4):
            self.copy(level).wait_send()


def greet(place):
    barrier = pltpu.get_barrier_semaphore()
    devices = (place.across, place.core, place.beside, place.near, place.far, place.both)
    for device in devices:
        pl.semaphore_signal(barrier, inc=1, device_id=device, device_id_type=MESH)
    pl.semaphore_wait(barrier, len(devices))


def across(r, place, number, source, target):
    return remote(source, target, r.over_sent.at[number], r.over_come.at[number], place.across)


def front_tail(r, place):
    own = at((place.y * 2 + place.c) * 256, 256)
    high, low = halves(r.small_in[3, 48:64])
    r.fold_sum[0:16, :] = high
    r.fold_sum[16:32, :] = low
    both = nn(r.fold_sum[...], r.attn[1])
    mine = iota((HEADS, D), 1) >> 6 == iota((HEADS, D), 0)
    query = col_sum(jnp.where(mine, both[0:HEADS] + both[HEADS : 2 * HEADS], 0.0))
    r.query_row[0:1, :] = query
    high, low = halves(query)
    row = iota((16, D), 0)
    pair = jnp.where(row == 0, high.astype(F32), jnp.where(row == 1, low.astype(F32), 0.0))
    r.query_pair[...] = pair.astype(BF)

    @pl.when(place.high + place.low == 0)
    def _():
        first = jnp.broadcast_to(r.vecs[0:1, own].astype(F32), (16, 256))
        first = jnp.where(iota((16, 256), 0) < 2, first, 0.0).astype(BF)
        r.attn_out[...] = tn(first, r.query_pair[...])
        r.vec_out[...] = col_sum(nt(r.query_pair[...], r.attn[0, own, :]))

    @pl.when((place.high == 0) & (place.low == 1))
    def _():
        left = jnp.concatenate([r.fold_sum[0:16, own], r.fold_sum[16:32, own], r.fold_sum[0:16, own]], axis=0)
        right = jnp.concatenate([r.qhead[0:16, :], r.qhead[0:16, :], r.qhead[16:32, :]], axis=0)
        r.attn_out[...] = tn(left, right)
        r.vec_out[...] = r.query_row[0:1, own]

    @pl.when(place.high == 1)
    def _():
        r.vec_out[...] = r.small_in[3, pl.ds(64 + place.low, 1), own]


def front_section(r, place):
    def load(number, source, target):
        return pltpu.make_async_copy(source, target, r.loads.at[number])

    mine = place.me * 128
    half = FF // 2
    loads = [
        load(0, r.patches_in.at[0], r.pix.at[0:128]),
        load(1, r.patches_in.at[1], r.pix.at[128:256]),
        load(2, r.weight_in, r.raw),
        load(3, r.attn_in.at[0, 0], r.attn.at[0]),
        load(4, r.attn_in.at[0, 1], r.attn.at[1]),
        load(5, r.attn_in.at[0, 2], r.attn.at[2]),
        load(6, r.attn_in.at[0, 3], r.attn.at[3]),
        load(7, r.cot_in.at[0], r.bufs.at[1, place.plane(0), at((place.y * 2 + place.c) * 256, 128)]),
        load(8, r.cot_in.at[1], r.bufs.at[1, place.plane(0), at((place.y * 2 + place.c) * 256 + 128, 128)]),
        load(9, r.mlp_in.at[:, at(mine, 128)], r.win.at[:, 0:128]),
        load(10, r.mlp_in.at[:, at(half + mine, 128)], r.win.at[:, 128:256]),
        load(11, r.mlp_out.at[at(mine, 128), :], r.wout.at[0:128]),
        load(12, r.mlp_out.at[at(half + mine, 128), :], r.wout.at[128:256]),
    ]
    for one in loads:
        one.start()
    cots = Share(r, place, 1, r.cot_sent, r.cot_come)
    hiddens = Share(r, place, 0, r.x_sent, r.x_come)
    greet(place)
    for one in loads[0:3]:
        one.wait()
    front_tables(r)
    loads[7].wait()
    loads[8].wait()
    cots.open()
    loads[3].wait()
    loads[4].wait()
    front_query(r)
    loads[5].wait()
    front_values(r)
    loads[6].wait()
    front_forward(r, r.act_out)
    send_front = across(r, place, 0, r.act_out, r.arrive)
    send_front.start()
    for one in loads[9:13]:
        one.wait()
    r.unit_bias[0:1, 0:128] = r.bias_in[:, at(mine, 128)]
    r.unit_bias[0:1, 128:256] = r.bias_in[:, at(half + mine, 128)]
    hidden_tables(r)
    for distance in range(1, 5):
        cots.pass_on(distance)
    for plane in range(4):
        cots.settle(plane)
    mine = hiddens.mine
    near = mine + 1 - 2 * place.low
    hiddens.wait(mine, hiddens.pair)
    hiddens.open()
    hiddens.pass_on(1)
    hiddens.settle(mine)
    hidden_plane(r, mine)
    hiddens.pass_on(2)
    across(r, place, 1, r.leave, r.arrive).wait_recv()

    def matrix_done(j, value):
        r.attn_out[j * 128 : (j + 1) * 128, :] = value

    def patch_done(j, value):
        r.patch_out[...] = value[0:24]
        r.gift_patch[...] = value[24:48]

    starts = (0, 256, 384, 0)

    def matrix_of(which, target):
        def room(j, level, start, rows):
            if level == 3:
                return r.last_room.at[at(j * 128 + start, rows)]
            return r.rooms.at[which * 2 + j, at(starts[level] + start, rows)]

        return Halving(
            place,
            lambda j, start, rows: r.grads.at[which * 2 + j, at(start, rows)],
            room,
            (256, 128, 128, 128),
            r.sum_sent.at[:, at(which * 4, 4)],
            r.sum_come.at[:, at(which * 4, 4)],
            matrix_done,
            target,
        )

    values, outs = matrix_of(0, (0, 1)), matrix_of(1, (1, 1))
    patch_starts = (0, 384, 576, 672)
    pixels = Halving(
        place,
        lambda j, start, rows: r.patch_sum.at[at(start, rows)],
        lambda j, level, start, rows: r.patch_rooms.at[at(patch_starts[level] + start, rows)],
        (384, 192, 96, 48),
        r.patch_sent,
        r.patch_come,
        patch_done,
    )
    front_back_out(r, r.arrive)
    outs.begin(0, 0)
    outs.begin(1, 0)
    front_back_values(r, r.arrive)
    outs.finish(0, 0)
    outs.finish(1, 0)
    front_back_heads(r)
    outs.finish(0, 1)
    outs.finish(1, 1)
    front_back_inputs(r, r.input_out, r.gift_half)
    give_half = across(r, place, 2, r.gift_half, r.gift_half)
    give_half.start()
    hiddens.pass_on(3)
    front_back_table(r)
    front_back_projection(r)
    values.begin(0, 0)
    values.begin(1, 0)
    outs.finish(0, 2)
    outs.finish(1, 2)
    front_back_pixels(r)
    values.finish(0, 0)
    values.finish(1, 0)
    r.small[66:72, :] = jnp.zeros((6, D), F32)
    smalls = Doubling(r, place, 72, r.small_sent, r.small_come)
    smalls.begin()
    front_back_order(r)
    pixels.begin(0, 0)
    outs.finish(0, 3)
    outs.finish(1, 3)
    hiddens.pass_on(4)
    smalls.finish(0)
    pixels.finish(0, 0)
    hiddens.settle(near)
    hidden_plane(r, near)
    values.finish(0, 1)
    values.finish(1, 1)
    smalls.finish(1)
    pixels.finish(0, 1)
    far = mine + 2 - 4 * place.high
    hiddens.settle(far)
    hidden_plane(r, far)
    values.finish(0, 2)
    values.finish(1, 2)
    smalls.finish(2)
    pixels.finish(0, 2)
    both = 3 - mine
    hiddens.settle(both)
    hidden_plane(r, both)
    r.gift[0] = r.unit_two[128:256, :].astype(BF)
    r.gift[1] = r.d_mid[128:256, :].astype(BF)
    bias = col_sum(r.bias_sum[...].T)
    r.gift_bias[...] = jnp.broadcast_to(bias[:, 128:256], (8, 128))
    gifts = [across(r, place, 3, r.gift, r.gift), across(r, place, 4, r.gift_bias, r.gift_bias)]
    for one in gifts:
        one.start()
    smalls.finish(3)
    give_var = across(r, place, 5, r.small_in.at[3, 0:48], r.gift_var)
    give_var.start()
    pixels.finish(0, 3)
    give_patch = across(r, place, 6, r.gift_patch, r.gift_patch)
    give_patch.start()
    r.win_out[...] = r.unit_two[0:128, :].T
    r.wout_out[...] = r.d_mid[0:128, :]
    r.bias_out[...] = bias[:, 0:128]
    r.var_out[...] = r.small_in[3, 0:48]
    front_tail(r, place)
    values.finish(0, 3)
    values.finish(1, 3)
    take_small = across(r, place, 7, r.small_in.at[3, 0:16], r.gift_var.at[0:16])
    take_small.wait_recv()
    r.gain_out[...] = r.gift_var[4:6, :]
    r.shift_out[...] = r.gift_var[6:9, :]
    give_attn = pltpu.make_async_copy(r.attn_out, r.attn_final, r.loads.at[13])
    give_attn.start()
    cots.close()
    hiddens.close()
    for j in range(2):
        values.close(j)
        outs.close(j)
    pixels.close(0)
    smalls.close()
    for one in (send_front, give_half, *gifts, give_var, give_patch):
        one.wait_send()
    give_attn.wait()


def trunk_section(r, place):
    def load(number, source, target):
        return pltpu.make_async_copy(source, target, r.loads.at[number])

    outs = [load(n, r.mlp_out.at[n * 1024 : (n + 1) * 1024], r.bufs.at[1, n]) for n in range(4)]
    cots = [load(4 + n, r.cot_in.at[n], r.cot.at[n * 128 : (n + 1) * 128]) for n in range(2)]
    attns = [load(6 + n, r.attn_in.at[0, n], r.attn.at[n]) for n in range(4)]
    ins = [load(10 + n, r.mlp_in.at[:, n * 1024 : (n + 1) * 1024], r.bufs.at[0, n]) for n in range(4)]
    for one in (*cots, *outs, *attns, *ins):
        one.start()
    r.small[0:24, :] = jnp.zeros((24, D), F32)
    greet(place)
    for one in (*cots, *outs):
        one.wait()
    trunk_ahead(r)
    for one in (*attns, *ins):
        one.wait()
    across(r, place, 0, r.act_out, r.arrive).wait_recv()
    trunk_attention(r, r.arrive)
    plane, pair = place.plane(0), place.y * 2 + place.c
    send_x = remote(
        r.second,
        r.bufs.at[0, plane, at(pair * 256, 256)],
        r.over_sent.at[0],
        r.x_come.at[plane * 4 + pair],
        place.across,
    )
    send_x.start()
    trunk_hidden(r)
    send_x.wait_send()
    trunk_back(r, r.leave)
    send_in = across(r, place, 1, r.leave, r.arrive)
    send_in.start()
    trunk_out(r, r.act_out)
    for level, device in enumerate(place.levels()):
        pl.semaphore_signal(r.ready.at[level], inc=1, device_id=device, device_id_type=MESH)
    smalls = Doubling(r, place, 16, r.small_sent, r.small_come)
    smalls.begin()
    trunk_weights(r)
    for level in range(4):
        pl.semaphore_wait(r.ready.at[level], 1)

    def matrix_done(j, value):
        r.attn_out[j * 64 : (j + 1) * 64, :] = value

    starts = (0, 512, 768, 896)
    matrices = Halving(
        place,
        lambda j, start, rows: r.bufs.at[0, j, at(start, rows)],
        lambda j, level, start, rows: r.bufs.at[1, j, at(starts[level] + start, rows)],
        (512, 256, 128, 64),
        r.sum_sent.at[:, 0:4],
        r.sum_come.at[:, 0:4],
        matrix_done,
    )
    for j in range(4):
        matrices.begin(j, 0)
    for level in range(4):
        smalls.finish(level)
    send_small = across(r, place, 7, r.small_in.at[3, 0:16], r.gift_var.at[0:16])
    send_small.start()
    for turn in range(7):
        for level in range(4):
            if 0 <= turn - level < 4:
                matrices.finish(turn - level, level)
    give_attn = pltpu.make_async_copy(r.attn_out, r.attn_final, r.loads.at[14])
    give_attn.start()
    own = at((place.y * 2 + place.c) * 256, 256)
    r.vec_out[...] = r.small_in[3, pl.ds(place.high * 2 + place.low, 1), own]
    r.gain_out[...] = r.small_in[3, 4:6]
    r.shift_out[...] = r.small_in[3, 6:9]
    across(r, place, 2, r.gift_half, r.gift_half).wait_recv()
    r.input_out[...] = r.gift_half[...].astype(F32)
    across(r, place, 3, r.gift, r.gift).wait_recv()
    across(r, place, 4, r.gift_bias, r.gift_bias).wait_recv()
    r.win_out[...] = r.gift[0].astype(F32).T
    r.wout_out[...] = r.gift[1].astype(F32)
    r.bias_out[...] = r.gift_bias[0:1, :]
    across(r, place, 5, r.small_in.at[3, 0:48], r.gift_var).wait_recv()
    r.var_out[...] = r.gift_var[...]
    across(r, place, 6, r.gift_patch, r.gift_patch).wait_recv()
    r.patch_out[...] = r.gift_patch[...]
    for j in range(4):
        matrices.close(j)
    smalls.close()
    send_in.wait_send()
    send_small.wait_send()
    give_attn.wait()


CELL_ROWS = (CELLS, D)
SCRATCH = dict(
    attn=((4, D, D), BF),
    bufs=((2, 4, D, D), BF),
    grads=((4, 512, D), BF),
    rooms=((4, 512, D), BF),
    last_room=((256, D), BF),
    patch_rooms=((720, D), BF),
    table=((WIDE, D), BF),
    mid=((WIDE, D), BF),
    turned=((D, WIDE), BF),
    pat=((CELLS, WIDE), BF),
    qhead=((32, D), BF),
    fold=((16, D), BF),
    fold_sum=((32, D), BF),
    query_pair=((16, D), BF),
    query_row=((8, D), F32),
    score=((16, WIDE), F32),
    uses=((16, 1, WIDE), F32),
    probs=((32, 128, 128), F32),
    resid=(CELL_ROWS, F32),
    unit_one=(CELL_ROWS, F32),
    unit_two=(CELL_ROWS, F32),
    d_mid=(CELL_ROWS, F32),
    rstd_one=((CELLS, LANES), F32),
    rstd_two=((CELLS, LANES), F32),
    normed=(CELL_ROWS, BF),
    k=(CELL_ROWS, BF),
    v=(CELL_ROWS, BF),
    mixed=(CELL_ROWS, BF),
    d_low=(CELL_ROWS, BF),
    arrive=(CELL_ROWS, BF),
    turn_a=((D, CELLS), BF),
    turn_b=((D, CELLS), BF),
    small=((72, D), F32),
    small_in=((4, 72, D), F32),
    unit_bias=((16, 256), BF),
    gift=((2, 128, D), BF),
    gift_bias=((8, 128), F32),
    gift_patch=((24, D), F32),
    gift_half=((CELLS, 384), BF),
    gift_var=((48, D), F32),
)
SEMAPHORES = dict(
    loads=(15,),
    over_sent=(8,),
    over_come=(8,),
    cot_sent=(18,),
    cot_come=(16,),
    x_sent=(18,),
    x_come=(16,),
    sum_sent=(4, 8),
    sum_come=(4, 8),
    patch_sent=(1, 4),
    patch_come=(1, 4),
    small_sent=(4,),
    small_come=(4,),
)
INPUTS = dict(
    patches_in=pl.ANY,
    masks=pltpu.VMEM,
    leads=pltpu.SMEM,
    cot_in=pl.ANY,
    weight_in=pl.ANY,
    embed=pltpu.VMEM,
    attn_in=pl.ANY,
    vecs=pltpu.VMEM,
    gains=pltpu.VMEM,
    shifts=pltpu.VMEM,
    mlp_in=pl.ANY,
    bias=pltpu.VMEM,
    bias_in=pltpu.VMEM,
    mlp_out=pl.ANY,
)
OUTPUTS = dict(
    act_out=(CELL_ROWS, BF),
    input_out=((CELLS, 384), F32),
    patch_out=((24, D), F32),
    var_out=((48, D), F32),
    attn_final=(CELL_ROWS, F32),
    vec_out=((1, 256), F32),
    gain_out=((2, D), F32),
    shift_out=((3, D), F32),
    win_out=((D, 128), F32),
    bias_out=((1, 128), F32),
    wout_out=((128, D), F32),
)


class Refs:
    pass


def fused_kernel(*refs):
    r = Refs()
    names = list(INPUTS) + list(OUTPUTS) + list(SCRATCH) + list(SEMAPHORES) + ["ready"]
    for name, ref in zip(names, refs, strict=True):
        setattr(r, name, ref)
    r.patch_sum = r.table.at[0:768]
    r.raw = r.turned.at[0:768, 0:D]
    for number, name in enumerate(("cot", "q", "second", "leave")):
        setattr(r, name, r.turned.at[number * 256 : number * 256 + 256, 0:D])
    r.pix = r.normed.at[:, 0 : V * PIX]
    r.input_sum = r.resid
    r.attn_out = r.resid
    r.agg = r.mixed
    r.dlow = r.d_low
    r.wout = r.k
    r.win_t = r.v
    r.win = r.turn_a
    r.keep = r.rstd_one
    r.units = r.unit_one.at[:, 0:256]
    r.bias_sum = r.unit_one.at[:, 256:512]
    place = Place()
    pl.when(place.section == 0)(lambda: front_section(r, place))
    pl.when(place.section == 1)(lambda: trunk_section(r, place))


def fused_shards(
    patches,
    masks,
    lead_times,
    cotangent,
    patch_weight,
    var_embed,
    attention,
    attn_vectors,
    norm_gains,
    trunk_shifts,
    mlp_in,
    mlp_in_bias,
    mlp_out,
):
    outs = pl.pallas_call(
        fused_kernel,
        in_specs=[pl.BlockSpec(memory_space=space) for space in INPUTS.values()],
        out_specs=[
            pl.BlockSpec(memory_space=pl.ANY if one == (CELL_ROWS, F32) else pltpu.VMEM)
            for one in OUTPUTS.values()
        ],
        out_shape=[jax.ShapeDtypeStruct(*one) for one in OUTPUTS.values()],
        scratch_shapes=[pltpu.VMEM(*one) for one in SCRATCH.values()]
        + [pltpu.SemaphoreType.DMA(one) for one in SEMAPHORES.values()]
        + [pltpu.SemaphoreType.REGULAR((4,))],
        compiler_params=pltpu.CompilerParams(
            collective_id=0, has_side_effects=True, vmem_limit_bytes=60 * 2**20
        ),
    )(
        patches,
        masks,
        lead_times,
        cotangent,
        patch_weight,
        var_embed,
        attention,
        attn_vectors[0],
        norm_gains,
        trunk_shifts,
        mlp_in,
        mlp_in_bias.reshape(4, 1, D),
        mlp_in_bias.reshape(1, FF),
        mlp_out,
    )
    act, inputs, patch, var, attn, vec, gain, shift, win, bias, wout = outs
    return (
        act.reshape(1, 2, 128, D),
        inputs.reshape(2, 128, 384),
        patch,
        var,
        attn[None],
        vec,
        gain,
        shift,
        win,
        bias.reshape(128),
        wout,
    )


def solution(mesh):
    in_specs = (
        P("dp", None, None),
        P("dp", None, None),
        P("dp"),
        P("dp", None, None),
        P(),
        P(),
        P("section", None, None, None),
        P("section", None, None),
        P(),
        P(),
        P(),
        P(),
        P(),
    )
    out_specs = (
        P("section", "dp", None, None),
        P("dp", None, "section"),
        P(("section", "dp"), None),
        P(),
        P("section", "dp", None),
        P("section", "dp"),
        P(),
        P(),
        P(None, ("section", "dp")),
        P(("section", "dp")),
        P(("section", "dp"), None),
    )
    small = mesh.shape["section"] == 2 and mesh.shape["dp"] == 16
    body = fused_shards if small else shards
    return jax.shard_map(body, mesh=mesh, in_specs=in_specs, out_specs=out_specs, check_vma=False)
```

```python
import functools

import jax
import jax.numpy as jnp
from jax import lax
from jax.experimental import pallas as pl
from jax.experimental.pallas import tpu as pltpu
from jax.sharding import PartitionSpec as P

D = 1024
HEADS = 16
HEAD = 64
FF = 4096
V = 48
PIX = 16


EPSILON = 1e-05
MASKED = -1e30
HIGHEST = lax.Precision.HIGHEST


def shortened(array):
    return jax.tree.map(lambda a: a.astype(jnp.bfloat16) if a.dtype == jnp.float32 else a, array)


def from_behind(value, axis, steps):
    count = lax.axis_size(axis)
    leading, last = (max(0, -steps), min(count, count - steps))
    return lax.ppermute(value, axis, [(source, source + steps) for source in range(leading, last)])


def layer_norm(features, gain_row, shift_row):
    row_mean = jnp.mean(features, axis=-1, keepdims=True)
    centred = features - row_mean
    spread = jnp.mean(centred * centred, axis=-1, keepdims=True)
    return centred * lax.rsqrt(spread + EPSILON) * gain_row + shift_row


def exact_gelu(inputs):
    return jax.nn.gelu(inputs, approximate=False)


def matmul(left_side, right_side):
    return jnp.dot(left_side, right_side, preferred_element_type=jnp.float32)


def matmul_tn(left_side, right_side):
    return lax.dot_general(
        left_side, right_side, (((0,), (0,)), ((), ())), preferred_element_type=jnp.float32
    )


def matmul_nt(left_side, right_side):
    return lax.dot_general(
        left_side, right_side, (((1,), (1,)), ((), ())), preferred_element_type=jnp.float32
    )


def updated(carried, changes):
    merged = dict(carried)
    merged.update(changes)
    return merged


def query_terms(layer_weights, layer_vectors):
    query_vec = matmul(layer_vectors[0][None, :], layer_weights[0])[0] + layer_vectors[1].astype(
        jnp.float32
    )
    key_wide = layer_weights[1].astype(jnp.float32).reshape(D, HEADS, HEAD)
    folded = jnp.einsum("dhk,hk->dh", key_wide, query_vec.reshape(HEADS, HEAD), precision=HIGHEST)
    return (query_vec, key_wide, folded)


def embed_block(pixel_rows, valid_cells, patch_weight, var_embed, folded_low, score_scale):
    cell_count = pixel_rows.shape[0]
    shaped = pixel_rows.reshape(cell_count, V, PIX)
    pieces = jnp.einsum(
        "tvp,vpd->tvd", shaped, patch_weight.reshape(V, PIX, D), preferred_element_type=jnp.float32
    )
    embedded = (pieces + var_embed.astype(jnp.float32)[None]).astype(jnp.bfloat16)
    scores = (
        jnp.einsum("tvd,dh->tvh", embedded, folded_low, preferred_element_type=jnp.float32)
        * score_scale
    )
    scores = jnp.where(valid_cells[:, :, None] > 0, scores, MASKED)
    weights = jax.nn.softmax(scores, axis=1)
    weights_low = weights.astype(jnp.bfloat16)
    pooled = jnp.einsum(
        "tvh,tvd->thd", weights_low, embedded, preferred_element_type=jnp.float32
    ).astype(jnp.bfloat16)
    return (shaped, embedded, weights, weights_low, pooled)


def pool_values(pooled, layer_weights, layer_vectors):
    cell_count = pooled.shape[0]
    projected = jnp.einsum(
        "thd,dhk->thk",
        pooled,
        layer_weights[2].reshape(D, HEADS, HEAD),
        preferred_element_type=jnp.float32,
    )
    return (projected.reshape(cell_count, D) + layer_vectors[2].astype(jnp.float32)).astype(
        jnp.bfloat16
    )


def front_block_back(
    pixel_rows,
    valid_cells,
    d_out,
    patch_weight,
    var_embed,
    layer_weights,
    layer_vectors,
    folded_low,
    score_scale,
):
    shaped, embedded, weights, weights_low, pooled = embed_block(
        pixel_rows, valid_cells, patch_weight, var_embed, folded_low, score_scale
    )
    values_low = pool_values(pooled, layer_weights, layer_vectors)
    cell_count = pixel_rows.shape[0]
    g_bo = jnp.sum(d_out.astype(jnp.float32), axis=0)
    g_wo = matmul_tn(values_low, d_out)
    d_values = matmul_nt(d_out, layer_weights[3])
    g_bv = jnp.sum(d_values, axis=0)
    d_values_low = d_values.astype(jnp.bfloat16).reshape(cell_count, HEADS, HEAD)
    g_wv = jnp.einsum(
        "thd,thk->dhk", pooled, d_values_low, preferred_element_type=jnp.float32
    ).reshape(D, D)
    d_pooled = jnp.einsum(
        "thk,dhk->thd",
        d_values_low,
        layer_weights[2].reshape(D, HEADS, HEAD),
        preferred_element_type=jnp.float32,
    ).astype(jnp.bfloat16)
    d_weights = jnp.einsum("thd,tvd->tvh", d_pooled, embedded, preferred_element_type=jnp.float32)
    d_embedded = jnp.einsum(
        "tvh,thd->tvd", weights_low, d_pooled, preferred_element_type=jnp.float32
    )
    d_scores = (weights * (d_weights - jnp.sum(weights * d_weights, axis=1, keepdims=True))).astype(
        jnp.bfloat16
    )
    g_folded = (
        jnp.einsum("tvd,tvh->dh", embedded, d_scores, preferred_element_type=jnp.float32)
        * score_scale
    )
    d_embedded = (
        d_embedded
        + jnp.einsum("tvh,dh->tvd", d_scores, folded_low, preferred_element_type=jnp.float32)
        * score_scale
    )
    g_var = jnp.sum(d_embedded, axis=0)
    d_embedded_low = d_embedded.astype(jnp.bfloat16)
    g_patch = jnp.einsum(
        "tvp,tvd->vpd", shaped, d_embedded_low, preferred_element_type=jnp.float32
    ).reshape(V * PIX, D)
    d_pixels = jnp.einsum(
        "tvd,vpd->tvp",
        d_embedded_low,
        patch_weight.reshape(V, PIX, D),
        preferred_element_type=jnp.float32,
    ).reshape(cell_count, V * PIX)
    return (g_wv, g_wo, g_bv, g_bo, g_folded, g_var, g_patch, d_pixels)


def layer_two(
    x_in,
    lead_hours,
    d_out,
    layer_weights,
    layer_vectors,
    norm_gains,
    trunk_shifts,
    mlp_in,
    mlp_in_bias,
    mlp_out,
):
    seq_len = x_in.shape[0]
    score_scale = HEAD ** (-0.5)
    gain_rows = norm_gains.astype(jnp.float32)
    shift_rows = trunk_shifts.astype(jnp.float32)
    vec_rows = layer_vectors.astype(jnp.float32)
    lead_scale = lead_hours.astype(jnp.float32) / 100.0
    resid_in = x_in.astype(jnp.float32) + lead_scale * shift_rows[2]
    normed, first_back = jax.vjp(layer_norm, resid_in, gain_rows[0], shift_rows[0])
    normed_low = normed.astype(jnp.bfloat16)
    queries = (
        (matmul(normed_low, layer_weights[0]) + vec_rows[0])
        .astype(jnp.bfloat16)
        .reshape(seq_len, HEADS, HEAD)
    )
    key_rows = (
        matmul(normed_low, layer_weights[1]).astype(jnp.bfloat16).reshape(seq_len, HEADS, HEAD)
    )
    value_rows = (
        (matmul(normed_low, layer_weights[2]) + vec_rows[1])
        .astype(jnp.bfloat16)
        .reshape(seq_len, HEADS, HEAD)
    )
    scores = (
        jnp.einsum("qhd,khd->hqk", queries, key_rows, preferred_element_type=jnp.float32)
        * score_scale
    )
    attn_probs = jax.nn.softmax(scores, axis=-1)
    probs_low = attn_probs.astype(jnp.bfloat16)
    mixed_heads = (
        jnp.einsum("hqk,khd->qhd", probs_low, value_rows, preferred_element_type=jnp.float32)
        .reshape(seq_len, D)
        .astype(jnp.bfloat16)
    )
    resid_mid = resid_in + matmul(mixed_heads, layer_weights[3]) + vec_rows[2]
    normed_two, second_back = jax.vjp(layer_norm, resid_mid, gain_rows[1], shift_rows[1])
    normed_two_low = normed_two.astype(jnp.bfloat16)
    hidden_pre = matmul(normed_two_low, mlp_in) + mlp_in_bias.astype(jnp.float32)
    hidden, gelu_back = jax.vjp(exact_gelu, hidden_pre)
    hidden_low = hidden.astype(jnp.bfloat16)
    produced = (resid_mid + matmul(hidden_low, mlp_out) + vec_rows[3]).astype(jnp.bfloat16)
    d_final = d_out.astype(jnp.float32)
    g_b2 = jnp.sum(d_final, axis=0)
    g_wout = matmul_tn(hidden_low, d_out)
    d_hidden = matmul_nt(d_out, mlp_out)
    d_pre = gelu_back(d_hidden)[0]
    g_bin = jnp.sum(d_pre, axis=0)
    d_pre_low = d_pre.astype(jnp.bfloat16)
    g_win = matmul_tn(normed_two_low, d_pre_low)
    d_mid_norm, g_gain_two, g_shift_two = second_back(matmul_nt(d_pre_low, mlp_in))
    d_mid = d_final + d_mid_norm
    g_bo = jnp.sum(d_mid, axis=0)
    d_mid_low = d_mid.astype(jnp.bfloat16)
    g_wo = matmul_tn(mixed_heads, d_mid_low)
    d_mixed = (
        matmul_nt(d_mid_low, layer_weights[3]).astype(jnp.bfloat16).reshape(seq_len, HEADS, HEAD)
    )
    d_probs = jnp.einsum("qhd,khd->hqk", d_mixed, value_rows, preferred_element_type=jnp.float32)
    d_values = jnp.einsum(
        "hqk,qhd->khd", probs_low, d_mixed, preferred_element_type=jnp.float32
    ).reshape(seq_len, D)
    d_scores = (
        attn_probs * (d_probs - jnp.sum(attn_probs * d_probs, axis=-1, keepdims=True))
    ).astype(jnp.bfloat16)
    d_queries = (
        jnp.einsum("hqk,khd->qhd", d_scores, key_rows, preferred_element_type=jnp.float32).reshape(
            seq_len, D
        )
        * score_scale
    )
    d_keys = (
        jnp.einsum("hqk,qhd->khd", d_scores, queries, preferred_element_type=jnp.float32).reshape(
            seq_len, D
        )
        * score_scale
    )
    g_bq = jnp.sum(d_queries, axis=0)
    g_bv = jnp.sum(d_values, axis=0)
    d_queries_low = d_queries.astype(jnp.bfloat16)
    d_keys_low = d_keys.astype(jnp.bfloat16)
    d_values_low = d_values.astype(jnp.bfloat16)
    g_wq = matmul_tn(normed_low, d_queries_low)
    g_wk = matmul_tn(normed_low, d_keys_low)
    g_wv = matmul_tn(normed_low, d_values_low)
    d_normed = (
        matmul_nt(d_queries_low, layer_weights[0])
        + matmul_nt(d_keys_low, layer_weights[1])
        + matmul_nt(d_values_low, layer_weights[2])
    )
    d_in_norm, g_gain_one, g_shift_one = first_back(d_normed)
    d_in = d_mid + d_in_norm
    g_lead = lead_scale * jnp.sum(d_in, axis=0)
    return (
        produced,
        d_in.astype(jnp.bfloat16),
        jnp.stack([g_wq, g_wk, g_wv, g_wo]),
        jnp.stack([g_bq, g_bv, g_bo, g_b2]),
        jnp.stack([g_gain_one, g_gain_two]),
        jnp.stack([g_shift_one, g_shift_two, g_lead]),
        g_win,
        g_bin,
        g_wout,
    )


def send_forward(sent_rows):
    return from_behind(shortened(sent_rows), "section", 1).astype(sent_rows.dtype)


def shards(
    patches,
    masks,
    lead_times,
    cotangent,
    patch_weight,
    var_embed,
    attention,
    attn_vectors,
    norm_gains,
    trunk_shifts,
    mlp_in,
    mlp_in_bias,
    mlp_out,
):
    micro_count, seq_len, pixel_width = patches.shape
    block_rows = min(128, seq_len)
    score_scale = HEAD ** (-0.5)
    layer_weights = attention[0]
    layer_vectors = attn_vectors[0]
    on_front = lax.axis_index("section") == 0
    empty_rows = jnp.zeros((seq_len, D), jnp.bfloat16)
    carried = {
        "attn": jnp.zeros((4, D, D), jnp.float32),
        "vec": jnp.zeros((4, D), jnp.float32),
        "u_sum": jnp.zeros((D, HEADS), jnp.float32),
        "patch": jnp.zeros((V * PIX, D), jnp.float32),
        "var": jnp.zeros((V, D), jnp.float32),
        "gains": jnp.zeros((2, D), jnp.float32),
        "shifts": jnp.zeros((3, D), jnp.float32),
        "w_in": jnp.zeros((D, FF), jnp.float32),
        "b_in": jnp.zeros((FF,), jnp.float32),
        "w_out": jnp.zeros((FF, D), jnp.float32),
        "outputs": jnp.zeros((micro_count, seq_len, D), jnp.bfloat16),
        "pixels": jnp.zeros((micro_count, seq_len, pixel_width), jnp.float32),
        "returned": jnp.zeros((micro_count, seq_len, D), jnp.bfloat16),
    }

    def front_forward(carried, mb_index):
        query_vec, key_wide, folded = query_terms(layer_weights, layer_vectors)
        folded_low = folded.astype(jnp.bfloat16)
        valid_cells = masks[mb_index, :, 0:block_rows].T
        block_parts = embed_block(
            patches[mb_index, 0:block_rows],
            valid_cells,
            patch_weight,
            var_embed,
            folded_low,
            score_scale,
        )
        values_low = pool_values(block_parts[4], layer_weights, layer_vectors)
        pieces = [
            (matmul(values_low, layer_weights[3]) + layer_vectors[3].astype(jnp.float32)).astype(
                jnp.bfloat16
            )
        ]
        produced = jnp.concatenate(pieces, axis=0)
        return (
            updated(carried, {"outputs": carried["outputs"].at[mb_index].set(produced)}),
            produced,
        )

    def front_backward(carried, mb_index, d_front):
        query_vec, key_wide, folded = query_terms(layer_weights, layer_vectors)
        folded_low = folded.astype(jnp.bfloat16)
        attn_sum = carried["attn"]
        vec_sum = carried["vec"]
        u_total = carried["u_sum"]
        var_total = carried["var"]
        patch_total = carried["patch"]
        valid_cells = masks[mb_index, :, 0:block_rows].T
        block_grads = front_block_back(
            patches[mb_index, 0:block_rows],
            valid_cells,
            d_front[0:block_rows],
            patch_weight,
            var_embed,
            layer_weights,
            layer_vectors,
            folded_low,
            score_scale,
        )
        attn_sum = attn_sum.at[2].add(block_grads[0]).at[3].add(block_grads[1])
        vec_sum = vec_sum.at[2].add(block_grads[2]).at[3].add(block_grads[3])
        u_total = u_total + block_grads[4]
        var_total = var_total + block_grads[5]
        patch_total = patch_total + block_grads[6]
        pixel_pieces = [block_grads[7]]
        pixel_grads = carried["pixels"].at[mb_index].set(jnp.concatenate(pixel_pieces, axis=0))
        return updated(
            carried,
            {
                "attn": attn_sum,
                "vec": vec_sum,
                "u_sum": u_total,
                "var": var_total,
                "patch": patch_total,
                "pixels": pixel_grads,
            },
        )

    def back_step(carried, mb_index, arriving):
        produced, d_front, attn_part, vec_part, gain_part, shift_part, g_win, g_bin, g_wout = (
            layer_two(
                arriving,
                lead_times[mb_index],
                cotangent[mb_index],
                layer_weights,
                layer_vectors,
                norm_gains,
                trunk_shifts,
                mlp_in,
                mlp_in_bias,
                mlp_out,
            )
        )
        changes = {
            "attn": carried["attn"] + attn_part,
            "vec": carried["vec"] + vec_part,
            "gains": carried["gains"] + gain_part,
            "shifts": carried["shifts"] + shift_part,
            "w_in": carried["w_in"] + g_win,
            "b_in": carried["b_in"] + g_bin,
            "w_out": carried["w_out"] + g_wout,
            "outputs": carried["outputs"].at[mb_index].set(produced),
            "returned": carried["returned"].at[mb_index].set(d_front),
        }
        return (updated(carried, changes), d_front)

    def finish_front(carried):
        query_vec, key_wide, folded = query_terms(layer_weights, layer_vectors)
        u_total = carried["u_sum"]
        d_key = (u_total[:, :, None] * query_vec.reshape(HEADS, HEAD)[None]).reshape(D, D)
        d_query_vec = jnp.einsum("dh,dhk->hk", u_total, key_wide, precision=HIGHEST).reshape(D)
        d_query_weight = layer_vectors[0].astype(jnp.float32)[:, None] * d_query_vec[None, :]
        d_query = jnp.dot(layer_weights[0].astype(jnp.float32), d_query_vec, precision=HIGHEST)
        attn_sum = carried["attn"].at[0].set(d_query_weight).at[1].set(d_key)
        vec_sum = carried["vec"].at[0].set(d_query).at[1].set(d_query_vec)
        return updated(carried, {"attn": attn_sum, "vec": vec_sum})

    arriving_act = empty_rows
    for step_number in range(micro_count + 1):

        def front_turn(inputs, step_number=step_number):
            carried, act_in = inputs
            sent_rows = empty_rows
            if step_number < micro_count:
                carried, sent_rows = front_forward(carried, step_number)
            return (carried, sent_rows)

        def back_turn(inputs, step_number=step_number):
            carried, act_in = inputs
            if step_number >= 1:
                carried, returned_rows = back_step(carried, step_number - 1, act_in)
            return (carried, empty_rows)

        carried, sent_act = lax.cond(on_front, front_turn, back_turn, (carried, arriving_act))
        if step_number < micro_count:
            arriving_act = send_forward(sent_act)
    gradients_back = from_behind(shortened(carried["returned"]), "section", -1)

    def front_all(kept_state):
        for mb_index in range(micro_count):
            kept_state = front_backward(kept_state, mb_index, gradients_back[mb_index])
        return kept_state

    carried = lax.cond(on_front, front_all, lambda kept_state: kept_state, carried)
    carried = lax.cond(on_front, finish_front, lambda kept_state: kept_state, carried)
    attn_grads, vec_grads = (
        lax.psum_scatter(
            carried["attn"].reshape(1, 4 * D, D), "dp", scatter_dimension=1, tiled=True
        ),
        lax.psum_scatter(carried["vec"].reshape(1, 4 * D), "dp", scatter_dimension=1, tiled=True),
    )
    win_grads, bin_grads, wout_grads, patch_grads = (
        lax.psum_scatter(carried["w_in"], ("section", "dp"), scatter_dimension=1, tiled=True),
        lax.psum_scatter(carried["b_in"], ("section", "dp"), scatter_dimension=0, tiled=True),
        lax.psum_scatter(carried["w_out"], ("section", "dp"), scatter_dimension=0, tiled=True),
        lax.psum_scatter(carried["patch"], ("section", "dp"), scatter_dimension=0, tiled=True),
    )
    var_grads, gain_grads, shift_grads = lax.psum(
        (carried["var"], carried["gains"], carried["shifts"]), ("section", "dp")
    )
    pixel_half = pixel_width // 2
    moved = from_behind(shortened(carried["pixels"][:, :, pixel_half:]), "section", 1)
    input_grads = jnp.where(on_front, carried["pixels"][:, :, :pixel_half], moved)
    activations = carried["outputs"][None]
    return (
        activations,
        input_grads,
        patch_grads,
        var_grads,
        attn_grads,
        vec_grads,
        gain_grads,
        shift_grads,
        win_grads,
        bin_grads,
        wout_grads,
    )


F32 = jnp.float32
BF = jnp.bfloat16
I32 = jnp.int32
MESH = pl.DeviceIdType.MESH
CELLS = 256
SLOT = 64
WIDE = 1152
LANES = 128
SCALE = 0.125
ROOT_HALF = 0.7071067811865476
ROOT_TAU = 0.3989422804014327


def nn(a, b):
    return jnp.dot(a, b, preferred_element_type=F32)


def nt(a, b):
    return lax.dot_general(a, b, (((1,), (1,)), ((), ())), preferred_element_type=F32)


def tn(a, b):
    return lax.dot_general(a, b, (((0,), (0,)), ((), ())), preferred_element_type=F32)


def at(start, size):
    if isinstance(start, int):
        return pl.ds(start, size)
    return pl.ds(pl.multiple_of(start, size), size)


def each(count, body, unroll=1):
    def step(index, carry):
        body(index)
        return carry

    lax.fori_loop(0, count, step, 0, unroll=unroll)


def iota(shape, dim):
    return lax.broadcasted_iota(I32, shape, dim)


def halves(value):
    high = value.astype(BF)
    return high, (value - high.astype(F32)).astype(BF)


def pixel_column(slot):
    return ((slot & (SLOT - 1)) << 4) + (slot >> 6)


def slot_tile(index, rows, columns):
    match = pixel_column(iota((rows, 1), 0) + index * rows)
    return jnp.where(iota((rows, columns), 1) == match, 1.0, 0.0).astype(BF)


def spread(tile):
    return jnp.concatenate([tile] * (WIDE // LANES), axis=1)


def front_tables(r):
    def place(index):
        tile = slot_tile(index, 256, V * PIX)
        r.table[at(index * 256, 256), :] = nn(tile, r.raw[...]).astype(BF)
        r.pat[:, at(index * 256, 256)] = nt(r.pix[...], tile).astype(BF)

    each(4, place, 4)
    r.table[1024:1072, :] = r.embed[...]
    r.table[1072:WIDE, :] = jnp.zeros((WIDE - 1072, D), BF)
    lane = iota((CELLS, LANES), 1)
    r.pat[:, 1024:WIDE] = jnp.where(lane < V, 1.0, 0.0).astype(BF)
    twice = jnp.where(iota((V, LANES), 1) & (SLOT - 1) == iota((V, LANES), 0), 1.0, 0.0).astype(BF)
    for sample in range(2):
        present = tn(r.masks[sample].astype(F32).astype(BF), twice)
        r.keep[sample * 128 : sample * 128 + 128, :] = present


def front_query(r):
    first = jnp.broadcast_to(r.vecs[0:1, :], (16, D))
    query = nn(first, r.attn[0])[0:1, :] + r.vecs[1:2, :].astype(F32)
    own = iota((HEADS, D), 1) >> 6 == iota((HEADS, D), 0)
    high, low = halves(jnp.where(own, jnp.broadcast_to(query, (HEADS, D)), 0.0))
    r.qhead[0:HEADS, :] = high
    r.qhead[HEADS : 2 * HEADS, :] = low
    both = nt(r.qhead[...], r.attn[1])
    folded = (both[0:HEADS] + both[HEADS : 2 * HEADS]).astype(BF)
    r.fold[...] = folded
    r.score[...] = nt(folded, r.table[...]) * SCALE


def front_values(r):
    def tile(index):
        lanes = at(index * 256, 256)
        r.mid[:, lanes] = nn(r.table[...], r.attn[2, :, lanes]).astype(BF)

    each(4, tile, 4)


def front_scores(r, head):
    row = r.score[pl.ds(head, 1), :]
    total = None
    for k in range(WIDE // LANES):
        part = r.pat[:, k * LANES : (k + 1) * LANES].astype(F32) * row[:, k * LANES : (k + 1) * LANES]
        total = part if total is None else total + part
    total = total + pltpu.roll(total, SLOT, 1)
    total = jnp.where(r.keep[...] > 0.5, total, MASKED)
    top = jnp.max(total, axis=1, keepdims=True)
    grown = jnp.exp(total - top)
    return grown / (0.5 * jnp.sum(grown, axis=1, keepdims=True))


def front_forward(r, out):
    first_half = iota((CELLS, LANES), 1) < HEAD

    def pair(index):
        lanes = at(index * LANES, LANES)
        found = []
        for part in range(2):
            head = index * 2 + part
            weights = front_scores(r, head)
            r.probs[at(head * 2, 2)] = weights.reshape(2, 128, LANES)
            pooled = r.pat[...] * spread(weights.astype(BF))
            found.append(nn(pooled, r.mid[:, lanes]))
        values = jnp.where(first_half, found[0], found[1]) + r.vecs[2:3, lanes].astype(F32)
        r.agg[:, lanes] = values.astype(BF)

    each(HEADS // 2, pair, 2)

    def tile(index):
        lanes = at(index * 256, 256)
        out[:, lanes] = (nn(r.agg[...], r.attn[3, :, lanes]) + r.vecs[3:4, lanes].astype(F32)).astype(BF)

    each(4, tile, 4)


def front_back_values(r, d_out):
    def tile(index):
        rows = at(index * 256, 256)
        grad = nt(d_out[...], r.attn[3, rows, :])
        r.small[16:17, rows] = jnp.sum(grad, axis=0, keepdims=True)
        r.small[17:18, rows] = jnp.sum(d_out[:, rows].astype(F32), axis=0, keepdims=True)
        r.dlow[:, rows] = grad.astype(BF)

    each(4, tile, 4)
    r.turn_a[...] = r.dlow[...].T


def front_back_heads(r):
    first_half = iota((CELLS, LANES), 1) < HEAD
    r.input_sum[...] = jnp.zeros((CELLS, D), F32)

    def pair(index):
        lanes = at(index * LANES, LANES)
        grads = r.dlow[:, lanes]
        mid = r.mid[:, lanes]
        for part in range(2):
            head = index * 2 + part
            mine = first_half if part == 0 else jnp.logical_not(first_half)
            own = jnp.where(mine, grads, jnp.zeros_like(grads))
            weights = r.probs[at(head * 2, 2)].reshape(CELLS, LANES)
            low = weights.astype(BF)
            lowf = low.astype(F32)
            total = None
            for k in range(WIDE // 384):
                wide = nt(own, mid[k * 384 : (k + 1) * 384, :])
                for j in range(3):
                    n = k * 3 + j
                    cols = slice(n * LANES, (n + 1) * LANES)
                    piece = wide[:, j * LANES : (j + 1) * LANES]
                    term = piece * r.pat[:, cols].astype(F32)
                    total = term if total is None else total + term
                    if n < 8:
                        r.input_sum[:, cols] = r.input_sum[:, cols] + lowf * piece
            total = total + pltpu.roll(total, SLOT, 1)
            inner = 0.5 * jnp.sum(weights * total, axis=1, keepdims=True)
            d_score = (weights * (total - inner)).astype(BF).astype(F32)
            row = r.score[pl.ds(head, 1), :]
            for n in range(9):
                cols = slice(n * LANES, (n + 1) * LANES)
                if n < 8:
                    r.input_sum[:, cols] = r.input_sum[:, cols] + d_score * row[:, cols]
                r.uses[head, :, cols] = SCALE * jnp.sum(
                    d_score * r.pat[:, cols].astype(F32), axis=0, keepdims=True
                )
            pooled = r.pat[...] * spread(low)
            r.turned[at(head * HEAD, HEAD), :] = nn(r.turn_a[at(head * HEAD, HEAD), :], pooled).astype(BF)

    each(HEADS // 2, pair, 2)


def put_rows(sums, quarter, value):
    y, c = quarter // 2, quarter % 2
    for j in range(2):
        sums[at(j * 512 + (c * 2 + y) * 128, 128), :] = value[j * 128 : (j + 1) * 128].astype(BF)


def front_back_out(r, d_out):
    r.turn_b[...] = r.agg[...].T

    def tile(index):
        put_rows(r.sums[3], index, nn(r.turn_b[at(index * 256, 256), :], d_out[...]))

    each(4, tile, 4)


def front_back_table(r):
    uses = jnp.concatenate([r.uses[h] for h in range(HEADS)], axis=0).astype(BF)
    r.small[0:16, :] = nn(uses, r.table[...])
    r.mid[...] = r.turned[...].T


def front_back_projection(r):
    def values(index):
        rows = at(index * 256, 256)
        put_rows(r.sums[2], index, tn(r.table[:, rows], r.mid[...]))

    each(4, values, 4)


def front_back_pixels(r):
    uses = jnp.concatenate([r.uses[h] for h in range(HEADS)], axis=0).astype(BF)

    def pixels(index):
        lanes = at(index * 256, 256)
        full = nt(r.mid[...], r.attn[2, lanes, :]) + tn(uses, r.fold[:, lanes])
        r.turned[:, lanes] = full[0:1024].astype(BF)
        r.var_sum[:, lanes] = full[1024:1072].astype(BF)

    each(4, pixels, 4)


def front_back_order(r):
    def order(index):
        row = iota((256, 1), 0) + index * 256
        piece, k = row // 48, row % 48
        owner = ((piece & 1) * 2 + ((piece >> 1) & 1)) * 4 + ((piece >> 2) & 1) * 2 + (piece >> 3)
        natural = owner * 24 + jnp.where(k < 24, k, k + 360)
        slot = (natural & (PIX - 1)) * SLOT + (natural >> 4)
        pick = jnp.where(iota((256, D), 1) == slot, 1.0, 0.0).astype(BF)
        r.patch_sum[at(index * 256, 256), :] = nn(pick, r.turned[:, 0:1024]).astype(BF)

    each(3, order, 3)


def front_back_inputs(r, own_half, other_half):
    low = r.input_sum[...].astype(BF)
    r.dlow[...] = low
    for half, out in ((0, own_half), (1, other_half)):
        column = pixel_column(iota((D, 1), 0)) - half * 384
        pick = jnp.where(iota((D, 384), 1) == column, 1.0, 0.0).astype(BF)
        out[...] = nn(r.dlow[...], pick).astype(out.dtype)


def row_mean(x):
    return jnp.mean(x, axis=1, keepdims=True)


def col_sum(x):
    return jnp.sum(x, axis=0, keepdims=True)


def trunk_ahead(r):
    def tile(index):
        n, k = index // 4, index % 4
        found = nt(r.cot[...], r.bufs[at(4096 + index * 256, 256), :])
        r.grads_flat[at(n * 512, 256), at(k * 256, 256)] = found.astype(BF)

    each(16, tile, 4)
    r.small[3:4, :] = col_sum(r.cot[...].astype(F32))


def normalise(r, source, spread_rows, unit, gain, shift, out):
    def rows_of(index):
        rows = at(index * 64, 64)
        x = source[rows, :]
        centred = x - row_mean(x)
        rstd = lax.rsqrt(row_mean(centred * centred) + EPSILON)
        scaled = centred * rstd
        unit[rows, :] = scaled
        spread_rows[rows, :] = jnp.broadcast_to(rstd, (64, LANES))
        out[rows, :] = (scaled * gain + shift).astype(BF)

    each(4, rows_of, 4)


def trunk_attention(r, front):
    shift_rows = r.shifts[...].astype(F32)
    gain_rows = r.gains[...].astype(F32)

    def enter(index):
        rows = at(index * 128, 128)
        lead = r.leads[index].astype(F32) / 100.0
        r.resid[rows, :] = front[rows, :].astype(F32) + lead * shift_rows[2:3]

    each(2, enter)
    normalise(r, r.resid, r.rstd_one, r.unit_one, gain_rows[0:1], shift_rows[0:1], r.normed)

    def project(index):
        lanes = at(index * 256, 256)
        x = r.normed[...]
        r.q[:, lanes] = (nn(x, r.attn[0, :, lanes]) + r.vecs[0:1, lanes].astype(F32)).astype(BF)
        r.k[:, lanes] = nn(x, r.attn[1, :, lanes]).astype(BF)
        r.v[:, lanes] = (nn(x, r.attn[2, :, lanes]) + r.vecs[1:2, lanes].astype(F32)).astype(BF)

    each(4, project, 4)
    first = iota((128, LANES), 1) < HEAD

    def pair(index):
        sample, hp = index // 8, index % 8
        rows, lanes = at(sample * 128, 128), at(hp * LANES, LANES)
        q, k, v = r.q[rows, lanes], r.k[rows, lanes], r.v[rows, lanes]
        none = jnp.zeros_like(q)
        mixed = None
        for part in range(2):
            mine = first if part == 0 else jnp.logical_not(first)
            scores = nt(jnp.where(mine, q, none), k) * SCALE
            grown = jnp.exp(scores - jnp.max(scores, axis=1, keepdims=True))
            probs = grown / jnp.sum(grown, axis=1, keepdims=True)
            r.probs[index * 2 + part] = probs
            term = nn(probs.astype(BF), jnp.where(mine, v, none))
            mixed = term if mixed is None else mixed + term
        r.mixed[rows, lanes] = mixed.astype(BF)

    each(16, pair, 4)

    def leave(index):
        lanes = at(index * 256, 256)
        grown = nn(r.mixed[...], r.attn[3, :, lanes]) + r.vecs[2:3, lanes].astype(F32)
        r.resid[:, lanes] = r.resid[:, lanes] + grown

    each(4, leave, 4)
    normalise(r, r.resid, r.rstd_two, r.unit_two, gain_rows[1:2], shift_rows[1:2], r.x_own)


def bias_row(r, start, count):
    return r.bias_in[at(start, count)].astype(F32).reshape(1, count)


def curve(x):
    area = 0.5 + 0.5 * lax.erf(x * ROOT_HALF)
    return x * area, area + x * (ROOT_TAU * jnp.exp(-0.5 * x * x))


def trunk_hidden(r):
    def tile(index):
        n, k = index // 4, index % 4
        lanes = at(k * 256, 256)
        pre = nn(r.x_own[...], r.bufs[at(n * 1024, 1024), lanes]) + bias_row(r, index * 256, 256)
        value, slope = curve(pre)
        r.grads_flat[at(n * 512 + 256, 256), lanes] = value.astype(BF)
        r.grads_flat[at(n * 512, 256), lanes] = (r.grads_flat[at(n * 512, 256), lanes].astype(F32) * slope).astype(BF)

    each(16, tile, 4)

    def back(index):
        rows = at(index * 256, 256)
        total = None
        for n in range(4):
            term = nt(r.grads_flat[n * 512 : n * 512 + 256, :], r.bufs[at(n * 1024 + index * 256, 256), :])
            total = term if total is None else total + term
        r.d_mid[:, rows] = total

    each(4, back, 4)


def norm_back(grad, unit, rstd, gain):
    scaled = grad * gain
    along = row_mean(scaled * unit)
    return rstd * (scaled - row_mean(scaled) - unit * along)


def trunk_back(r):
    gain_rows = r.gains[...].astype(F32)
    r.small[2:3, :] = jnp.zeros((1, D), F32)
    r.small[4:9, :] = jnp.zeros((5, D), F32)

    def second(index):
        rows = at(index * 64, 64)
        grad, unit = r.d_mid[rows, :], r.unit_two[rows, :]
        mid = r.cot[rows, :].astype(F32) + norm_back(grad, unit, r.rstd_two[rows, 0:1], gain_rows[1:2])
        r.d_mid[rows, :] = mid
        r.d_low[rows, :] = mid.astype(BF)
        r.small[2:3, :] += col_sum(mid)
        r.small[5:6, :] += col_sum(grad * unit)
        r.small[7:8, :] += col_sum(grad)

    each(4, second, 4)


def trunk_back_heads(r):
    def mix(index):
        rows = at(index * 256, 256)
        r.second[:, rows] = nt(r.d_low[...], r.attn[3, rows, :]).astype(BF)

    each(4, mix, 4)
    first = iota((128, LANES), 1) < HEAD
    r.small[0:2, :] = jnp.zeros((2, D), F32)

    def pair(index):
        sample, hp = index // 8, index % 8
        rows, lanes = at(sample * 128, 128), at(hp * LANES, LANES)
        q, k, v = r.q[rows, lanes], r.k[rows, lanes], r.v[rows, lanes]
        d_mixed = r.second[rows, lanes]
        none = jnp.zeros_like(q)
        d_q = d_k = d_v = None
        for part in range(2):
            mine = first if part == 0 else jnp.logical_not(first)
            own = jnp.where(mine, d_mixed, none)
            probs = r.probs[index * 2 + part]
            d_probs = nt(own, v)
            inner = jnp.sum(probs * d_probs, axis=1, keepdims=True)
            d_scores = (probs * (d_probs - inner)).astype(BF)
            terms = (
                nn(d_scores, jnp.where(mine, k, none)),
                tn(d_scores, jnp.where(mine, q, none)),
                tn(probs.astype(BF), own),
            )
            d_q = terms[0] if d_q is None else d_q + terms[0]
            d_k = terms[1] if d_k is None else d_k + terms[1]
            d_v = terms[2] if d_v is None else d_v + terms[2]
        d_q = d_q * SCALE
        r.q[rows, lanes] = d_q.astype(BF)
        r.k[rows, lanes] = (d_k * SCALE).astype(BF)
        r.v[rows, lanes] = d_v.astype(BF)
        r.small[0:1, lanes] += col_sum(d_q)
        r.small[1:2, lanes] += col_sum(d_v)

    each(16, pair, 4)


def trunk_back_in(r, d_in):
    gain_rows = r.gains[...].astype(F32)

    def inward(index):
        rows = at(index * 256, 256)
        total = nt(r.q[...], r.attn[0, rows, :]) + nt(r.k[...], r.attn[1, rows, :])
        r.unit_two[:, rows] = total + nt(r.v[...], r.attn[2, rows, :])

    each(4, inward, 4)

    def start(index):
        rows = at(index * 64, 64)
        grad, unit = r.unit_two[rows, :], r.unit_one[rows, :]
        whole = r.d_mid[rows, :] + norm_back(grad, unit, r.rstd_one[rows, 0:1], gain_rows[0:1])
        d_in[rows, :] = whole.astype(BF)
        lead = r.leads[index // 2].astype(F32) / 100.0
        r.small[4:5, :] += col_sum(grad * unit)
        r.small[6:7, :] += col_sum(grad)
        r.small[8:9, :] += lead * col_sum(whole)

    each(4, start, 4)


def trunk_out(r, out):
    def tile(index):
        lanes = at(index * 256, 256)
        total = r.resid[:, lanes] + r.vecs[3:4, lanes].astype(F32)
        for n in range(4):
            total = total + nn(r.grads_flat[n * 512 + 256 : n * 512 + 512, :], r.bufs[4096 + n * 1024 : 5120 + n * 1024, lanes])
        out[:, lanes] = total.astype(BF)

    each(4, tile, 4)


def trunk_weight_out(r):
    r.turn_b[...] = r.mixed[...].T

    def quarter(index):
        put_rows(r.sums[3], index, nn(r.turn_b[at(index * 256, 256), :], r.d_low[...]))

    each(4, quarter, 4)


def trunk_weights(r):
    r.turn_a[...] = r.normed[...].T

    def quarter(index):
        rows = at(index * 256, 256)
        for m, right in enumerate((r.q, r.k, r.v)):
            put_rows(r.sums[m], index, nn(r.turn_a[rows, :], right[...]))

    each(4, quarter, 2)


def hidden_loads(r, place, load):
    loads = []
    for part, owner in enumerate((place.me, place.me + 2 - 4 * place.y)):
        units = at((place.section * 16 + owner) * 128, 128)
        side = slice(part * 128, part * 128 + 128)
        loads.append(load(15 + part * 2, r.mlp_in.at[:, units], r.win.at[:, side]))
        loads.append(load(16 + part * 2, r.mlp_out.at[units, :], r.wout.at[side]))
    return loads


def hidden_tables(r, place):
    r.win_t[...] = r.win[...].T
    for part, owner in enumerate((place.me, place.me + 2 - 4 * place.y)):
        both = bias_row(r, (place.section * 16 + owner - place.c) * 128, 256)
        first = jnp.broadcast_to(place.c == 0, (1, 128))
        row = jnp.where(first, both[:, 0:128], both[:, 128:256])
        r.units[part * 128 : part * 128 + 128, :] = jnp.broadcast_to(row, (256, 128)).T
    r.unit_two[...] = jnp.zeros((256, D), F32)
    r.d_mid[...] = jnp.zeros((256, D), F32)
    r.bias_sum[...] = jnp.zeros((256, 256), F32)


def hidden_plane(r, plane):
    def tile(index):
        x, cot = r.gather[plane, at(index * 256, 256), :], r.gather[plane, at(512 + index * 256, 256), :]
        value, slope = curve(nt(r.win_t[...], x) + r.units[...])
        grad = nt(r.wout[...], cot) * slope
        r.bias_sum[...] += grad
        r.unit_two[...] += nn(grad.astype(BF), x)
        r.d_mid[...] += nn(value.astype(BF), cot)

    each(2, tile, 2)


def hidden_exchange(r, place):
    r.gift[0] = r.unit_two[128:256, :].astype(BF)
    r.gift[1] = r.d_mid[128:256, :].astype(BF)
    r.gift_bias[...] = jnp.broadcast_to(col_sum(r.bias_sum[...].T), (8, 256))
    gifts = [
        remote(r.gift, r.gift_in, r.gift_sent.at[0], r.gift_come.at[0], place.beside),
        remote(r.gift_bias, r.gift_bias_in, r.gift_sent.at[1], r.gift_come.at[1], place.beside),
    ]
    for one in gifts:
        one.start()
    return gifts


def hidden_finish(r, gifts):
    for one in gifts:
        one.wait()
    r.win_out[...] = (r.unit_two[0:128, :] + r.gift_in[0].astype(F32)).T
    r.wout_out[...] = r.d_mid[0:128, :] + r.gift_in[1].astype(F32)
    r.bias_out[...] = r.gift_bias[0:1, 0:128] + r.gift_bias_in[0:1, 128:256]


def remote(source, target, sent, arrived, device):
    return pltpu.make_async_remote_copy(
        src_ref=source,
        dst_ref=target,
        send_sem=sent,
        recv_sem=arrived,
        device_id=device,
        device_id_type=MESH,
    )


class Place:
    def __init__(self):
        self.section = lax.axis_index("section")
        self.me = lax.axis_index("dp")
        self.c = self.me % 2
        self.y = (self.me // 2) % 2
        self.low = (self.me // 4) % 2
        self.high = self.me // 8
        self.across = {"section": 1 - self.section}
        self.core = {"dp": self.me + 1 - 2 * self.c}
        self.beside = {"dp": self.me + 2 - 4 * self.y}
        self.near = {"dp": self.me + 4 - 8 * self.low}
        self.far = {"dp": self.me + 8 - 16 * self.high}
        self.both = {"dp": self.me + 12 - 8 * self.low - 16 * self.high}

    def plane(self, step):
        low = (self.low + step % 2) % 2
        high = (self.high + step // 2) % 2
        return high * 2 + low

    def levels(self):
        return (self.core, self.beside, self.near, self.far)


class Share:
    def __init__(self, r, place, base, sent, arrived):
        self.place, self.base, self.sent, self.arrived = place, base, sent, arrived
        self.buf = r.gather
        self.mine = place.high * 2 + place.low

    def block(self, plane, c):
        return self.buf.at[plane, at(self.base + c * 256, 256)]

    def copy(self, plane, c, number, device):
        block = self.block(plane, c)
        return remote(block, block, self.sent.at[number], self.arrived.at[plane * 2 + c], device)

    def wait(self, plane, c):
        self.copy(plane, c, 0, self.place.core).wait_recv()

    def along(self, plane, number, to_upper):
        device = {"dp": self.place.me + (4 if to_upper else -4)}
        pl.when(self.mine < 3 if to_upper else self.mine > 0)(
            lambda: self.copy(plane, self.place.c, number, device).start()
        )

    def open(self):
        self.along(self.mine, 0, True)
        self.along(self.mine, 1, False)
        self.copy(self.mine, self.place.c, 2 + self.mine, self.place.core).start()

    def pass_on(self, distance):
        for below in (True, False):
            plane = self.mine - distance if below else self.mine + distance

            @pl.when(plane >= 0 if below else plane < 4)
            def _():
                self.wait(plane, self.place.c)
                self.along(plane, 6 + plane, below)
                self.copy(plane, self.place.c, 2 + plane, self.place.core).start()

    def settle(self, plane):
        self.wait(plane, 1 - self.place.c)

    def close(self):
        def done(number):
            self.copy(0, 0, number, self.place.core).wait_send()

        pl.when(self.mine < 3)(lambda: done(0))
        pl.when(self.mine > 0)(lambda: done(1))
        for number in range(2, 6):
            done(number)
        for plane in range(4):
            gone = ((plane < self.mine) & (self.mine < 3)) | ((plane > self.mine) & (self.mine > 0))
            pl.when(gone)(functools.partial(done, 6 + plane))


class Halving:
    def __init__(self, place, source, room, sizes, sent, arrived, done, target=None):
        self.place, self.source, self.room, self.sizes = place, source, room, sizes
        self.sent, self.arrived, self.done, self.target = sent, arrived, done, target
        self.bits = (place.c, place.y, place.low, place.high)

    def takes(self, level):
        if self.target is None or level < 2:
            return None
        on_low = self.place.low == self.target[0]
        return on_low if level == 2 else on_low & (self.place.high == self.target[1])

    def gives(self, level):
        if self.target is None or level < 2:
            return None
        on_low = self.place.low == self.target[0]
        return jnp.logical_not(on_low) if level == 2 else on_low & (self.place.high != self.target[1])

    def when(self, condition, action):
        if condition is None:
            action()
        else:
            pl.when(condition)(action)

    def part(self, j, level, side):
        rows = self.sizes[level]
        start = 0 if self.target is not None and level >= 2 else side * rows
        return self.source(j, start, rows) if level == 0 else self.room(j, level - 1, start, rows)

    def copy(self, j, level):
        give = self.part(j, level, 1 - self.bits[level])
        target = self.room(j, level, 0, self.sizes[level])
        device = self.place.levels()[level]
        return remote(give, target, self.sent.at[j, level], self.arrived.at[j, level], device)

    def begin(self, j, level):
        self.when(self.gives(level), lambda: self.copy(j, level).start())

    def finish(self, j, level):
        self.when(self.takes(level), lambda: self.take(j, level))
        if level < 3:
            self.begin(j, level + 1)

    def take(self, j, level):
        self.copy(j, level).wait_recv()
        mine = self.part(j, level, self.bits[level])
        room = self.room(j, level, 0, self.sizes[level])
        total = mine[...].astype(F32) + room[...].astype(F32)
        if level == 3:
            self.done(j, total)
        else:
            room[...] = total.astype(BF)

    def close(self, j):
        for level in range(4):
            self.when(self.gives(level), lambda: self.copy(j, level).wait_send())


class Doubling:
    def __init__(self, place, rows, own, come, sent, arrived):
        self.place, self.rows, self.own, self.come = place, rows, own, come
        self.sent, self.arrived = sent, arrived

    def before(self, level):
        return self.own.at[0 : self.rows] if level == 0 else self.come.at[level - 1, 0 : self.rows]

    def copy(self, level):
        target = self.come.at[level, 0 : self.rows]
        device = self.place.levels()[level]
        return remote(self.before(level), target, self.sent.at[level], self.arrived.at[level], device)

    def begin(self):
        self.copy(0).start()

    def finish(self, level):
        self.copy(level).wait_recv()
        room = self.come.at[level, 0 : self.rows]
        total = self.before(level)[...].astype(F32) + room[...].astype(F32)
        room[...] = total.astype(room.dtype)
        if level < 3:
            self.copy(level + 1).start()

    def close(self):
        for level in range(4):
            self.copy(level).wait_send()


def matrix_sums(r, place, which):
    sums, rooms = r.sums[which], r.matrix_rooms[which]
    starts = (0, 256, 384)

    def room(j, level, start, rows):
        if level == 3:
            return r.last_room.at[at(j * 128 + start, rows)]
        return rooms.at[at(j * 512 + starts[level] + start, rows)]

    def done(j, value):
        r.attn_out[j * 128 : (j + 1) * 128, :] = value

    return Halving(
        place,
        lambda j, start, rows: sums.at[at(j * 512 + start, rows)],
        room,
        (256, 128, 128, 128),
        r.sum_sent.at[:, at(which * 4, 4)],
        r.sum_come.at[:, at(which * 4, 4)],
        done,
        (which % 2, which // 2),
    )


def greet(place):
    barrier = pltpu.get_barrier_semaphore()
    devices = (place.across, place.core, place.beside, place.near, place.far, place.both)
    for device in devices:
        pl.semaphore_signal(barrier, inc=1, device_id=device, device_id_type=MESH)
    pl.semaphore_wait(barrier, len(devices))


def across(r, place, number, source, target):
    return remote(source, target, r.over_sent.at[number], r.over_come.at[number], place.across)


def front_tail(r, place):
    own = at((place.y * 2 + place.c) * 256, 256)
    high, low = halves(r.small_in[3, 0:16])
    r.fold_sum[0:16, :] = high
    r.fold_sum[16:32, :] = low
    both = nn(r.fold_sum[...], r.attn[1])
    mine = iota((HEADS, D), 1) >> 6 == iota((HEADS, D), 0)
    query = col_sum(jnp.where(mine, both[0:HEADS] + both[HEADS : 2 * HEADS], 0.0))
    r.query_row[0:1, :] = query
    high, low = halves(query)
    row = iota((16, D), 0)
    pair = jnp.where(row == 0, high.astype(F32), jnp.where(row == 1, low.astype(F32), 0.0))
    r.query_pair[...] = pair.astype(BF)

    @pl.when(place.high + place.low == 0)
    def _():
        first = jnp.broadcast_to(r.vecs[0:1, own].astype(F32), (16, 256))
        first = jnp.where(iota((16, 256), 0) < 2, first, 0.0).astype(BF)
        r.attn_out[...] = tn(first, r.query_pair[...])
        r.vec_out[...] = col_sum(nt(r.query_pair[...], r.attn[0, own, :]))

    @pl.when((place.high == 0) & (place.low == 1))
    def _():
        left = jnp.concatenate([r.fold_sum[0:16, own], r.fold_sum[16:32, own], r.fold_sum[0:16, own]], axis=0)
        right = jnp.concatenate([r.qhead[0:16, :], r.qhead[0:16, :], r.qhead[16:32, :]], axis=0)
        r.attn_out[...] = tn(left, right)
        r.vec_out[...] = r.query_row[0:1, own]

    @pl.when(place.high == 1)
    def _():
        r.vec_out[...] = r.small_in[3, pl.ds(16 + place.low, 1), own]


def front_section(r, place):
    def load(number, source, target):
        return pltpu.make_async_copy(source, target, r.loads.at[number])

    cots = Share(r, place, 512, r.cot_sent, r.cot_come)
    hiddens = Share(r, place, 0, r.x_sent, r.x_come)
    mine = hiddens.mine
    loads = [
        load(0, r.patches_in.at[0], r.pix.at[0:128]),
        load(1, r.patches_in.at[1], r.pix.at[128:256]),
        load(2, r.weight_in, r.raw),
        load(7, r.cot_in.at[0], cots.block(mine, place.c).at[0:128]),
        load(8, r.cot_in.at[1], cots.block(mine, place.c).at[128:256]),
        load(3, r.attn_in.at[0, 0], r.attn.at[0]),
        load(4, r.attn_in.at[0, 1], r.attn.at[1]),
        load(5, r.attn_in.at[0, 2], r.attn.at[2]),
        load(6, r.attn_in.at[0, 3], r.attn.at[3]),
    ]
    units = hidden_loads(r, place, load)
    for one in loads + units:
        one.start()
    r.small[16:24, :] = jnp.zeros((8, D), F32)
    greet(place)
    for one in loads[0:3]:
        one.wait()
    front_tables(r)
    loads[3].wait()
    loads[4].wait()
    cots.open()
    loads[5].wait()
    loads[6].wait()
    front_query(r)
    loads[7].wait()
    front_values(r)
    loads[8].wait()
    front_forward(r, r.act_out)
    send_front = across(r, place, 0, r.act_out, r.arrive)
    send_front.start()
    for one in units:
        one.wait()
    hidden_tables(r, place)
    for distance in range(1, 4):
        cots.pass_on(distance)
    for plane in range(4):
        cots.settle(plane)
    near = mine + 1 - 2 * place.low
    far = mine + 2 - 4 * place.high
    both = 3 - mine
    hiddens.wait(mine, place.c)
    hiddens.open()
    hiddens.settle(mine)
    hidden_plane(r, mine)
    hiddens.pass_on(1)
    hiddens.settle(near)
    hidden_plane(r, near)
    across(r, place, 1, r.leave, r.arrive).wait_recv()

    def patch_done(j, value):
        r.patch_out[...] = value[0:24]
        r.gift_patch[...] = value[24:48]

    values, outs = matrix_sums(r, place, 2), matrix_sums(r, place, 3)
    patch_starts = (0, 384, 576, 672)
    pixels = Halving(
        place,
        lambda j, start, rows: r.patch_sum.at[at(start, rows)],
        lambda j, level, start, rows: r.patch_rooms.at[at(patch_starts[level] + start, rows)],
        (384, 192, 96, 48),
        r.patch_sent,
        r.patch_come,
        patch_done,
    )
    smalls = Doubling(place, 24, r.small, r.small_in, r.small_sent, r.small_come)
    embeds = Doubling(place, 48, r.var_sum, r.var_in, r.var_sent, r.var_come)
    front_back_out(r, r.arrive)
    outs.begin(0, 0)
    outs.begin(1, 0)
    front_back_values(r, r.arrive)
    outs.finish(0, 0)
    outs.finish(1, 0)
    hiddens.pass_on(2)
    front_back_heads(r)
    front_back_table(r)
    outs.finish(0, 1)
    outs.finish(1, 1)
    smalls.begin()
    front_back_projection(r)
    values.begin(0, 0)
    values.begin(1, 0)
    hiddens.pass_on(3)
    front_back_pixels(r)
    values.finish(0, 0)
    values.finish(1, 0)
    smalls.finish(0)
    front_back_order(r)
    pixels.begin(0, 0)
    embeds.begin()
    front_back_inputs(r, r.input_out, r.gift_half)
    give_half = across(r, place, 2, r.gift_half, r.gift_half)
    give_half.start()
    hiddens.settle(far)
    hidden_plane(r, far)
    outs.finish(0, 2)
    outs.finish(1, 2)
    smalls.finish(1)
    embeds.finish(0)
    values.finish(0, 1)
    pixels.finish(0, 0)
    hiddens.settle(both)
    hidden_plane(r, both)
    values.finish(1, 1)
    values.finish(0, 2)
    smalls.finish(2)
    embeds.finish(1)
    outs.finish(0, 3)
    outs.finish(1, 3)
    values.finish(1, 2)
    pixels.finish(0, 1)
    gifts = hidden_exchange(r, place)
    smalls.finish(3)
    front_tail(r, place)
    embeds.finish(2)
    pixels.finish(0, 2)
    values.finish(0, 3)
    values.finish(1, 3)
    pixels.finish(0, 3)
    give_patch = across(r, place, 6, r.gift_patch, r.gift_patch)
    give_patch.start()
    embeds.finish(3)
    give_var = across(r, place, 5, r.var_in.at[3], r.gift_var)
    give_var.start()
    give_attn = load(13, r.attn_out, r.attn_final)
    give_attn.start()
    r.var_out[...] = r.var_in[3].astype(F32)
    hidden_finish(r, gifts)
    across(r, place, 7, r.small_in.at[3, 0:16], r.gift_small).wait_recv()
    r.gain_out[...] = r.gift_small[4:6, :]
    r.shift_out[...] = r.gift_small[6:9, :]
    cots.close()
    hiddens.close()
    for j in range(2):
        values.close(j)
        outs.close(j)
    pixels.close(0)
    smalls.close()
    embeds.close()
    for one in (send_front, give_half, give_var, give_patch):
        one.wait_send()
    give_attn.wait()


def trunk_section(r, place):
    def load(number, source, target):
        return pltpu.make_async_copy(source, target, r.loads.at[number])

    cots = Share(r, place, 512, r.cot_sent, r.cot_come)
    hiddens = Share(r, place, 0, r.x_sent, r.x_come)
    mine = hiddens.mine
    r.cot = cots.block(mine, place.c)
    r.x_own = hiddens.block(mine, place.c)
    given = [load(4 + n, r.cot_in.at[n], r.cot.at[n * 128 : (n + 1) * 128]) for n in range(2)]
    outs = [load(n, r.mlp_out.at[n * 1024 : (n + 1) * 1024], r.bufs.at[4096 + n * 1024 : 5120 + n * 1024]) for n in range(4)]
    attns = [load(6 + n, r.attn_in.at[0, n], r.attn.at[n]) for n in range(4)]
    ins = [load(10 + n, r.mlp_in.at[:, n * 1024 : (n + 1) * 1024], r.bufs.at[n * 1024 : (n + 1) * 1024]) for n in range(4)]
    for one in (*given, *outs, *attns, *ins):
        one.start()
    r.small[...] = jnp.zeros((24, D), F32)
    greet(place)
    for one in given:
        one.wait()
    cots.open()
    for one in outs:
        one.wait()
    trunk_ahead(r)
    for one in (*attns, *ins):
        one.wait()
    cots.pass_on(1)
    across(r, place, 0, r.act_out, r.arrive).wait_recv()
    trunk_attention(r, r.arrive)
    send_x = remote(r.x_own, r.x_own, r.over_sent.at[0], r.x_come.at[mine * 2 + place.c], place.across)
    send_x.start()
    hiddens.open()
    cots.pass_on(2)
    trunk_hidden(r)

    def tell(ready):
        for level, device in enumerate(place.levels()):
            pl.semaphore_signal(ready.at[level], inc=1, device_id=device, device_id_type=MESH)

    def heed(ready):
        for level in range(4):
            pl.semaphore_wait(ready.at[level], 1)

    tell(r.ready)
    trunk_back(r)
    trunk_weight_out(r)
    heed(r.ready)
    outs_sum = matrix_sums(r, place, 3)
    for j in range(2):
        outs_sum.begin(j, 0)
    hiddens.pass_on(1)
    trunk_back_heads(r)
    for j in range(2):
        outs_sum.finish(j, 0)
    trunk_back_in(r, r.leave)
    send_in = across(r, place, 1, r.leave, r.arrive)
    send_in.start()
    hiddens.pass_on(2)
    trunk_out(r, r.act_out)
    tell(r.ready_two)
    cots.pass_on(3)
    smalls = Doubling(place, 24, r.small, r.small_in, r.small_sent, r.small_come)
    smalls.begin()
    trunk_weights(r)
    units = hidden_loads(r, place, load)
    for one in units:
        one.start()
    heed(r.ready_two)
    sums = [matrix_sums(r, place, which) for which in range(3)]
    parts = [(one, j) for one in reversed(sums) for j in range(2)]
    for one, j in parts:
        one.begin(j, 0)
    outs_sum.finish(0, 1)
    outs_sum.finish(1, 1)
    for one, j in parts[0:2]:
        one.finish(j, 0)
    smalls.finish(0)
    for one in units:
        one.wait()
    hidden_tables(r, place)
    near = mine + 1 - 2 * place.low
    far = mine + 2 - 4 * place.high
    both = 3 - mine

    def plane_work(plane):
        cots.settle(plane)
        hiddens.settle(plane)
        hidden_plane(r, plane)

    plane_work(mine)
    plane_work(near)
    hiddens.pass_on(3)
    outs_sum.finish(0, 2)
    outs_sum.finish(1, 2)
    smalls.finish(1)
    for number, (one, j) in enumerate(parts):
        one.finish(j, 1)
        if number + 2 < len(parts):
            later, k = parts[number + 2]
            later.finish(k, 0)
        if number == 0:
            plane_work(far)
        if number == 1:
            plane_work(both)
            gifts = hidden_exchange(r, place)
        if number == 2:
            smalls.finish(2)
            outs_sum.finish(0, 3)
            outs_sum.finish(1, 3)
        if number == 3:
            smalls.finish(3)
            send_small = across(r, place, 7, r.small_in.at[3, 0:16], r.gift_small)
            send_small.start()
        if number >= 2:
            earlier, k = parts[number - 2]
            earlier.finish(k, 2)
        if number >= 4:
            earlier, k = parts[number - 4]
            earlier.finish(k, 3)
    for one, j in parts[4:6]:
        one.finish(j, 2)
    for one, j in parts[2:6]:
        one.finish(j, 3)
    own = at((place.y * 2 + place.c) * 256, 256)
    r.vec_out[...] = r.small_in[3, pl.ds(mine, 1), own]
    r.gain_out[...] = r.small_in[3, 4:6]
    r.shift_out[...] = r.small_in[3, 6:9]
    give_attn = load(14, r.attn_out, r.attn_final)
    give_attn.start()
    hidden_finish(r, gifts)
    across(r, place, 2, r.gift_half, r.gift_half).wait_recv()
    r.input_out[...] = r.gift_half[...].astype(F32)
    across(r, place, 5, r.var_in.at[3], r.gift_var).wait_recv()
    r.var_out[...] = r.gift_var[...].astype(F32)
    across(r, place, 6, r.gift_patch, r.gift_patch).wait_recv()
    r.patch_out[...] = r.gift_patch[...]
    cots.close()
    hiddens.close()
    for one in (*sums, outs_sum):
        for j in range(2):
            one.close(j)
    smalls.close()
    for one in (send_x, send_in, send_small):
        one.wait_send()
    give_attn.wait()


CELL_ROWS = (CELLS, D)
SCRATCH = dict(
    attn=((4, D, D), BF),
    bufs=((8 * D, D), BF),
    gather=((4, D, D), BF),
    last_room=((256, D), BF),
    grads_flat=((2 * D, D), BF),
    turned=((D, WIDE), BF),
    pat=((CELLS, WIDE), BF),
    qhead=((32, D), BF),
    fold=((16, D), BF),
    fold_sum=((32, D), BF),
    query_pair=((16, D), BF),
    query_row=((8, D), F32),
    score=((16, WIDE), F32),
    uses=((16, 1, WIDE), F32),
    probs=((32, 128, 128), F32),
    resid=(CELL_ROWS, F32),
    unit_one=(CELL_ROWS, F32),
    unit_two=(CELL_ROWS, F32),
    d_mid=(CELL_ROWS, F32),
    rstd_one=((CELLS, LANES), F32),
    rstd_two=((CELLS, LANES), F32),
    normed=(CELL_ROWS, BF),
    k=(CELL_ROWS, BF),
    v=(CELL_ROWS, BF),
    mixed=(CELL_ROWS, BF),
    d_low=(CELL_ROWS, BF),
    arrive=(CELL_ROWS, BF),
    turn_a=((D, CELLS), BF),
    turn_b=((D, CELLS), BF),
    small=((24, D), F32),
    small_in=((4, 24, D), F32),
    var_sum=((48, D), BF),
    var_in=((4, 48, D), BF),
    gift=((2, 128, D), BF),
    gift_in=((2, 128, D), BF),
    gift_bias=((8, 256), F32),
    gift_bias_in=((8, 256), F32),
    gift_var=((48, D), BF),
    gift_small=((16, D), F32),
    gift_patch=((24, D), F32),
    gift_half=((CELLS, 384), BF),
)
SEMAPHORES = dict(
    loads=(19,),
    over_sent=(8,),
    over_come=(8,),
    cot_sent=(10,),
    cot_come=(8,),
    x_sent=(10,),
    x_come=(8,),
    var_sent=(4,),
    var_come=(4,),
    gift_sent=(2,),
    gift_come=(2,),
    sum_sent=(2, 16),
    sum_come=(2, 16),
    patch_sent=(1, 4),
    patch_come=(1, 4),
    small_sent=(4,),
    small_come=(4,),
)
INPUTS = dict(
    patches_in=pl.ANY,
    masks=pltpu.VMEM,
    leads=pltpu.SMEM,
    cot_in=pl.ANY,
    weight_in=pl.ANY,
    embed=pltpu.VMEM,
    attn_in=pl.ANY,
    vecs=pltpu.VMEM,
    gains=pltpu.VMEM,
    shifts=pltpu.VMEM,
    mlp_in=pl.ANY,
    bias_in=pltpu.VMEM,
    mlp_out=pl.ANY,
)
OUTPUTS = dict(
    act_out=(CELL_ROWS, BF),
    input_out=((CELLS, 384), F32),
    patch_out=((24, D), F32),
    var_out=((48, D), F32),
    attn_final=(CELL_ROWS, F32),
    vec_out=((1, 256), F32),
    gain_out=((2, D), F32),
    shift_out=((3, D), F32),
    win_out=((D, 128), F32),
    bias_out=((1, 128), F32),
    wout_out=((128, D), F32),
)


class Refs:
    pass


def fused_kernel(*refs):
    r = Refs()
    names = list(INPUTS) + list(OUTPUTS) + list(SCRATCH) + list(SEMAPHORES) + ["ready", "ready_two"]
    for name, ref in zip(names, refs, strict=True):
        setattr(r, name, ref)
    r.table = r.bufs.at[0:WIDE]
    r.mid = r.bufs.at[WIDE : 2 * WIDE]
    r.patch_rooms = r.bufs.at[4352:5072]
    r.patch_sum = r.table.at[0:768]
    r.raw = r.turned.at[0:768, 0:D]
    for number, name in enumerate(("q", "second", "leave")):
        setattr(r, name, r.turned.at[number * 256 : number * 256 + 256, 0:D])
    r.pix = r.normed.at[:, 0 : V * PIX]
    r.input_sum = r.resid
    r.attn_out = r.resid
    r.agg = r.mixed
    r.dlow = r.d_low
    r.wout = r.k
    r.win_t = r.v
    r.win = r.turn_a
    r.keep = r.rstd_one
    r.units = r.unit_one.at[:, 0:256]
    r.bias_sum = r.unit_one.at[:, 256:512]
    place = Place()

    @pl.when(place.section == 0)
    def _():
        r.sums = (None, None, r.grads_flat.at[0:D], r.grads_flat.at[D : 2 * D])
        r.matrix_rooms = (None, None, r.bufs.at[2304:3328], r.bufs.at[3328:4352])
        front_section(r, place)

    @pl.when(place.section == 1)
    def _():
        r.sums = tuple(r.bufs.at[at(start, D)] for start in (2 * D, 3 * D, 4 * D, 0))
        r.matrix_rooms = tuple(r.bufs.at[at(start, D)] for start in (5 * D, 6 * D, 7 * D, D))
        trunk_section(r, place)


def hand_on(*refs):
    count = len(OUTPUTS)
    given, taken, rooms = (refs[count * part : count * (part + 1)] for part in range(3))
    sems = refs[3 * count]
    ins = [pltpu.make_async_copy(given[n], rooms[n], sems.at[0, n]) for n in range(count)]
    outs = [pltpu.make_async_copy(rooms[n], taken[n], sems.at[1, n]) for n in range(count)]
    for one in ins:
        one.start()
    for first, then in zip(ins, outs):
        first.wait()
        then.start()
    for one in outs:
        one.wait()


def fused_shards(
    patches,
    masks,
    lead_times,
    cotangent,
    patch_weight,
    var_embed,
    attention,
    attn_vectors,
    norm_gains,
    trunk_shifts,
    mlp_in,
    mlp_in_bias,
    mlp_out,
):
    outs = pl.pallas_call(
        fused_kernel,
        in_specs=[pl.BlockSpec(memory_space=space) for space in INPUTS.values()],
        out_specs=[
            pl.BlockSpec(memory_space=pl.ANY if one == (CELL_ROWS, F32) else pltpu.VMEM)
            for one in OUTPUTS.values()
        ],
        out_shape=[jax.ShapeDtypeStruct(*one) for one in OUTPUTS.values()],
        scratch_shapes=[pltpu.VMEM(*one) for one in SCRATCH.values()]
        + [pltpu.SemaphoreType.DMA(one) for one in SEMAPHORES.values()]
        + [pltpu.SemaphoreType.REGULAR((4,))] * 2,
        compiler_params=pltpu.CompilerParams(
            collective_id=0, has_side_effects=True, vmem_limit_bytes=60 * 2**20
        ),
    )(
        patches,
        masks,
        lead_times,
        cotangent,
        patch_weight,
        var_embed,
        attention,
        attn_vectors[0],
        norm_gains,
        trunk_shifts,
        mlp_in,
        mlp_in_bias,
        mlp_out,
    )
    outs = pl.pallas_call(
        hand_on,
        in_specs=[pl.BlockSpec(memory_space=pl.ANY)] * len(outs),
        out_specs=[pl.BlockSpec(memory_space=pl.ANY)] * len(outs),
        out_shape=[jax.ShapeDtypeStruct(*one) for one in OUTPUTS.values()],
        scratch_shapes=[pltpu.VMEM(*one) for one in OUTPUTS.values()]
        + [pltpu.SemaphoreType.DMA((2, len(outs)))],
    )(*outs)
    act, inputs, patch, var, attn, vec, gain, shift, win, bias, wout = outs
    return (
        act.reshape(1, 2, 128, D),
        inputs.reshape(2, 128, 384),
        patch,
        var,
        attn[None],
        vec,
        gain,
        shift,
        win,
        bias.reshape(128),
        wout,
    )


def solution(mesh):
    in_specs = (
        P("dp", None, None),
        P("dp", None, None),
        P("dp"),
        P("dp", None, None),
        P(),
        P(),
        P("section", None, None, None),
        P("section", None, None),
        P(),
        P(),
        P(),
        P(),
        P(),
    )
    out_specs = (
        P("section", "dp", None, None),
        P("dp", None, "section"),
        P(("section", "dp"), None),
        P(),
        P("section", "dp", None),
        P("section", "dp"),
        P(),
        P(),
        P(None, ("section", "dp")),
        P(("section", "dp")),
        P(("section", "dp"), None),
    )
    small = mesh.shape["section"] == 2 and mesh.shape["dp"] == 16
    body = fused_shards if small else shards
    return jax.shard_map(body, mesh=mesh, in_specs=in_specs, out_specs=out_specs, check_vma=False)
```

```python
import functools
import types

import jax
import jax.numpy as jnp
from jax import lax
from jax.experimental import pallas as pl
from jax.experimental.pallas import tpu as pltpu
from jax.sharding import PartitionSpec as P

D = 1024
HEADS = 16
HEAD = 64
FF = 4096
V = 48
PIX = 16


EPSILON = 1e-05
MASKED = -1e30
HIGHEST = lax.Precision.HIGHEST


def shortened(array):
    return jax.tree.map(lambda a: a.astype(jnp.bfloat16) if a.dtype == jnp.float32 else a, array)


def from_behind(value, axis, steps):
    count = lax.axis_size(axis)
    leading, last = (max(0, -steps), min(count, count - steps))
    return lax.ppermute(value, axis, [(source, source + steps) for source in range(leading, last)])


def layer_norm(features, gain_row, shift_row):
    row_mean = jnp.mean(features, axis=-1, keepdims=True)
    centred = features - row_mean
    spread = jnp.mean(centred * centred, axis=-1, keepdims=True)
    return centred * lax.rsqrt(spread + EPSILON) * gain_row + shift_row


def exact_gelu(inputs):
    return jax.nn.gelu(inputs, approximate=False)


def matmul(left_side, right_side):
    return jnp.dot(left_side, right_side, preferred_element_type=jnp.float32)


def matmul_tn(left_side, right_side):
    return lax.dot_general(
        left_side, right_side, (((0,), (0,)), ((), ())), preferred_element_type=jnp.float32
    )


def matmul_nt(left_side, right_side):
    return lax.dot_general(
        left_side, right_side, (((1,), (1,)), ((), ())), preferred_element_type=jnp.float32
    )


def updated(carried, changes):
    merged = dict(carried)
    merged.update(changes)
    return merged


def query_terms(layer_weights, layer_vectors):
    query_vec = matmul(layer_vectors[0][None, :], layer_weights[0])[0] + layer_vectors[1].astype(
        jnp.float32
    )
    key_wide = layer_weights[1].astype(jnp.float32).reshape(D, HEADS, HEAD)
    folded = jnp.einsum("dhk,hk->dh", key_wide, query_vec.reshape(HEADS, HEAD), precision=HIGHEST)
    return (query_vec, key_wide, folded)


def embed_block(pixel_rows, valid_cells, patch_weight, var_embed, folded_low, score_scale):
    cell_count = pixel_rows.shape[0]
    shaped = pixel_rows.reshape(cell_count, V, PIX)
    pieces = jnp.einsum(
        "tvp,vpd->tvd", shaped, patch_weight.reshape(V, PIX, D), preferred_element_type=jnp.float32
    )
    embedded = (pieces + var_embed.astype(jnp.float32)[None]).astype(jnp.bfloat16)
    scores = (
        jnp.einsum("tvd,dh->tvh", embedded, folded_low, preferred_element_type=jnp.float32)
        * score_scale
    )
    scores = jnp.where(valid_cells[:, :, None] > 0, scores, MASKED)
    weights = jax.nn.softmax(scores, axis=1)
    weights_low = weights.astype(jnp.bfloat16)
    pooled = jnp.einsum(
        "tvh,tvd->thd", weights_low, embedded, preferred_element_type=jnp.float32
    ).astype(jnp.bfloat16)
    return (shaped, embedded, weights, weights_low, pooled)


def pool_values(pooled, layer_weights, layer_vectors):
    cell_count = pooled.shape[0]
    projected = jnp.einsum(
        "thd,dhk->thk",
        pooled,
        layer_weights[2].reshape(D, HEADS, HEAD),
        preferred_element_type=jnp.float32,
    )
    return (projected.reshape(cell_count, D) + layer_vectors[2].astype(jnp.float32)).astype(
        jnp.bfloat16
    )


def front_block_back(
    pixel_rows,
    valid_cells,
    d_out,
    patch_weight,
    var_embed,
    layer_weights,
    layer_vectors,
    folded_low,
    score_scale,
):
    shaped, embedded, weights, weights_low, pooled = embed_block(
        pixel_rows, valid_cells, patch_weight, var_embed, folded_low, score_scale
    )
    values_low = pool_values(pooled, layer_weights, layer_vectors)
    cell_count = pixel_rows.shape[0]
    g_bo = jnp.sum(d_out.astype(jnp.float32), axis=0)
    g_wo = matmul_tn(values_low, d_out)
    d_values = matmul_nt(d_out, layer_weights[3])
    g_bv = jnp.sum(d_values, axis=0)
    d_values_low = d_values.astype(jnp.bfloat16).reshape(cell_count, HEADS, HEAD)
    g_wv = jnp.einsum(
        "thd,thk->dhk", pooled, d_values_low, preferred_element_type=jnp.float32
    ).reshape(D, D)
    d_pooled = jnp.einsum(
        "thk,dhk->thd",
        d_values_low,
        layer_weights[2].reshape(D, HEADS, HEAD),
        preferred_element_type=jnp.float32,
    ).astype(jnp.bfloat16)
    d_weights = jnp.einsum("thd,tvd->tvh", d_pooled, embedded, preferred_element_type=jnp.float32)
    d_embedded = jnp.einsum(
        "tvh,thd->tvd", weights_low, d_pooled, preferred_element_type=jnp.float32
    )
    d_scores = (weights * (d_weights - jnp.sum(weights * d_weights, axis=1, keepdims=True))).astype(
        jnp.bfloat16
    )
    g_folded = (
        jnp.einsum("tvd,tvh->dh", embedded, d_scores, preferred_element_type=jnp.float32)
        * score_scale
    )
    d_embedded = (
        d_embedded
        + jnp.einsum("tvh,dh->tvd", d_scores, folded_low, preferred_element_type=jnp.float32)
        * score_scale
    )
    g_var = jnp.sum(d_embedded, axis=0)
    d_embedded_low = d_embedded.astype(jnp.bfloat16)
    g_patch = jnp.einsum(
        "tvp,tvd->vpd", shaped, d_embedded_low, preferred_element_type=jnp.float32
    ).reshape(V * PIX, D)
    d_pixels = jnp.einsum(
        "tvd,vpd->tvp",
        d_embedded_low,
        patch_weight.reshape(V, PIX, D),
        preferred_element_type=jnp.float32,
    ).reshape(cell_count, V * PIX)
    return (g_wv, g_wo, g_bv, g_bo, g_folded, g_var, g_patch, d_pixels)


def layer_two(
    x_in,
    lead_hours,
    d_out,
    layer_weights,
    layer_vectors,
    norm_gains,
    trunk_shifts,
    mlp_in,
    mlp_in_bias,
    mlp_out,
):
    seq_len = x_in.shape[0]
    score_scale = HEAD ** (-0.5)
    gain_rows = norm_gains.astype(jnp.float32)
    shift_rows = trunk_shifts.astype(jnp.float32)
    vec_rows = layer_vectors.astype(jnp.float32)
    lead_scale = lead_hours.astype(jnp.float32) / 100.0
    resid_in = x_in.astype(jnp.float32) + lead_scale * shift_rows[2]
    normed, first_back = jax.vjp(layer_norm, resid_in, gain_rows[0], shift_rows[0])
    normed_low = normed.astype(jnp.bfloat16)
    queries = (
        (matmul(normed_low, layer_weights[0]) + vec_rows[0])
        .astype(jnp.bfloat16)
        .reshape(seq_len, HEADS, HEAD)
    )
    key_rows = (
        matmul(normed_low, layer_weights[1]).astype(jnp.bfloat16).reshape(seq_len, HEADS, HEAD)
    )
    value_rows = (
        (matmul(normed_low, layer_weights[2]) + vec_rows[1])
        .astype(jnp.bfloat16)
        .reshape(seq_len, HEADS, HEAD)
    )
    scores = (
        jnp.einsum("qhd,khd->hqk", queries, key_rows, preferred_element_type=jnp.float32)
        * score_scale
    )
    attn_probs = jax.nn.softmax(scores, axis=-1)
    probs_low = attn_probs.astype(jnp.bfloat16)
    mixed_heads = (
        jnp.einsum("hqk,khd->qhd", probs_low, value_rows, preferred_element_type=jnp.float32)
        .reshape(seq_len, D)
        .astype(jnp.bfloat16)
    )
    resid_mid = resid_in + matmul(mixed_heads, layer_weights[3]) + vec_rows[2]
    normed_two, second_back = jax.vjp(layer_norm, resid_mid, gain_rows[1], shift_rows[1])
    normed_two_low = normed_two.astype(jnp.bfloat16)
    hidden_pre = matmul(normed_two_low, mlp_in) + mlp_in_bias.astype(jnp.float32)
    hidden, gelu_back = jax.vjp(exact_gelu, hidden_pre)
    hidden_low = hidden.astype(jnp.bfloat16)
    produced = (resid_mid + matmul(hidden_low, mlp_out) + vec_rows[3]).astype(jnp.bfloat16)
    d_final = d_out.astype(jnp.float32)
    g_b2 = jnp.sum(d_final, axis=0)
    g_wout = matmul_tn(hidden_low, d_out)
    d_hidden = matmul_nt(d_out, mlp_out)
    d_pre = gelu_back(d_hidden)[0]
    g_bin = jnp.sum(d_pre, axis=0)
    d_pre_low = d_pre.astype(jnp.bfloat16)
    g_win = matmul_tn(normed_two_low, d_pre_low)
    d_mid_norm, g_gain_two, g_shift_two = second_back(matmul_nt(d_pre_low, mlp_in))
    d_mid = d_final + d_mid_norm
    g_bo = jnp.sum(d_mid, axis=0)
    d_mid_low = d_mid.astype(jnp.bfloat16)
    g_wo = matmul_tn(mixed_heads, d_mid_low)
    d_mixed = (
        matmul_nt(d_mid_low, layer_weights[3]).astype(jnp.bfloat16).reshape(seq_len, HEADS, HEAD)
    )
    d_probs = jnp.einsum("qhd,khd->hqk", d_mixed, value_rows, preferred_element_type=jnp.float32)
    d_values = jnp.einsum(
        "hqk,qhd->khd", probs_low, d_mixed, preferred_element_type=jnp.float32
    ).reshape(seq_len, D)
    d_scores = (
        attn_probs * (d_probs - jnp.sum(attn_probs * d_probs, axis=-1, keepdims=True))
    ).astype(jnp.bfloat16)
    d_queries = (
        jnp.einsum("hqk,khd->qhd", d_scores, key_rows, preferred_element_type=jnp.float32).reshape(
            seq_len, D
        )
        * score_scale
    )
    d_keys = (
        jnp.einsum("hqk,qhd->khd", d_scores, queries, preferred_element_type=jnp.float32).reshape(
            seq_len, D
        )
        * score_scale
    )
    g_bq = jnp.sum(d_queries, axis=0)
    g_bv = jnp.sum(d_values, axis=0)
    d_queries_low = d_queries.astype(jnp.bfloat16)
    d_keys_low = d_keys.astype(jnp.bfloat16)
    d_values_low = d_values.astype(jnp.bfloat16)
    g_wq = matmul_tn(normed_low, d_queries_low)
    g_wk = matmul_tn(normed_low, d_keys_low)
    g_wv = matmul_tn(normed_low, d_values_low)
    d_normed = (
        matmul_nt(d_queries_low, layer_weights[0])
        + matmul_nt(d_keys_low, layer_weights[1])
        + matmul_nt(d_values_low, layer_weights[2])
    )
    d_in_norm, g_gain_one, g_shift_one = first_back(d_normed)
    d_in = d_mid + d_in_norm
    g_lead = lead_scale * jnp.sum(d_in, axis=0)
    return (
        produced,
        d_in.astype(jnp.bfloat16),
        jnp.stack([g_wq, g_wk, g_wv, g_wo]),
        jnp.stack([g_bq, g_bv, g_bo, g_b2]),
        jnp.stack([g_gain_one, g_gain_two]),
        jnp.stack([g_shift_one, g_shift_two, g_lead]),
        g_win,
        g_bin,
        g_wout,
    )


def send_forward(sent_rows):
    return from_behind(shortened(sent_rows), "section", 1).astype(sent_rows.dtype)


def shards(
    patches,
    masks,
    lead_times,
    cotangent,
    patch_weight,
    var_embed,
    attention,
    attn_vectors,
    norm_gains,
    trunk_shifts,
    mlp_in,
    mlp_in_bias,
    mlp_out,
):
    micro_count, seq_len, pixel_width = patches.shape
    block_rows = min(128, seq_len)
    score_scale = HEAD ** (-0.5)
    layer_weights = attention[0]
    layer_vectors = attn_vectors[0]
    on_front = lax.axis_index("section") == 0
    empty_rows = jnp.zeros((seq_len, D), jnp.bfloat16)
    carried = {
        "attn": jnp.zeros((4, D, D), jnp.float32),
        "vec": jnp.zeros((4, D), jnp.float32),
        "u_sum": jnp.zeros((D, HEADS), jnp.float32),
        "patch": jnp.zeros((V * PIX, D), jnp.float32),
        "var": jnp.zeros((V, D), jnp.float32),
        "gains": jnp.zeros((2, D), jnp.float32),
        "shifts": jnp.zeros((3, D), jnp.float32),
        "w_in": jnp.zeros((D, FF), jnp.float32),
        "b_in": jnp.zeros((FF,), jnp.float32),
        "w_out": jnp.zeros((FF, D), jnp.float32),
        "outputs": jnp.zeros((micro_count, seq_len, D), jnp.bfloat16),
        "pixels": jnp.zeros((micro_count, seq_len, pixel_width), jnp.float32),
        "returned": jnp.zeros((micro_count, seq_len, D), jnp.bfloat16),
    }

    def front_forward(carried, mb_index):
        query_vec, key_wide, folded = query_terms(layer_weights, layer_vectors)
        folded_low = folded.astype(jnp.bfloat16)
        valid_cells = masks[mb_index, :, 0:block_rows].T
        block_parts = embed_block(
            patches[mb_index, 0:block_rows],
            valid_cells,
            patch_weight,
            var_embed,
            folded_low,
            score_scale,
        )
        values_low = pool_values(block_parts[4], layer_weights, layer_vectors)
        pieces = [
            (matmul(values_low, layer_weights[3]) + layer_vectors[3].astype(jnp.float32)).astype(
                jnp.bfloat16
            )
        ]
        produced = jnp.concatenate(pieces, axis=0)
        return (
            updated(carried, {"outputs": carried["outputs"].at[mb_index].set(produced)}),
            produced,
        )

    def front_backward(carried, mb_index, d_front):
        query_vec, key_wide, folded = query_terms(layer_weights, layer_vectors)
        folded_low = folded.astype(jnp.bfloat16)
        attn_sum = carried["attn"]
        vec_sum = carried["vec"]
        u_total = carried["u_sum"]
        var_total = carried["var"]
        patch_total = carried["patch"]
        valid_cells = masks[mb_index, :, 0:block_rows].T
        block_grads = front_block_back(
            patches[mb_index, 0:block_rows],
            valid_cells,
            d_front[0:block_rows],
            patch_weight,
            var_embed,
            layer_weights,
            layer_vectors,
            folded_low,
            score_scale,
        )
        attn_sum = attn_sum.at[2].add(block_grads[0]).at[3].add(block_grads[1])
        vec_sum = vec_sum.at[2].add(block_grads[2]).at[3].add(block_grads[3])
        u_total = u_total + block_grads[4]
        var_total = var_total + block_grads[5]
        patch_total = patch_total + block_grads[6]
        pixel_pieces = [block_grads[7]]
        pixel_grads = carried["pixels"].at[mb_index].set(jnp.concatenate(pixel_pieces, axis=0))
        return updated(
            carried,
            {
                "attn": attn_sum,
                "vec": vec_sum,
                "u_sum": u_total,
                "var": var_total,
                "patch": patch_total,
                "pixels": pixel_grads,
            },
        )

    def back_step(carried, mb_index, arriving):
        produced, d_front, attn_part, vec_part, gain_part, shift_part, g_win, g_bin, g_wout = (
            layer_two(
                arriving,
                lead_times[mb_index],
                cotangent[mb_index],
                layer_weights,
                layer_vectors,
                norm_gains,
                trunk_shifts,
                mlp_in,
                mlp_in_bias,
                mlp_out,
            )
        )
        changes = {
            "attn": carried["attn"] + attn_part,
            "vec": carried["vec"] + vec_part,
            "gains": carried["gains"] + gain_part,
            "shifts": carried["shifts"] + shift_part,
            "w_in": carried["w_in"] + g_win,
            "b_in": carried["b_in"] + g_bin,
            "w_out": carried["w_out"] + g_wout,
            "outputs": carried["outputs"].at[mb_index].set(produced),
            "returned": carried["returned"].at[mb_index].set(d_front),
        }
        return (updated(carried, changes), d_front)

    def finish_front(carried):
        query_vec, key_wide, folded = query_terms(layer_weights, layer_vectors)
        u_total = carried["u_sum"]
        d_key = (u_total[:, :, None] * query_vec.reshape(HEADS, HEAD)[None]).reshape(D, D)
        d_query_vec = jnp.einsum("dh,dhk->hk", u_total, key_wide, precision=HIGHEST).reshape(D)
        d_query_weight = layer_vectors[0].astype(jnp.float32)[:, None] * d_query_vec[None, :]
        d_query = jnp.dot(layer_weights[0].astype(jnp.float32), d_query_vec, precision=HIGHEST)
        attn_sum = carried["attn"].at[0].set(d_query_weight).at[1].set(d_key)
        vec_sum = carried["vec"].at[0].set(d_query).at[1].set(d_query_vec)
        return updated(carried, {"attn": attn_sum, "vec": vec_sum})

    arriving_act = empty_rows
    for step_number in range(micro_count + 1):

        def front_turn(inputs, step_number=step_number):
            carried, act_in = inputs
            sent_rows = empty_rows
            if step_number < micro_count:
                carried, sent_rows = front_forward(carried, step_number)
            return (carried, sent_rows)

        def back_turn(inputs, step_number=step_number):
            carried, act_in = inputs
            if step_number >= 1:
                carried, returned_rows = back_step(carried, step_number - 1, act_in)
            return (carried, empty_rows)

        carried, sent_act = lax.cond(on_front, front_turn, back_turn, (carried, arriving_act))
        if step_number < micro_count:
            arriving_act = send_forward(sent_act)
    gradients_back = from_behind(shortened(carried["returned"]), "section", -1)

    def front_all(kept_state):
        for mb_index in range(micro_count):
            kept_state = front_backward(kept_state, mb_index, gradients_back[mb_index])
        return kept_state

    carried = lax.cond(on_front, front_all, lambda kept_state: kept_state, carried)
    carried = lax.cond(on_front, finish_front, lambda kept_state: kept_state, carried)
    attn_grads, vec_grads = (
        lax.psum_scatter(
            carried["attn"].reshape(1, 4 * D, D), "dp", scatter_dimension=1, tiled=True
        ),
        lax.psum_scatter(carried["vec"].reshape(1, 4 * D), "dp", scatter_dimension=1, tiled=True),
    )
    win_grads, bin_grads, wout_grads, patch_grads = (
        lax.psum_scatter(carried["w_in"], ("section", "dp"), scatter_dimension=1, tiled=True),
        lax.psum_scatter(carried["b_in"], ("section", "dp"), scatter_dimension=0, tiled=True),
        lax.psum_scatter(carried["w_out"], ("section", "dp"), scatter_dimension=0, tiled=True),
        lax.psum_scatter(carried["patch"], ("section", "dp"), scatter_dimension=0, tiled=True),
    )
    var_grads, gain_grads, shift_grads = lax.psum(
        (carried["var"], carried["gains"], carried["shifts"]), ("section", "dp")
    )
    pixel_half = pixel_width // 2
    moved = from_behind(shortened(carried["pixels"][:, :, pixel_half:]), "section", 1)
    input_grads = jnp.where(on_front, carried["pixels"][:, :, :pixel_half], moved)
    activations = carried["outputs"][None]
    return (
        activations,
        input_grads,
        patch_grads,
        var_grads,
        attn_grads,
        vec_grads,
        gain_grads,
        shift_grads,
        win_grads,
        bin_grads,
        wout_grads,
    )


F32 = jnp.float32
BF = jnp.bfloat16
I32 = jnp.int32
MESH = pl.DeviceIdType.MESH
CELLS = 256
SLOT = 64
WIDE = 1152
LANES = 128
SCALE = 0.125
ROOT_HALF = 0.7071067811865476
ROOT_TAU = 0.3989422804014327


def nn(a, b):
    return jnp.dot(a, b, preferred_element_type=F32)


def nt(a, b):
    return lax.dot_general(a, b, (((1,), (1,)), ((), ())), preferred_element_type=F32)


def tn(a, b):
    return lax.dot_general(a, b, (((0,), (0,)), ((), ())), preferred_element_type=F32)


def at(start, size):
    if isinstance(start, int):
        return pl.ds(start, size)
    return pl.ds(pl.multiple_of(start, size), size)


def each(count, body, unroll=1):
    def step(index, carry):
        body(index)
        return carry

    lax.fori_loop(0, count, step, 0, unroll=unroll)


def iota(shape, dim):
    return lax.broadcasted_iota(I32, shape, dim)


def halves(value):
    high = value.astype(BF)
    return high, (value - high.astype(F32)).astype(BF)


def pixel_column(slot):
    return ((slot & (SLOT - 1)) << 4) + (slot >> 6)


def slot_tile(index, rows, columns):
    match = pixel_column(iota((rows, 1), 0) + index * rows)
    return jnp.where(iota((rows, columns), 1) == match, 1.0, 0.0).astype(BF)


def spread(tile):
    return jnp.concatenate([tile] * (WIDE // LANES), axis=1)


def front_tables(r):
    def place(index):
        tile = slot_tile(index, 256, V * PIX)
        r.table[at(index * 256, 256), :] = nn(tile, r.raw[...]).astype(BF)
        r.pat[:, at(index * 256, 256)] = nt(r.pix[...], tile).astype(BF)

    each(4, place, 4)
    r.table[1024:1072, :] = r.embed[...]
    r.table[1072:WIDE, :] = jnp.zeros((WIDE - 1072, D), BF)
    lane = iota((CELLS, LANES), 1)
    r.pat[:, 1024:WIDE] = jnp.where(lane < V, 1.0, 0.0).astype(BF)
    twice = jnp.where(iota((V, LANES), 1) & (SLOT - 1) == iota((V, LANES), 0), 1.0, 0.0).astype(BF)
    for sample in range(2):
        present = tn(r.masks[sample].astype(F32).astype(BF), twice)
        r.keep[sample * 128 : sample * 128 + 128, :] = present


def front_query(r):
    first = jnp.broadcast_to(r.vecs[0:1, :], (16, D))
    query = nn(first, r.attn[0])[0:1, :] + r.vecs[1:2, :].astype(F32)
    own = iota((HEADS, D), 1) >> 6 == iota((HEADS, D), 0)
    high, low = halves(jnp.where(own, jnp.broadcast_to(query, (HEADS, D)), 0.0))
    r.qhead[0:HEADS, :] = high
    r.qhead[HEADS : 2 * HEADS, :] = low
    both = nt(r.qhead[...], r.attn[1])
    folded = (both[0:HEADS] + both[HEADS : 2 * HEADS]).astype(BF)
    r.fold[...] = folded
    r.score[...] = nt(folded, r.table[...]) * SCALE


def front_values(r):
    def tile(index):
        lanes = at(index * 256, 256)
        r.mid[:, lanes] = nn(r.table[...], r.attn[2, :, lanes]).astype(BF)

    each(4, tile, 4)


def front_scores(r, head, rows):
    row = r.score[pl.ds(head, 1), :]
    total = None
    for k in range(WIDE // LANES):
        cols = slice(k * LANES, (k + 1) * LANES)
        part = r.pat[rows, cols].astype(F32) * row[:, cols]
        total = part if total is None else total + part
    total = total + pltpu.roll(total, SLOT, 1)
    total = jnp.where(r.keep[rows, :] > 0.5, total, MASKED)
    top = jnp.max(total, axis=1, keepdims=True)
    grown = jnp.exp(total - top)
    return grown / (0.5 * jnp.sum(grown, axis=1, keepdims=True))


def front_forward(r, out, sample):
    rows = slice(sample * 128, sample * 128 + 128)
    first_half = iota((128, LANES), 1) < HEAD

    def pair(index):
        lanes = at(index * LANES, LANES)
        pooled = []
        for part in range(2):
            head = index * 2 + part
            weights = front_scores(r, head, rows)
            r.probs[head * 2 + sample] = weights
            pooled.append(r.pat[rows, :] * spread(weights.astype(BF)))
        found = nn(jnp.concatenate(pooled, axis=0), r.mid[:, lanes])
        values = jnp.where(first_half, found[0:128], found[128:256]) + r.vecs[2:3, lanes].astype(F32)
        r.agg[rows, lanes] = values.astype(BF)

    each(HEADS // 2, pair, 2)

    def tile(index):
        lanes = at(index * 256, 256)
        found = nn(r.agg[rows, :], r.attn[3, :, lanes]) + r.vecs[3:4, lanes].astype(F32)
        out[rows, lanes] = found.astype(BF)

    each(4, tile, 4)


def front_back_values(r, d_out, sample):
    cells = slice(sample * 128, sample * 128 + 128)

    def tile(index):
        rows = at(index * 256, 256)
        grad = nt(d_out[cells, :], r.attn[3, rows, :])
        sums = (jnp.sum(grad, axis=0, keepdims=True), jnp.sum(d_out[cells, rows].astype(F32), axis=0, keepdims=True))
        for row, value in zip((16, 17), sums):
            r.small[row : row + 1, rows] = value if sample == 0 else r.small[row : row + 1, rows] + value
        r.dlow[cells, rows] = grad.astype(BF)

    each(4, tile, 4)
    r.turn_a[:, cells] = r.dlow[cells, :].T


def front_back_heads(r, sample):
    rows = slice(sample * 128, sample * 128 + 128)
    first_half = iota((128, LANES), 1) < HEAD
    r.input_sum[rows, :] = jnp.zeros((128, D), F32)

    def pair(index):
        lanes = at(index * LANES, LANES)
        grads = r.dlow[rows, lanes]
        none = jnp.zeros_like(grads)
        own = jnp.concatenate([jnp.where(first_half, grads, none), jnp.where(first_half, none, grads)], axis=0)
        mid = r.mid[:, lanes]
        weights = [r.probs[(index * 2 + part) * 2 + sample] for part in range(2)]
        lows = [weight.astype(BF) for weight in weights]
        totals = [None, None]
        for k in range(WIDE // 384):
            wide = nt(own, mid[k * 384 : (k + 1) * 384, :])
            for j in range(3):
                n = k * 3 + j
                cols = slice(n * LANES, (n + 1) * LANES)
                pixels = r.pat[rows, cols].astype(F32)
                pieces = [wide[part * 128 : part * 128 + 128, j * LANES : (j + 1) * LANES] for part in range(2)]
                for part in range(2):
                    term = pieces[part] * pixels
                    totals[part] = term if totals[part] is None else totals[part] + term
                if n < 8:
                    sums = lows[0].astype(F32) * pieces[0] + lows[1].astype(F32) * pieces[1]
                    r.input_sum[rows, cols] = r.input_sum[rows, cols] + sums
        scores = []
        for part in range(2):
            total = totals[part] + pltpu.roll(totals[part], SLOT, 1)
            inner = 0.5 * jnp.sum(weights[part] * total, axis=1, keepdims=True)
            scores.append((weights[part] * (total - inner)).astype(BF).astype(F32))
        along = [r.score[pl.ds(index * 2 + part, 1), :] for part in range(2)]
        for n in range(9):
            cols = slice(n * LANES, (n + 1) * LANES)
            if n < 8:
                sums = scores[0] * along[0][:, cols] + scores[1] * along[1][:, cols]
                r.input_sum[rows, cols] = r.input_sum[rows, cols] + sums
            pixels = r.pat[rows, cols].astype(F32)
            for part in range(2):
                head = index * 2 + part
                use = SCALE * jnp.sum(scores[part] * pixels, axis=0, keepdims=True)
                r.uses[head, :, cols] = use if sample == 0 else r.uses[head, :, cols] + use
        for part in range(2):
            spot = at((index * 2 + part) * HEAD, HEAD)
            pooled = r.pat[rows, :] * spread(lows[part])
            found = nn(r.turn_a[spot, rows], pooled)
            if sample == 1:
                found = found + r.turned[spot, :].astype(F32)
            r.turned[spot, :] = found.astype(BF)

    each(HEADS // 2, pair, 2)


def put_rows(sums, quarter, value):
    y, c = quarter // 2, quarter % 2
    for j in range(2):
        sums[at(j * 512 + (c * 2 + y) * 128, 128), :] = value[j * 128 : (j + 1) * 128].astype(BF)


def front_back_out(r, d_out):
    r.turn_b[...] = r.agg[...].T

    def tile(index):
        put_rows(r.sums[3], index, nn(r.turn_b[at(index * 256, 256), :], d_out[...]))

    each(4, tile, 4)


def front_back_table(r):
    uses = jnp.concatenate([r.uses[h] for h in range(HEADS)], axis=0).astype(BF)
    r.small[0:16, :] = nn(uses, r.table[...])
    r.mid[...] = r.turned[...].T


def front_back_projection(r):
    def values(index):
        rows = at(index * 256, 256)
        put_rows(r.sums[2], index, tn(r.table[:, rows], r.mid[...]))

    each(4, values, 4)


def front_back_pixels(r):
    uses = jnp.concatenate([r.uses[h] for h in range(HEADS)], axis=0).astype(BF)

    def pixels(index):
        lanes = at(index * 256, 256)
        full = nt(r.mid[...], r.attn[2, lanes, :]) + tn(uses, r.fold[:, lanes])
        r.turned[:, lanes] = full[0:1024].astype(BF)
        r.var_sum[:, lanes] = full[1024:1072].astype(BF)

    each(4, pixels, 4)


def front_back_order(r):
    def order(index):
        row = iota((256, 1), 0) + index * 256
        piece, k = row // 48, row % 48
        owner = ((piece & 1) * 2 + ((piece >> 1) & 1)) * 4 + ((piece >> 2) & 1) * 2 + (piece >> 3)
        natural = owner * 24 + jnp.where(k < 24, k, k + 360)
        slot = (natural & (PIX - 1)) * SLOT + (natural >> 4)
        pick = jnp.where(iota((256, D), 1) == slot, 1.0, 0.0).astype(BF)
        r.patch_sum[at(index * 256, 256), :] = nn(pick, r.turned[:, 0:1024]).astype(BF)

    each(3, order, 3)


def front_back_inputs(r, own_half, other_half):
    low = r.input_sum[...].astype(BF)
    r.dlow[...] = low
    for half, out in ((0, own_half), (1, other_half)):
        column = pixel_column(iota((D, 1), 0)) - half * 384
        pick = jnp.where(iota((D, 384), 1) == column, 1.0, 0.0).astype(BF)
        out[...] = nn(r.dlow[...], pick).astype(out.dtype)


def row_mean(x):
    return jnp.mean(x, axis=1, keepdims=True)


def col_sum(x):
    return jnp.sum(x, axis=0, keepdims=True)


def trunk_ahead(r):
    def tile(index):
        n, k = index // 4, index % 4
        found = nt(r.cot[...], r.bufs[at(4096 + index * 256, 256), :])
        r.grads_flat[at(n * 512, 256), at(k * 256, 256)] = found.astype(BF)

    each(16, tile, 4)
    r.small[3:4, :] = col_sum(r.cot[...].astype(F32))


def normalise(r, source, spread_rows, unit, gain, shift, out):
    def rows_of(index):
        rows = at(index * 64, 64)
        x = source[rows, :]
        centred = x - row_mean(x)
        rstd = lax.rsqrt(row_mean(centred * centred) + EPSILON)
        scaled = centred * rstd
        unit[rows, :] = scaled
        spread_rows[rows, :] = jnp.broadcast_to(rstd, (64, LANES))
        out[rows, :] = (scaled * gain + shift).astype(BF)

    each(4, rows_of, 4)


def trunk_attention(r, front):
    shift_rows = r.shifts[...].astype(F32)
    gain_rows = r.gains[...].astype(F32)

    def enter(index):
        rows = at(index * 128, 128)
        lead = r.leads[index].astype(F32) / 100.0
        r.resid[rows, :] = front[rows, :].astype(F32) + lead * shift_rows[2:3]

    each(2, enter)
    normalise(r, r.resid, r.rstd_one, r.unit_one, gain_rows[0:1], shift_rows[0:1], r.normed)

    def project(index):
        lanes = at(index * 256, 256)
        x = r.normed[...]
        r.q[:, lanes] = (nn(x, r.attn[0, :, lanes]) + r.vecs[0:1, lanes].astype(F32)).astype(BF)
        r.k[:, lanes] = nn(x, r.attn[1, :, lanes]).astype(BF)
        r.v[:, lanes] = (nn(x, r.attn[2, :, lanes]) + r.vecs[1:2, lanes].astype(F32)).astype(BF)

    each(4, project, 4)
    first = iota((128, LANES), 1) < HEAD

    def pair(index):
        sample, hp = index // 8, index % 8
        rows, lanes = at(sample * 128, 128), at(hp * LANES, LANES)
        q, k, v = r.q[rows, lanes], r.k[rows, lanes], r.v[rows, lanes]
        none = jnp.zeros_like(q)
        mixed = None
        for part in range(2):
            mine = first if part == 0 else jnp.logical_not(first)
            scores = nt(jnp.where(mine, q, none), k) * SCALE
            grown = jnp.exp(scores - jnp.max(scores, axis=1, keepdims=True))
            probs = grown / jnp.sum(grown, axis=1, keepdims=True)
            r.probs[index * 2 + part] = probs
            term = nn(probs.astype(BF), jnp.where(mine, v, none))
            mixed = term if mixed is None else mixed + term
        r.mixed[rows, lanes] = mixed.astype(BF)

    each(16, pair, 4)

    def leave(index):
        lanes = at(index * 256, 256)
        grown = nn(r.mixed[...], r.attn[3, :, lanes]) + r.vecs[2:3, lanes].astype(F32)
        r.resid[:, lanes] = r.resid[:, lanes] + grown

    each(4, leave, 4)
    normalise(r, r.resid, r.rstd_two, r.unit_two, gain_rows[1:2], shift_rows[1:2], r.x_own)


def bias_row(r, start, count):
    return r.bias_in[at(start, count)].astype(F32).reshape(1, count)


def curve(x):
    area = 0.5 + 0.5 * lax.erf(x * ROOT_HALF)
    return x * area, area + x * (ROOT_TAU * jnp.exp(-0.5 * x * x))


def trunk_hidden(r):
    def tile(index):
        n, k = index // 4, index % 4
        lanes = at(k * 256, 256)
        pre = nn(r.x_own[...], r.bufs[at(n * 1024, 1024), lanes]) + bias_row(r, index * 256, 256)
        value, slope = curve(pre)
        r.grads_flat[at(n * 512 + 256, 256), lanes] = value.astype(BF)
        r.grads_flat[at(n * 512, 256), lanes] = (r.grads_flat[at(n * 512, 256), lanes].astype(F32) * slope).astype(BF)

    each(16, tile, 4)

    def back(index):
        rows = at(index * 256, 256)
        total = None
        for n in range(4):
            term = nt(r.grads_flat[n * 512 : n * 512 + 256, :], r.bufs[at(n * 1024 + index * 256, 256), :])
            total = term if total is None else total + term
        r.d_mid[:, rows] = total

    each(4, back, 4)


def norm_back(grad, unit, rstd, gain):
    scaled = grad * gain
    along = row_mean(scaled * unit)
    return rstd * (scaled - row_mean(scaled) - unit * along)


def trunk_back(r):
    gain_rows = r.gains[...].astype(F32)
    r.small[2:3, :] = jnp.zeros((1, D), F32)
    r.small[4:9, :] = jnp.zeros((5, D), F32)

    def second(index):
        rows = at(index * 64, 64)
        grad, unit = r.d_mid[rows, :], r.unit_two[rows, :]
        mid = r.cot[rows, :].astype(F32) + norm_back(grad, unit, r.rstd_two[rows, 0:1], gain_rows[1:2])
        r.d_mid[rows, :] = mid
        r.d_low[rows, :] = mid.astype(BF)
        r.small[2:3, :] += col_sum(mid)
        r.small[5:6, :] += col_sum(grad * unit)
        r.small[7:8, :] += col_sum(grad)

    each(4, second, 4)


def trunk_mix(r):
    def mix(index):
        rows = at(index * 256, 256)
        r.second[:, rows] = nt(r.d_low[...], r.attn[3, rows, :]).astype(BF)

    each(4, mix, 4)
    r.small[0:2, :] = jnp.zeros((2, D), F32)


def trunk_back_heads(r, sample):
    first = iota((128, LANES), 1) < HEAD
    rows = slice(sample * 128, sample * 128 + 128)

    def pair(hp):
        index = sample * 8 + hp
        lanes = at(hp * LANES, LANES)
        q, k, v = r.q[rows, lanes], r.k[rows, lanes], r.v[rows, lanes]
        d_mixed = r.second[rows, lanes]
        none = jnp.zeros_like(q)
        d_q = d_k = d_v = None
        for part in range(2):
            mine = first if part == 0 else jnp.logical_not(first)
            own = jnp.where(mine, d_mixed, none)
            probs = r.probs[index * 2 + part]
            d_probs = nt(own, v)
            inner = jnp.sum(probs * d_probs, axis=1, keepdims=True)
            d_scores = (probs * (d_probs - inner)).astype(BF)
            terms = (
                nn(d_scores, jnp.where(mine, k, none)),
                tn(d_scores, jnp.where(mine, q, none)),
                tn(probs.astype(BF), own),
            )
            d_q = terms[0] if d_q is None else d_q + terms[0]
            d_k = terms[1] if d_k is None else d_k + terms[1]
            d_v = terms[2] if d_v is None else d_v + terms[2]
        d_q = d_q * SCALE
        r.q[rows, lanes] = d_q.astype(BF)
        r.k[rows, lanes] = (d_k * SCALE).astype(BF)
        r.v[rows, lanes] = d_v.astype(BF)
        r.small[0:1, lanes] += col_sum(d_q)
        r.small[1:2, lanes] += col_sum(d_v)

    each(8, pair, 4)


def trunk_back_in(r, d_in, sample):
    gain_rows = r.gains[...].astype(F32)
    cells = slice(sample * 128, sample * 128 + 128)

    def inward(index):
        rows = at(index * 256, 256)
        total = nt(r.q[cells, :], r.attn[0, rows, :]) + nt(r.k[cells, :], r.attn[1, rows, :])
        r.unit_two[cells, rows] = total + nt(r.v[cells, :], r.attn[2, rows, :])

    each(4, inward, 4)

    def start(index):
        rows = at(sample * 128 + index * 64, 64)
        grad, unit = r.unit_two[rows, :], r.unit_one[rows, :]
        whole = r.d_mid[rows, :] + norm_back(grad, unit, r.rstd_one[rows, 0:1], gain_rows[0:1])
        d_in[rows, :] = whole.astype(BF)
        lead = r.leads[sample].astype(F32) / 100.0
        r.small[4:5, :] += col_sum(grad * unit)
        r.small[6:7, :] += col_sum(grad)
        r.small[8:9, :] += lead * col_sum(whole)

    each(2, start, 2)


def trunk_out(r, out):
    def tile(index):
        lanes = at(index * 256, 256)
        total = r.resid[:, lanes] + r.vecs[3:4, lanes].astype(F32)
        for n in range(4):
            total = total + nn(r.grads_flat[n * 512 + 256 : n * 512 + 512, :], r.bufs[4096 + n * 1024 : 5120 + n * 1024, lanes])
        out[:, lanes] = total.astype(BF)

    each(4, tile, 4)


def trunk_weight_out(r):
    r.turn_b[...] = r.mixed[...].T

    def quarter(index):
        put_rows(r.sums[3], index, nn(r.turn_b[at(index * 256, 256), :], r.d_low[...]))

    each(4, quarter, 4)


def trunk_weights(r, which):
    right = (r.q, r.k, r.v)[which]

    def quarter(index):
        put_rows(r.sums[which], index, nn(r.turn_a[at(index * 256, 256), :], right[...]))

    each(4, quarter, 4)


def trunk_turn(r):
    r.turn_a[...] = r.normed[...].T


def hidden_loads(r, place, load):
    loads = []
    for part, owner in enumerate((place.me, place.me + 2 - 4 * place.y)):
        units = at((place.section * 16 + owner) * 128, 128)
        side = slice(part * 128, part * 128 + 128)
        loads.append(load(15 + part * 2, r.mlp_in.at[:, units], r.win.at[:, side]))
        loads.append(load(16 + part * 2, r.mlp_out.at[units, :], r.wout.at[side]))
    return loads


def hidden_tables(r, place):
    r.win_t[...] = r.win[...].T
    for part, owner in enumerate((place.me, place.me + 2 - 4 * place.y)):
        both = bias_row(r, (place.section * 16 + owner - place.c) * 128, 256)
        first = jnp.broadcast_to(place.c == 0, (1, 128))
        row = jnp.where(first, both[:, 0:128], both[:, 128:256])
        r.units[part * 128 : part * 128 + 128, :] = jnp.broadcast_to(row, (256, 128)).T
    r.unit_two[...] = jnp.zeros((256, D), F32)
    r.d_mid[...] = jnp.zeros((256, D), F32)
    r.bias_sum[...] = jnp.zeros((256, 256), F32)


def hidden_plane(r, plane):
    def tile(index):
        x, cot = r.gather[plane, at(index * 256, 256), :], r.gather[plane, at(512 + index * 256, 256), :]
        value, slope = curve(nt(r.win_t[...], x) + r.units[...])
        grad = nt(r.wout[...], cot) * slope
        r.bias_sum[...] += grad
        r.unit_two[...] += nn(grad.astype(BF), x)
        r.d_mid[...] += nn(value.astype(BF), cot)

    each(2, tile, 2)


def hidden_gifts(r, place):
    return [
        remote(r.gift, r.gift_in, r.gift_sent.at[0], r.gift_come.at[0], place.beside),
        remote(r.gift_bias, r.gift_bias_in, r.gift_sent.at[1], r.gift_come.at[1], place.beside),
    ]


def hidden_exchange(r, gifts):
    r.gift[0] = r.unit_two[128:256, :].astype(BF)
    r.gift[1] = r.d_mid[128:256, :].astype(BF)
    r.gift_bias[...] = jnp.broadcast_to(col_sum(r.bias_sum[...].T), (8, 256))
    for one in gifts:
        one.start()


def hidden_finish(r, gifts):
    for one in gifts:
        one.wait()
    r.win_out[...] = (r.unit_two[0:128, :] + r.gift_in[0].astype(F32)).T
    r.wout_out[...] = r.d_mid[0:128, :] + r.gift_in[1].astype(F32)
    r.bias_out[...] = r.gift_bias[0:1, 0:128] + r.gift_bias_in[0:1, 128:256]


def remote(source, target, sent, arrived, device):
    return pltpu.make_async_remote_copy(
        src_ref=source,
        dst_ref=target,
        send_sem=sent,
        recv_sem=arrived,
        device_id=device,
        device_id_type=MESH,
    )


class Place:
    def __init__(self):
        self.section = lax.axis_index("section")
        self.me = lax.axis_index("dp")
        self.c = self.me % 2
        self.y = (self.me // 2) % 2
        self.low = (self.me // 4) % 2
        self.high = self.me // 8
        self.across = {"section": 1 - self.section}
        self.core = {"dp": self.me + 1 - 2 * self.c}
        self.beside = {"dp": self.me + 2 - 4 * self.y}
        self.near = {"dp": self.me + 4 - 8 * self.low}
        self.far = {"dp": self.me + 8 - 16 * self.high}
        self.both = {"dp": self.me + 12 - 8 * self.low - 16 * self.high}

    def plane(self, step):
        low = (self.low + step % 2) % 2
        high = (self.high + step // 2) % 2
        return high * 2 + low

    def levels(self):
        return (self.core, self.beside, self.near, self.far)


class Share:
    def __init__(self, r, place, base, sent, arrived):
        self.place, self.base, self.sent, self.arrived = place, base, sent, arrived
        self.buf = r.gather
        self.mine = place.high * 2 + place.low

    def block(self, plane, c):
        return self.buf.at[plane, at(self.base + c * 256, 256)]

    def copy(self, plane, c, number, device):
        block = self.block(plane, c)
        return remote(block, block, self.sent.at[number], self.arrived.at[plane * 2 + c], device)

    def wait(self, plane, c):
        self.copy(plane, c, 0, self.place.core).wait_recv()

    def along(self, plane, number, to_upper):
        device = {"dp": self.place.me + (4 if to_upper else -4)}
        pl.when(self.mine < 3 if to_upper else self.mine > 0)(
            lambda: self.copy(plane, self.place.c, number, device).start()
        )

    def open(self):
        self.along(self.mine, 0, True)
        self.along(self.mine, 1, False)
        self.copy(self.mine, self.place.c, 2 + self.mine, self.place.core).start()

    def pass_on(self, distance):
        for below in (True, False):
            plane = self.mine - distance if below else self.mine + distance

            @pl.when(plane >= 0 if below else plane < 4)
            def _():
                self.wait(plane, self.place.c)
                self.along(plane, 6 + plane, below)
                self.copy(plane, self.place.c, 2 + plane, self.place.core).start()

    def settle(self, plane):
        self.wait(plane, 1 - self.place.c)

    def close(self):
        def done(number):
            self.copy(0, 0, number, self.place.core).wait_send()

        pl.when(self.mine < 3)(lambda: done(0))
        pl.when(self.mine > 0)(lambda: done(1))
        for number in range(2, 6):
            done(number)
        for plane in range(4):
            gone = ((plane < self.mine) & (self.mine < 3)) | ((plane > self.mine) & (self.mine > 0))
            pl.when(gone)(functools.partial(done, 6 + plane))


class Halving:
    def __init__(self, place, source, room, sizes, sent, arrived, done, target=None):
        self.place, self.source, self.room, self.sizes = place, source, room, sizes
        self.sent, self.arrived, self.done, self.target = sent, arrived, done, target
        self.bits = (place.c, place.y, place.low, place.high)

    def takes(self, level):
        if self.target is None or level < 2:
            return None
        on_low = self.place.low == self.target[0]
        return on_low if level == 2 else on_low & (self.place.high == self.target[1])

    def gives(self, level):
        if self.target is None or level < 2:
            return None
        on_low = self.place.low == self.target[0]
        return jnp.logical_not(on_low) if level == 2 else on_low & (self.place.high != self.target[1])

    def when(self, condition, action):
        if condition is None:
            action()
        else:
            pl.when(condition)(action)

    def part(self, j, level, side):
        rows = self.sizes[level]
        start = 0 if self.target is not None and level >= 2 else side * rows
        return self.source(j, start, rows) if level == 0 else self.room(j, level - 1, start, rows)

    def copy(self, j, level):
        give = self.part(j, level, 1 - self.bits[level])
        target = self.room(j, level, 0, self.sizes[level])
        device = self.place.levels()[level]
        return remote(give, target, self.sent.at[j, level], self.arrived.at[j, level], device)

    def begin(self, j, level):
        self.when(self.gives(level), lambda: self.copy(j, level).start())

    def finish(self, j, level):
        self.when(self.takes(level), lambda: self.take(j, level))
        if level < 3:
            self.begin(j, level + 1)

    def take(self, j, level):
        self.copy(j, level).wait_recv()
        mine = self.part(j, level, self.bits[level])
        room = self.room(j, level, 0, self.sizes[level])
        step = 64 if self.sizes[level] % 64 == 0 else 48

        def add(index):
            rows = at(index * step, step)
            total = mine[rows, :].astype(F32) + room[rows, :].astype(F32)
            if level == 3:
                self.done(j, index * step, total)
            else:
                room[rows, :] = total.astype(BF)

        each(self.sizes[level] // step, add)

    def close(self, j):
        for level in range(4):
            self.when(self.gives(level), lambda: self.copy(j, level).wait_send())


class Doubling:
    def __init__(self, place, rows, own, come, sent, arrived):
        self.place, self.rows, self.own, self.come = place, rows, own, come
        self.sent, self.arrived = sent, arrived

    def before(self, level):
        return self.own.at[0 : self.rows] if level == 0 else self.come.at[level - 1, 0 : self.rows]

    def copy(self, level):
        target = self.come.at[level, 0 : self.rows]
        device = self.place.levels()[level]
        return remote(self.before(level), target, self.sent.at[level], self.arrived.at[level], device)

    def begin(self):
        self.copy(0).start()

    def finish(self, level):
        self.copy(level).wait_recv()
        room = self.come.at[level, 0 : self.rows]
        total = self.before(level)[...].astype(F32) + room[...].astype(F32)
        room[...] = total.astype(room.dtype)
        if level < 3:
            self.copy(level + 1).start()

    def close(self):
        for level in range(4):
            self.copy(level).wait_send()


def matrix_sums(r, place, which):
    sums, rooms = r.sums[which], r.matrix_rooms[which]
    starts = (0, 256, 384)

    def room(j, level, start, rows):
        if level == 3:
            return r.last_room.at[at(j * 128 + start, rows)]
        return rooms.at[at(j * 512 + starts[level] + start, rows)]

    def done(j, start, value):
        r.attn_out[at(j * 128 + start, 64), :] = value

    return Halving(
        place,
        lambda j, start, rows: sums.at[at(j * 512 + start, rows)],
        room,
        (256, 128, 128, 128),
        r.sum_sent.at[:, at(which * 4, 4)],
        r.sum_come.at[:, at(which * 4, 4)],
        done,
        (which % 2, which // 2),
    )


def greet(place):
    barrier = pltpu.get_barrier_semaphore()
    devices = (place.across, place.core, place.beside, place.near, place.far, place.both)
    for device in devices:
        pl.semaphore_signal(barrier, inc=1, device_id=device, device_id_type=MESH)
    return lambda: pl.semaphore_wait(barrier, len(devices))


def across(r, place, number, source, target):
    return remote(source, target, r.over_sent.at[number], r.over_come.at[number], place.across)


def front_tail(r, place):
    own = at((place.y * 2 + place.c) * 256, 256)
    high, low = halves(r.small_in[3, 0:16])
    r.fold_sum[0:16, :] = high
    r.fold_sum[16:32, :] = low
    both = nn(r.fold_sum[...], r.attn[1])
    mine = iota((HEADS, D), 1) >> 6 == iota((HEADS, D), 0)
    query = col_sum(jnp.where(mine, both[0:HEADS] + both[HEADS : 2 * HEADS], 0.0))
    r.query_row[0:1, :] = query
    high, low = halves(query)
    row = iota((16, D), 0)
    pair = jnp.where(row == 0, high.astype(F32), jnp.where(row == 1, low.astype(F32), 0.0))
    r.query_pair[...] = pair.astype(BF)

    @pl.when(place.high + place.low == 0)
    def _():
        first = jnp.broadcast_to(r.vecs[0:1, own].astype(F32), (16, 256))
        first = jnp.where(iota((16, 256), 0) < 2, first, 0.0).astype(BF)
        r.attn_out[...] = tn(first, r.query_pair[...])
        r.vec_out[...] = col_sum(nt(r.query_pair[...], r.attn[0, own, :]))

    @pl.when((place.high == 0) & (place.low == 1))
    def _():
        left = jnp.concatenate([r.fold_sum[0:16, own], r.fold_sum[16:32, own], r.fold_sum[0:16, own]], axis=0)
        right = jnp.concatenate([r.qhead[0:16, :], r.qhead[0:16, :], r.qhead[16:32, :]], axis=0)
        r.attn_out[...] = tn(left, right)
        r.vec_out[...] = r.query_row[0:1, own]

    @pl.when(place.high == 1)
    def _():
        r.vec_out[...] = r.small_in[3, pl.ds(16 + place.low, 1), own]


def front_section(r, place):
    def load(number, source, target):
        return pltpu.make_async_copy(source, target, r.loads.at[number])

    cots = Share(r, place, 512, r.cot_sent, r.cot_come)
    hiddens = Share(r, place, 0, r.x_sent, r.x_come)
    mine = hiddens.mine
    loads = [
        load(0, r.patches_in.at[0], r.pix.at[0:128]),
        load(1, r.patches_in.at[1], r.pix.at[128:256]),
        load(2, r.weight_in, r.raw),
        load(7, r.cot_in.at[0], cots.block(mine, place.c).at[0:128]),
        load(8, r.cot_in.at[1], cots.block(mine, place.c).at[128:256]),
        load(3, r.attn_in.at[0, 0], r.attn.at[0]),
        load(4, r.attn_in.at[0, 1], r.attn.at[1]),
        load(5, r.attn_in.at[0, 2], r.attn.at[2]),
        load(6, r.attn_in.at[0, 3], r.attn.at[3]),
    ]
    units = hidden_loads(r, place, load)
    met = greet(place)
    for one in loads + units:
        one.start()
    r.small[16:24, :] = jnp.zeros((8, D), F32)
    for one in loads[0:3]:
        one.wait()
    front_tables(r)
    loads[3].wait()
    loads[4].wait()
    met()
    cots.open()
    loads[5].wait()
    loads[6].wait()
    front_query(r)
    loads[7].wait()
    front_values(r)
    loads[8].wait()
    send_front = []
    for sample in range(2):
        front_forward(r, r.act_out, sample)
        rows = slice(sample * 128, sample * 128 + 128)
        send_front.append(across(r, place, (0, 3)[sample], r.act_out.at[rows], r.arrive.at[rows]))
        send_front[sample].start()
    for one in units:
        one.wait()
    hidden_tables(r, place)
    for distance in range(1, 4):
        cots.pass_on(distance)
    for plane in range(4):
        cots.settle(plane)
    near = mine + 1 - 2 * place.low
    far = mine + 2 - 4 * place.high
    both = 3 - mine

    def patch_done(j, start, value):
        r.patch_out[...] = value[0:24]
        r.gift_patch[...] = value[24:48]

    values, outs = matrix_sums(r, place, 2), matrix_sums(r, place, 3)
    patch_starts = (0, 384, 576, 672)
    pixels = Halving(
        place,
        lambda j, start, rows: r.patch_sum.at[at(start, rows)],
        lambda j, level, start, rows: r.patch_rooms.at[at(patch_starts[level] + start, rows)],
        (384, 192, 96, 48),
        r.patch_sent,
        r.patch_come,
        patch_done,
    )
    smalls = Doubling(place, 24, r.small, r.small_in, r.small_sent, r.small_come)
    embeds = Doubling(place, 48, r.var_sum, r.var_in, r.var_sent, r.var_come)
    gifts = hidden_gifts(r, place)
    give_half = across(r, place, 2, r.gift_half, r.gift_half)
    give_patch = across(r, place, 6, r.gift_patch, r.gift_patch)
    give_var = across(r, place, 5, r.var_in.at[3], r.gift_var)

    def cells():
        hiddens.wait(mine, place.c)
        hiddens.open()

    def plane(which):
        hiddens.settle(which)
        hidden_plane(r, which)

    def come(sample):
        rows = slice(sample * 128, sample * 128 + 128)
        across(r, place, (1, 4)[sample], r.leave.at[rows], r.arrive.at[rows]).wait_recv()

    def back_out():
        front_back_out(r, r.arrive)
        outs.begin(0, 0)
        outs.begin(1, 0)

    def projection():
        front_back_projection(r)
        values.begin(0, 0)
        values.begin(1, 0)

    def table():
        front_back_table(r)
        smalls.begin()

    def pixel_rows():
        front_back_pixels(r)
        embeds.begin()

    def order():
        front_back_order(r)
        pixels.begin(0, 0)

    def inputs():
        front_back_inputs(r, r.input_out, r.gift_half)
        give_half.start()

    def patch_last():
        pixels.finish(0, 3)
        give_patch.start()

    def var_last():
        embeds.finish(3)
        give_var.start()

    t = types.SimpleNamespace(
        cells=cells,
        own=lambda: plane(mine),
        pass1=lambda: hiddens.pass_on(1),
        near=lambda: plane(near),
        come0=lambda: come(0),
        come1=lambda: come(1),
        back_out=back_out,
        back_values0=lambda: front_back_values(r, r.arrive, 0),
        back_values1=lambda: front_back_values(r, r.arrive, 1),
        pass2=lambda: hiddens.pass_on(2),
        heads0=lambda: front_back_heads(r, 0),
        heads1=lambda: front_back_heads(r, 1),
        table=table,
        projection=projection,
        pass3=lambda: hiddens.pass_on(3),
        pixel_rows=pixel_rows,
        order=order,
        inputs=inputs,
        far=lambda: plane(far),
        both=lambda: plane(both),
        exchange=lambda: hidden_exchange(r, gifts),
        small0=lambda: smalls.finish(0),
        small1=lambda: smalls.finish(1),
        small2=lambda: smalls.finish(2),
        small3=lambda: smalls.finish(3),
        tail=lambda: front_tail(r, place),
        embed0=lambda: embeds.finish(0),
        embed1=lambda: embeds.finish(1),
        embed2=lambda: embeds.finish(2),
        embed3=var_last,
        patch0=lambda: pixels.finish(0, 0),
        patch1=lambda: pixels.finish(0, 1),
        patch2=lambda: pixels.finish(0, 2),
        patch3=patch_last,
        a00=lambda: outs.finish(0, 0),
        a01=lambda: outs.finish(0, 1),
        a02=lambda: outs.finish(0, 2),
        a03=lambda: outs.finish(0, 3),
        a10=lambda: outs.finish(1, 0),
        a11=lambda: outs.finish(1, 1),
        a12=lambda: outs.finish(1, 2),
        a13=lambda: outs.finish(1, 3),
        v00=lambda: values.finish(0, 0),
        v01=lambda: values.finish(0, 1),
        v02=lambda: values.finish(0, 2),
        v03=lambda: values.finish(0, 3),
        v10=lambda: values.finish(1, 0),
        v11=lambda: values.finish(1, 1),
        v12=lambda: values.finish(1, 2),
        v13=lambda: values.finish(1, 3),
    )
    t.cells()
    t.pass1()
    t.come0()
    t.back_values0()
    t.heads0()
    t.come1()
    t.back_out()
    t.a00()
    t.back_values1()
    t.pass2()
    t.heads1()
    t.a10()
    t.a01()
    t.table()
    t.projection()
    t.inputs()
    t.small0()
    t.a11()
    t.v00()
    t.pass3()
    t.pixel_rows()
    t.order()
    t.a02()
    t.embed0()
    t.small1()
    t.v01()
    t.patch0()
    t.small2()
    t.both()
    t.embed1()
    t.a12()
    t.v10()
    t.far()
    t.near()
    t.embed2()
    t.small3()
    t.patch1()
    t.v11()
    t.v02()
    t.own()
    t.embed3()
    t.exchange()
    t.patch2()
    t.v03()
    t.a13()
    t.tail()
    t.v12()
    t.a03()
    t.patch3()
    t.v13()
    give_attn = load(13, r.attn_out, r.attn_final)
    give_attn.start()
    r.var_out[...] = r.var_in[3].astype(F32)
    hidden_finish(r, gifts)
    across(r, place, 7, r.small_in.at[3, 0:16], r.gift_small).wait_recv()
    r.gain_out[...] = r.gift_small[4:6, :]
    r.shift_out[...] = r.gift_small[6:9, :]
    cots.close()
    hiddens.close()
    for j in range(2):
        values.close(j)
        outs.close(j)
    pixels.close(0)
    smalls.close()
    embeds.close()
    for one in (*send_front, give_half, give_var, give_patch):
        one.wait_send()
    give_attn.wait()


def trunk_section(r, place):
    def load(number, source, target):
        return pltpu.make_async_copy(source, target, r.loads.at[number])

    cots = Share(r, place, 512, r.cot_sent, r.cot_come)
    hiddens = Share(r, place, 0, r.x_sent, r.x_come)
    mine = hiddens.mine
    r.cot = cots.block(mine, place.c)
    r.x_own = hiddens.block(mine, place.c)
    given = [load(4 + n, r.cot_in.at[n], r.cot.at[n * 128 : (n + 1) * 128]) for n in range(2)]
    outs = [load(n, r.mlp_out.at[n * 1024 : (n + 1) * 1024], r.bufs.at[4096 + n * 1024 : 5120 + n * 1024]) for n in range(4)]
    attns = [load(6 + n, r.attn_in.at[0, n], r.attn.at[n]) for n in range(4)]
    ins = [load(10 + n, r.mlp_in.at[:, n * 1024 : (n + 1) * 1024], r.bufs.at[n * 1024 : (n + 1) * 1024]) for n in range(4)]
    met = greet(place)
    for one in (*given, *outs, *attns, *ins):
        one.start()
    met()
    r.small[...] = jnp.zeros((24, D), F32)
    for one in given:
        one.wait()
    cots.open()
    for one in outs:
        one.wait()
    trunk_ahead(r)
    for one in (*attns, *ins):
        one.wait()
    cots.pass_on(1)
    for sample in range(2):
        rows = slice(sample * 128, sample * 128 + 128)
        across(r, place, (0, 3)[sample], r.act_out.at[rows], r.arrive.at[rows]).wait_recv()
    send_x = remote(r.x_own, r.x_own, r.over_sent.at[0], r.x_come.at[mine * 2 + place.c], place.across)
    halves_of = [slice(sample * 128, sample * 128 + 128) for sample in range(2)]
    send_in = [
        across(r, place, number, r.leave.at[rows], r.arrive.at[rows]) for number, rows in zip((1, 4), halves_of)
    ]
    send_small = across(r, place, 7, r.small_in.at[3, 0:16], r.gift_small)
    near = mine + 1 - 2 * place.low
    far = mine + 2 - 4 * place.high
    both = 3 - mine
    sums = [matrix_sums(r, place, which) for which in range(4)]
    queries, keys, values, outs_sum = sums
    smalls = Doubling(place, 24, r.small, r.small_in, r.small_sent, r.small_come)
    gifts = hidden_gifts(r, place)
    units = hidden_loads(r, place, load)

    def tell(ready):
        for level, device in enumerate(place.levels()):
            pl.semaphore_signal(ready.at[level], inc=1, device_id=device, device_id_type=MESH)

    def heed(ready):
        for level in range(4):
            pl.semaphore_wait(ready.at[level], 1)

    def attention():
        trunk_attention(r, r.arrive)
        send_x.start()
        hiddens.open()

    def hidden():
        trunk_hidden(r)
        tell(r.ready)

    def weight_out():
        trunk_weight_out(r)
        heed(r.ready)
        outs_sum.begin(0, 0)
        outs_sum.begin(1, 0)

    def back_in(sample):
        trunk_back_in(r, r.leave, sample)
        send_in[sample].start()
        if sample == 1:
            smalls.begin()

    def out():
        trunk_out(r, r.act_out)
        tell(r.ready_two)

    def weights(which):
        trunk_weights(r, which)
        if which == 2:
            heed(r.ready_two)
        sums[which].begin(0, 0)
        sums[which].begin(1, 0)

    def tables():
        for one in units:
            one.start()
        for one in units:
            one.wait()
        hidden_tables(r, place)

    def plane(which):
        cots.settle(which)
        hiddens.settle(which)
        hidden_plane(r, which)

    def small_last():
        smalls.finish(3)
        send_small.start()

    t = types.SimpleNamespace(
        attention=attention,
        cot2=lambda: cots.pass_on(2),
        hidden=hidden,
        cot3=lambda: cots.pass_on(3),
        back=lambda: trunk_back(r),
        weight_out=weight_out,
        pass1=lambda: hiddens.pass_on(1),
        mix=lambda: trunk_mix(r),
        back_heads0=lambda: trunk_back_heads(r, 0),
        back_heads1=lambda: trunk_back_heads(r, 1),
        back_in0=lambda: back_in(0),
        back_in1=lambda: back_in(1),
        pass2=lambda: hiddens.pass_on(2),
        out=out,
        turn=lambda: trunk_turn(r),
        weight_v=lambda: weights(2),
        weight_k=lambda: weights(1),
        weight_q=lambda: weights(0),
        tables=tables,
        own=lambda: plane(mine),
        near=lambda: plane(near),
        pass3=lambda: hiddens.pass_on(3),
        far=lambda: plane(far),
        both=lambda: plane(both),
        exchange=lambda: hidden_exchange(r, gifts),
        small0=lambda: smalls.finish(0),
        small1=lambda: smalls.finish(1),
        small2=lambda: smalls.finish(2),
        small3=small_last,
        a00=lambda: outs_sum.finish(0, 0),
        a01=lambda: outs_sum.finish(0, 1),
        a02=lambda: outs_sum.finish(0, 2),
        a03=lambda: outs_sum.finish(0, 3),
        a10=lambda: outs_sum.finish(1, 0),
        a11=lambda: outs_sum.finish(1, 1),
        a12=lambda: outs_sum.finish(1, 2),
        a13=lambda: outs_sum.finish(1, 3),
        v00=lambda: values.finish(0, 0),
        v01=lambda: values.finish(0, 1),
        v02=lambda: values.finish(0, 2),
        v03=lambda: values.finish(0, 3),
        v10=lambda: values.finish(1, 0),
        v11=lambda: values.finish(1, 1),
        v12=lambda: values.finish(1, 2),
        v13=lambda: values.finish(1, 3),
        k00=lambda: keys.finish(0, 0),
        k01=lambda: keys.finish(0, 1),
        k02=lambda: keys.finish(0, 2),
        k03=lambda: keys.finish(0, 3),
        k10=lambda: keys.finish(1, 0),
        k11=lambda: keys.finish(1, 1),
        k12=lambda: keys.finish(1, 2),
        k13=lambda: keys.finish(1, 3),
        q00=lambda: queries.finish(0, 0),
        q01=lambda: queries.finish(0, 1),
        q02=lambda: queries.finish(0, 2),
        q03=lambda: queries.finish(0, 3),
        q10=lambda: queries.finish(1, 0),
        q11=lambda: queries.finish(1, 1),
        q12=lambda: queries.finish(1, 2),
        q13=lambda: queries.finish(1, 3),
    )
    t.cot2()
    t.attention()
    t.hidden()
    t.turn()
    t.back()
    t.mix()
    t.back_heads0()
    t.weight_out()
    t.back_in0()
    t.pass1()
    t.a00()
    t.back_heads1()
    t.back_in1()
    t.a10()
    t.a01()
    t.small0()
    t.out()
    t.cot3()
    t.weight_v()
    t.v10()
    t.pass2()
    t.weight_k()
    t.weight_q()
    t.k10()
    t.tables()
    t.own()
    t.v00()
    t.v11()
    t.q00()
    t.k11()
    t.pass3()
    t.both()
    t.near()
    t.k00()
    t.a02()
    t.small1()
    t.far()
    t.v01()
    t.q10()
    t.q01()
    t.k01()
    t.exchange()
    t.q02()
    t.k12()
    t.small2()
    t.v02()
    t.k02()
    t.v12()
    t.q11()
    t.small3()
    t.a03()
    t.a11()
    t.q12()
    t.k13()
    t.a12()
    t.v03()
    t.v13()
    t.q03()
    t.a13()
    t.q13()
    t.k03()
    own = at((place.y * 2 + place.c) * 256, 256)
    r.vec_out[...] = r.small_in[3, pl.ds(mine, 1), own]
    r.gain_out[...] = r.small_in[3, 4:6]
    r.shift_out[...] = r.small_in[3, 6:9]
    give_attn = load(14, r.attn_out, r.attn_final)
    give_attn.start()
    hidden_finish(r, gifts)
    across(r, place, 2, r.gift_half, r.gift_half).wait_recv()
    r.input_out[...] = r.gift_half[...].astype(F32)
    across(r, place, 5, r.var_in.at[3], r.gift_var).wait_recv()
    r.var_out[...] = r.gift_var[...].astype(F32)
    across(r, place, 6, r.gift_patch, r.gift_patch).wait_recv()
    r.patch_out[...] = r.gift_patch[...]
    cots.close()
    hiddens.close()
    for one in sums:
        for j in range(2):
            one.close(j)
    smalls.close()
    for one in (send_x, *send_in, send_small):
        one.wait_send()
    give_attn.wait()


CELL_ROWS = (CELLS, D)
SCRATCH = dict(
    attn=((4, D, D), BF),
    bufs=((8 * D, D), BF),
    gather=((4, D, D), BF),
    last_room=((256, D), BF),
    grads_flat=((2 * D, D), BF),
    turned=((D, WIDE), BF),
    pat=((CELLS, WIDE), BF),
    qhead=((32, D), BF),
    fold=((16, D), BF),
    fold_sum=((32, D), BF),
    query_pair=((16, D), BF),
    query_row=((8, D), F32),
    score=((16, WIDE), F32),
    uses=((16, 1, WIDE), F32),
    probs=((32, 128, 128), F32),
    resid=(CELL_ROWS, F32),
    unit_one=(CELL_ROWS, F32),
    unit_two=(CELL_ROWS, F32),
    d_mid=(CELL_ROWS, F32),
    rstd_one=((CELLS, LANES), F32),
    rstd_two=((CELLS, LANES), F32),
    normed=(CELL_ROWS, BF),
    k=(CELL_ROWS, BF),
    v=(CELL_ROWS, BF),
    mixed=(CELL_ROWS, BF),
    d_low=(CELL_ROWS, BF),
    arrive=(CELL_ROWS, BF),
    turn_a=((D, CELLS), BF),
    turn_b=((D, CELLS), BF),
    small=((24, D), F32),
    small_in=((4, 24, D), F32),
    var_sum=((48, D), BF),
    var_in=((4, 48, D), BF),
    gift=((2, 128, D), BF),
    gift_in=((2, 128, D), BF),
    gift_bias=((8, 256), F32),
    gift_bias_in=((8, 256), F32),
    gift_var=((48, D), BF),
    gift_small=((16, D), F32),
    gift_patch=((24, D), F32),
    gift_half=((CELLS, 384), BF),
)
SEMAPHORES = dict(
    loads=(19,),
    over_sent=(8,),
    over_come=(8,),
    cot_sent=(10,),
    cot_come=(8,),
    x_sent=(10,),
    x_come=(8,),
    var_sent=(4,),
    var_come=(4,),
    gift_sent=(2,),
    gift_come=(2,),
    sum_sent=(2, 16),
    sum_come=(2, 16),
    patch_sent=(1, 4),
    patch_come=(1, 4),
    small_sent=(4,),
    small_come=(4,),
)
INPUTS = dict(
    patches_in=pl.ANY,
    masks=pltpu.VMEM,
    leads=pltpu.SMEM,
    cot_in=pl.ANY,
    weight_in=pl.ANY,
    embed=pltpu.VMEM,
    attn_in=pl.ANY,
    vecs=pltpu.VMEM,
    gains=pltpu.VMEM,
    shifts=pltpu.VMEM,
    mlp_in=pl.ANY,
    bias_in=pltpu.VMEM,
    mlp_out=pl.ANY,
)
OUTPUTS = dict(
    act_out=(CELL_ROWS, BF),
    input_out=((CELLS, 384), F32),
    patch_out=((24, D), F32),
    var_out=((48, D), F32),
    attn_final=(CELL_ROWS, F32),
    vec_out=((1, 256), F32),
    gain_out=((2, D), F32),
    shift_out=((3, D), F32),
    win_out=((D, 128), F32),
    bias_out=((1, 128), F32),
    wout_out=((128, D), F32),
)


class Refs:
    pass


def fused_kernel(*refs):
    r = Refs()
    names = list(INPUTS) + list(OUTPUTS) + list(SCRATCH) + list(SEMAPHORES) + ["ready", "ready_two"]
    for name, ref in zip(names, refs, strict=True):
        setattr(r, name, ref)
    r.table = r.bufs.at[0:WIDE]
    r.mid = r.bufs.at[WIDE : 2 * WIDE]
    r.patch_rooms = r.bufs.at[4352:5072]
    r.patch_sum = r.table.at[0:768]
    r.raw = r.turned.at[0:768, 0:D]
    for number, name in enumerate(("q", "second", "leave")):
        setattr(r, name, r.turned.at[number * 256 : number * 256 + 256, 0:D])
    r.pix = r.normed.at[:, 0 : V * PIX]
    r.input_sum = r.resid
    r.attn_out = r.resid
    r.agg = r.mixed
    r.dlow = r.d_low
    r.wout = r.k
    r.win_t = r.v
    r.win = r.turn_a
    r.keep = r.rstd_one
    r.units = r.unit_one.at[:, 0:256]
    r.bias_sum = r.unit_one.at[:, 256:512]
    place = Place()

    @pl.when(place.section == 0)
    def _():
        r.sums = (None, None, r.grads_flat.at[0:D], r.grads_flat.at[D : 2 * D])
        r.matrix_rooms = (None, None, r.bufs.at[2304:3328], r.bufs.at[3328:4352])
        front_section(r, place)

    @pl.when(place.section == 1)
    def _():
        r.sums = tuple(r.bufs.at[at(start, D)] for start in (2 * D, 3 * D, 4 * D, 0))
        r.matrix_rooms = tuple(r.bufs.at[at(start, D)] for start in (5 * D, 6 * D, 7 * D, D))
        trunk_section(r, place)


def hand_on(*refs):
    count = len(OUTPUTS)
    given, taken, rooms = (refs[count * part : count * (part + 1)] for part in range(3))
    sems = refs[3 * count]
    ins = [pltpu.make_async_copy(given[n], rooms[n], sems.at[0, n]) for n in range(count)]
    outs = [pltpu.make_async_copy(rooms[n], taken[n], sems.at[1, n]) for n in range(count)]
    for one in ins:
        one.start()
    for first, then in zip(ins, outs):
        first.wait()
        then.start()
    for one in outs:
        one.wait()


def fused_shards(
    patches,
    masks,
    lead_times,
    cotangent,
    patch_weight,
    var_embed,
    attention,
    attn_vectors,
    norm_gains,
    trunk_shifts,
    mlp_in,
    mlp_in_bias,
    mlp_out,
):
    outs = pl.pallas_call(
        fused_kernel,
        in_specs=[pl.BlockSpec(memory_space=space) for space in INPUTS.values()],
        out_specs=[
            pl.BlockSpec(memory_space=pl.ANY if one == (CELL_ROWS, F32) else pltpu.VMEM)
            for one in OUTPUTS.values()
        ],
        out_shape=[jax.ShapeDtypeStruct(*one) for one in OUTPUTS.values()],
        scratch_shapes=[pltpu.VMEM(*one) for one in SCRATCH.values()]
        + [pltpu.SemaphoreType.DMA(one) for one in SEMAPHORES.values()]
        + [pltpu.SemaphoreType.REGULAR((4,))] * 2,
        compiler_params=pltpu.CompilerParams(
            collective_id=0, has_side_effects=True, vmem_limit_bytes=60 * 2**20
        ),
    )(
        patches,
        masks,
        lead_times,
        cotangent,
        patch_weight,
        var_embed,
        attention,
        attn_vectors[0],
        norm_gains,
        trunk_shifts,
        mlp_in,
        mlp_in_bias,
        mlp_out,
    )
    outs = pl.pallas_call(
        hand_on,
        in_specs=[pl.BlockSpec(memory_space=pl.ANY)] * len(outs),
        out_specs=[pl.BlockSpec(memory_space=pl.ANY)] * len(outs),
        out_shape=[jax.ShapeDtypeStruct(*one) for one in OUTPUTS.values()],
        scratch_shapes=[pltpu.VMEM(*one) for one in OUTPUTS.values()]
        + [pltpu.SemaphoreType.DMA((2, len(outs)))],
    )(*outs)
    act, inputs, patch, var, attn, vec, gain, shift, win, bias, wout = outs
    return (
        act.reshape(1, 2, 128, D),
        inputs.reshape(2, 128, 384),
        patch,
        var,
        attn[None],
        vec,
        gain,
        shift,
        win,
        bias.reshape(128),
        wout,
    )


def solution(mesh):
    in_specs = (
        P("dp", None, None),
        P("dp", None, None),
        P("dp"),
        P("dp", None, None),
        P(),
        P(),
        P("section", None, None, None),
        P("section", None, None),
        P(),
        P(),
        P(),
        P(),
        P(),
    )
    out_specs = (
        P("section", "dp", None, None),
        P("dp", None, "section"),
        P(("section", "dp"), None),
        P(),
        P("section", "dp", None),
        P("section", "dp"),
        P(),
        P(),
        P(None, ("section", "dp")),
        P(("section", "dp")),
        P(("section", "dp"), None),
    )
    small = mesh.shape["section"] == 2 and mesh.shape["dp"] == 16
    body = fused_shards if small else shards
    return jax.shard_map(body, mesh=mesh, in_specs=in_specs, out_specs=out_specs, check_vma=False)
```

```python
import functools
import types

import jax
import jax.numpy as jnp
from jax import lax
from jax.experimental import pallas as pl
from jax.experimental.pallas import tpu as pltpu
from jax.sharding import PartitionSpec as P

D = 1024
HEADS = 16
HEAD = 64
FF = 4096
V = 48
PIX = 16


EPSILON = 1e-05
MASKED = -1e30
HIGHEST = lax.Precision.HIGHEST


def shortened(array):
    return jax.tree.map(lambda a: a.astype(jnp.bfloat16) if a.dtype == jnp.float32 else a, array)


def from_behind(value, axis, steps):
    count = lax.axis_size(axis)
    leading, last = (max(0, -steps), min(count, count - steps))
    return lax.ppermute(value, axis, [(source, source + steps) for source in range(leading, last)])


def layer_norm(features, gain_row, shift_row):
    row_mean = jnp.mean(features, axis=-1, keepdims=True)
    centred = features - row_mean
    spread = jnp.mean(centred * centred, axis=-1, keepdims=True)
    return centred * lax.rsqrt(spread + EPSILON) * gain_row + shift_row


def exact_gelu(inputs):
    return jax.nn.gelu(inputs, approximate=False)


def matmul(left_side, right_side):
    return jnp.dot(left_side, right_side, preferred_element_type=jnp.float32)


def matmul_tn(left_side, right_side):
    return lax.dot_general(
        left_side, right_side, (((0,), (0,)), ((), ())), preferred_element_type=jnp.float32
    )


def matmul_nt(left_side, right_side):
    return lax.dot_general(
        left_side, right_side, (((1,), (1,)), ((), ())), preferred_element_type=jnp.float32
    )


def updated(carried, changes):
    merged = dict(carried)
    merged.update(changes)
    return merged


def query_terms(layer_weights, layer_vectors):
    query_vec = matmul(layer_vectors[0][None, :], layer_weights[0])[0] + layer_vectors[1].astype(
        jnp.float32
    )
    key_wide = layer_weights[1].astype(jnp.float32).reshape(D, HEADS, HEAD)
    folded = jnp.einsum("dhk,hk->dh", key_wide, query_vec.reshape(HEADS, HEAD), precision=HIGHEST)
    return (query_vec, key_wide, folded)


def embed_block(pixel_rows, valid_cells, patch_weight, var_embed, folded_low, score_scale):
    cell_count = pixel_rows.shape[0]
    shaped = pixel_rows.reshape(cell_count, V, PIX)
    pieces = jnp.einsum(
        "tvp,vpd->tvd", shaped, patch_weight.reshape(V, PIX, D), preferred_element_type=jnp.float32
    )
    embedded = (pieces + var_embed.astype(jnp.float32)[None]).astype(jnp.bfloat16)
    scores = (
        jnp.einsum("tvd,dh->tvh", embedded, folded_low, preferred_element_type=jnp.float32)
        * score_scale
    )
    scores = jnp.where(valid_cells[:, :, None] > 0, scores, MASKED)
    weights = jax.nn.softmax(scores, axis=1)
    weights_low = weights.astype(jnp.bfloat16)
    pooled = jnp.einsum(
        "tvh,tvd->thd", weights_low, embedded, preferred_element_type=jnp.float32
    ).astype(jnp.bfloat16)
    return (shaped, embedded, weights, weights_low, pooled)


def pool_values(pooled, layer_weights, layer_vectors):
    cell_count = pooled.shape[0]
    projected = jnp.einsum(
        "thd,dhk->thk",
        pooled,
        layer_weights[2].reshape(D, HEADS, HEAD),
        preferred_element_type=jnp.float32,
    )
    return (projected.reshape(cell_count, D) + layer_vectors[2].astype(jnp.float32)).astype(
        jnp.bfloat16
    )


def front_block_back(
    pixel_rows,
    valid_cells,
    d_out,
    patch_weight,
    var_embed,
    layer_weights,
    layer_vectors,
    folded_low,
    score_scale,
):
    shaped, embedded, weights, weights_low, pooled = embed_block(
        pixel_rows, valid_cells, patch_weight, var_embed, folded_low, score_scale
    )
    values_low = pool_values(pooled, layer_weights, layer_vectors)
    cell_count = pixel_rows.shape[0]
    g_bo = jnp.sum(d_out.astype(jnp.float32), axis=0)
    g_wo = matmul_tn(values_low, d_out)
    d_values = matmul_nt(d_out, layer_weights[3])
    g_bv = jnp.sum(d_values, axis=0)
    d_values_low = d_values.astype(jnp.bfloat16).reshape(cell_count, HEADS, HEAD)
    g_wv = jnp.einsum(
        "thd,thk->dhk", pooled, d_values_low, preferred_element_type=jnp.float32
    ).reshape(D, D)
    d_pooled = jnp.einsum(
        "thk,dhk->thd",
        d_values_low,
        layer_weights[2].reshape(D, HEADS, HEAD),
        preferred_element_type=jnp.float32,
    ).astype(jnp.bfloat16)
    d_weights = jnp.einsum("thd,tvd->tvh", d_pooled, embedded, preferred_element_type=jnp.float32)
    d_embedded = jnp.einsum(
        "tvh,thd->tvd", weights_low, d_pooled, preferred_element_type=jnp.float32
    )
    d_scores = (weights * (d_weights - jnp.sum(weights * d_weights, axis=1, keepdims=True))).astype(
        jnp.bfloat16
    )
    g_folded = (
        jnp.einsum("tvd,tvh->dh", embedded, d_scores, preferred_element_type=jnp.float32)
        * score_scale
    )
    d_embedded = (
        d_embedded
        + jnp.einsum("tvh,dh->tvd", d_scores, folded_low, preferred_element_type=jnp.float32)
        * score_scale
    )
    g_var = jnp.sum(d_embedded, axis=0)
    d_embedded_low = d_embedded.astype(jnp.bfloat16)
    g_patch = jnp.einsum(
        "tvp,tvd->vpd", shaped, d_embedded_low, preferred_element_type=jnp.float32
    ).reshape(V * PIX, D)
    d_pixels = jnp.einsum(
        "tvd,vpd->tvp",
        d_embedded_low,
        patch_weight.reshape(V, PIX, D),
        preferred_element_type=jnp.float32,
    ).reshape(cell_count, V * PIX)
    return (g_wv, g_wo, g_bv, g_bo, g_folded, g_var, g_patch, d_pixels)


def layer_two(
    x_in,
    lead_hours,
    d_out,
    layer_weights,
    layer_vectors,
    norm_gains,
    trunk_shifts,
    mlp_in,
    mlp_in_bias,
    mlp_out,
):
    seq_len = x_in.shape[0]
    score_scale = HEAD ** (-0.5)
    gain_rows = norm_gains.astype(jnp.float32)
    shift_rows = trunk_shifts.astype(jnp.float32)
    vec_rows = layer_vectors.astype(jnp.float32)
    lead_scale = lead_hours.astype(jnp.float32) / 100.0
    resid_in = x_in.astype(jnp.float32) + lead_scale * shift_rows[2]
    normed, first_back = jax.vjp(layer_norm, resid_in, gain_rows[0], shift_rows[0])
    normed_low = normed.astype(jnp.bfloat16)
    queries = (
        (matmul(normed_low, layer_weights[0]) + vec_rows[0])
        .astype(jnp.bfloat16)
        .reshape(seq_len, HEADS, HEAD)
    )
    key_rows = (
        matmul(normed_low, layer_weights[1]).astype(jnp.bfloat16).reshape(seq_len, HEADS, HEAD)
    )
    value_rows = (
        (matmul(normed_low, layer_weights[2]) + vec_rows[1])
        .astype(jnp.bfloat16)
        .reshape(seq_len, HEADS, HEAD)
    )
    scores = (
        jnp.einsum("qhd,khd->hqk", queries, key_rows, preferred_element_type=jnp.float32)
        * score_scale
    )
    attn_probs = jax.nn.softmax(scores, axis=-1)
    probs_low = attn_probs.astype(jnp.bfloat16)
    mixed_heads = (
        jnp.einsum("hqk,khd->qhd", probs_low, value_rows, preferred_element_type=jnp.float32)
        .reshape(seq_len, D)
        .astype(jnp.bfloat16)
    )
    resid_mid = resid_in + matmul(mixed_heads, layer_weights[3]) + vec_rows[2]
    normed_two, second_back = jax.vjp(layer_norm, resid_mid, gain_rows[1], shift_rows[1])
    normed_two_low = normed_two.astype(jnp.bfloat16)
    hidden_pre = matmul(normed_two_low, mlp_in) + mlp_in_bias.astype(jnp.float32)
    hidden, gelu_back = jax.vjp(exact_gelu, hidden_pre)
    hidden_low = hidden.astype(jnp.bfloat16)
    produced = (resid_mid + matmul(hidden_low, mlp_out) + vec_rows[3]).astype(jnp.bfloat16)
    d_final = d_out.astype(jnp.float32)
    g_b2 = jnp.sum(d_final, axis=0)
    g_wout = matmul_tn(hidden_low, d_out)
    d_hidden = matmul_nt(d_out, mlp_out)
    d_pre = gelu_back(d_hidden)[0]
    g_bin = jnp.sum(d_pre, axis=0)
    d_pre_low = d_pre.astype(jnp.bfloat16)
    g_win = matmul_tn(normed_two_low, d_pre_low)
    d_mid_norm, g_gain_two, g_shift_two = second_back(matmul_nt(d_pre_low, mlp_in))
    d_mid = d_final + d_mid_norm
    g_bo = jnp.sum(d_mid, axis=0)
    d_mid_low = d_mid.astype(jnp.bfloat16)
    g_wo = matmul_tn(mixed_heads, d_mid_low)
    d_mixed = (
        matmul_nt(d_mid_low, layer_weights[3]).astype(jnp.bfloat16).reshape(seq_len, HEADS, HEAD)
    )
    d_probs = jnp.einsum("qhd,khd->hqk", d_mixed, value_rows, preferred_element_type=jnp.float32)
    d_values = jnp.einsum(
        "hqk,qhd->khd", probs_low, d_mixed, preferred_element_type=jnp.float32
    ).reshape(seq_len, D)
    d_scores = (
        attn_probs * (d_probs - jnp.sum(attn_probs * d_probs, axis=-1, keepdims=True))
    ).astype(jnp.bfloat16)
    d_queries = (
        jnp.einsum("hqk,khd->qhd", d_scores, key_rows, preferred_element_type=jnp.float32).reshape(
            seq_len, D
        )
        * score_scale
    )
    d_keys = (
        jnp.einsum("hqk,qhd->khd", d_scores, queries, preferred_element_type=jnp.float32).reshape(
            seq_len, D
        )
        * score_scale
    )
    g_bq = jnp.sum(d_queries, axis=0)
    g_bv = jnp.sum(d_values, axis=0)
    d_queries_low = d_queries.astype(jnp.bfloat16)
    d_keys_low = d_keys.astype(jnp.bfloat16)
    d_values_low = d_values.astype(jnp.bfloat16)
    g_wq = matmul_tn(normed_low, d_queries_low)
    g_wk = matmul_tn(normed_low, d_keys_low)
    g_wv = matmul_tn(normed_low, d_values_low)
    d_normed = (
        matmul_nt(d_queries_low, layer_weights[0])
        + matmul_nt(d_keys_low, layer_weights[1])
        + matmul_nt(d_values_low, layer_weights[2])
    )
    d_in_norm, g_gain_one, g_shift_one = first_back(d_normed)
    d_in = d_mid + d_in_norm
    g_lead = lead_scale * jnp.sum(d_in, axis=0)
    return (
        produced,
        d_in.astype(jnp.bfloat16),
        jnp.stack([g_wq, g_wk, g_wv, g_wo]),
        jnp.stack([g_bq, g_bv, g_bo, g_b2]),
        jnp.stack([g_gain_one, g_gain_two]),
        jnp.stack([g_shift_one, g_shift_two, g_lead]),
        g_win,
        g_bin,
        g_wout,
    )


def send_forward(sent_rows):
    return from_behind(shortened(sent_rows), "section", 1).astype(sent_rows.dtype)


def shards(
    patches,
    masks,
    lead_times,
    cotangent,
    patch_weight,
    var_embed,
    attention,
    attn_vectors,
    norm_gains,
    trunk_shifts,
    mlp_in,
    mlp_in_bias,
    mlp_out,
):
    micro_count, seq_len, pixel_width = patches.shape
    block_rows = min(128, seq_len)
    score_scale = HEAD ** (-0.5)
    layer_weights = attention[0]
    layer_vectors = attn_vectors[0]
    on_front = lax.axis_index("section") == 0
    empty_rows = jnp.zeros((seq_len, D), jnp.bfloat16)
    carried = {
        "attn": jnp.zeros((4, D, D), jnp.float32),
        "vec": jnp.zeros((4, D), jnp.float32),
        "u_sum": jnp.zeros((D, HEADS), jnp.float32),
        "patch": jnp.zeros((V * PIX, D), jnp.float32),
        "var": jnp.zeros((V, D), jnp.float32),
        "gains": jnp.zeros((2, D), jnp.float32),
        "shifts": jnp.zeros((3, D), jnp.float32),
        "w_in": jnp.zeros((D, FF), jnp.float32),
        "b_in": jnp.zeros((FF,), jnp.float32),
        "w_out": jnp.zeros((FF, D), jnp.float32),
        "outputs": jnp.zeros((micro_count, seq_len, D), jnp.bfloat16),
        "pixels": jnp.zeros((micro_count, seq_len, pixel_width), jnp.float32),
        "returned": jnp.zeros((micro_count, seq_len, D), jnp.bfloat16),
    }

    def front_forward(carried, mb_index):
        query_vec, key_wide, folded = query_terms(layer_weights, layer_vectors)
        folded_low = folded.astype(jnp.bfloat16)
        valid_cells = masks[mb_index, :, 0:block_rows].T
        block_parts = embed_block(
            patches[mb_index, 0:block_rows],
            valid_cells,
            patch_weight,
            var_embed,
            folded_low,
            score_scale,
        )
        values_low = pool_values(block_parts[4], layer_weights, layer_vectors)
        pieces = [
            (matmul(values_low, layer_weights[3]) + layer_vectors[3].astype(jnp.float32)).astype(
                jnp.bfloat16
            )
        ]
        produced = jnp.concatenate(pieces, axis=0)
        return (
            updated(carried, {"outputs": carried["outputs"].at[mb_index].set(produced)}),
            produced,
        )

    def front_backward(carried, mb_index, d_front):
        query_vec, key_wide, folded = query_terms(layer_weights, layer_vectors)
        folded_low = folded.astype(jnp.bfloat16)
        attn_sum = carried["attn"]
        vec_sum = carried["vec"]
        u_total = carried["u_sum"]
        var_total = carried["var"]
        patch_total = carried["patch"]
        valid_cells = masks[mb_index, :, 0:block_rows].T
        block_grads = front_block_back(
            patches[mb_index, 0:block_rows],
            valid_cells,
            d_front[0:block_rows],
            patch_weight,
            var_embed,
            layer_weights,
            layer_vectors,
            folded_low,
            score_scale,
        )
        attn_sum = attn_sum.at[2].add(block_grads[0]).at[3].add(block_grads[1])
        vec_sum = vec_sum.at[2].add(block_grads[2]).at[3].add(block_grads[3])
        u_total = u_total + block_grads[4]
        var_total = var_total + block_grads[5]
        patch_total = patch_total + block_grads[6]
        pixel_pieces = [block_grads[7]]
        pixel_grads = carried["pixels"].at[mb_index].set(jnp.concatenate(pixel_pieces, axis=0))
        return updated(
            carried,
            {
                "attn": attn_sum,
                "vec": vec_sum,
                "u_sum": u_total,
                "var": var_total,
                "patch": patch_total,
                "pixels": pixel_grads,
            },
        )

    def back_step(carried, mb_index, arriving):
        produced, d_front, attn_part, vec_part, gain_part, shift_part, g_win, g_bin, g_wout = (
            layer_two(
                arriving,
                lead_times[mb_index],
                cotangent[mb_index],
                layer_weights,
                layer_vectors,
                norm_gains,
                trunk_shifts,
                mlp_in,
                mlp_in_bias,
                mlp_out,
            )
        )
        changes = {
            "attn": carried["attn"] + attn_part,
            "vec": carried["vec"] + vec_part,
            "gains": carried["gains"] + gain_part,
            "shifts": carried["shifts"] + shift_part,
            "w_in": carried["w_in"] + g_win,
            "b_in": carried["b_in"] + g_bin,
            "w_out": carried["w_out"] + g_wout,
            "outputs": carried["outputs"].at[mb_index].set(produced),
            "returned": carried["returned"].at[mb_index].set(d_front),
        }
        return (updated(carried, changes), d_front)

    def finish_front(carried):
        query_vec, key_wide, folded = query_terms(layer_weights, layer_vectors)
        u_total = carried["u_sum"]
        d_key = (u_total[:, :, None] * query_vec.reshape(HEADS, HEAD)[None]).reshape(D, D)
        d_query_vec = jnp.einsum("dh,dhk->hk", u_total, key_wide, precision=HIGHEST).reshape(D)
        d_query_weight = layer_vectors[0].astype(jnp.float32)[:, None] * d_query_vec[None, :]
        d_query = jnp.dot(layer_weights[0].astype(jnp.float32), d_query_vec, precision=HIGHEST)
        attn_sum = carried["attn"].at[0].set(d_query_weight).at[1].set(d_key)
        vec_sum = carried["vec"].at[0].set(d_query).at[1].set(d_query_vec)
        return updated(carried, {"attn": attn_sum, "vec": vec_sum})

    arriving_act = empty_rows
    for step_number in range(micro_count + 1):

        def front_turn(inputs, step_number=step_number):
            carried, act_in = inputs
            sent_rows = empty_rows
            if step_number < micro_count:
                carried, sent_rows = front_forward(carried, step_number)
            return (carried, sent_rows)

        def back_turn(inputs, step_number=step_number):
            carried, act_in = inputs
            if step_number >= 1:
                carried, returned_rows = back_step(carried, step_number - 1, act_in)
            return (carried, empty_rows)

        carried, sent_act = lax.cond(on_front, front_turn, back_turn, (carried, arriving_act))
        if step_number < micro_count:
            arriving_act = send_forward(sent_act)
    gradients_back = from_behind(shortened(carried["returned"]), "section", -1)

    def front_all(kept_state):
        for mb_index in range(micro_count):
            kept_state = front_backward(kept_state, mb_index, gradients_back[mb_index])
        return kept_state

    carried = lax.cond(on_front, front_all, lambda kept_state: kept_state, carried)
    carried = lax.cond(on_front, finish_front, lambda kept_state: kept_state, carried)
    attn_grads, vec_grads = (
        lax.psum_scatter(
            carried["attn"].reshape(1, 4 * D, D), "dp", scatter_dimension=1, tiled=True
        ),
        lax.psum_scatter(carried["vec"].reshape(1, 4 * D), "dp", scatter_dimension=1, tiled=True),
    )
    win_grads, bin_grads, wout_grads, patch_grads = (
        lax.psum_scatter(carried["w_in"], ("section", "dp"), scatter_dimension=1, tiled=True),
        lax.psum_scatter(carried["b_in"], ("section", "dp"), scatter_dimension=0, tiled=True),
        lax.psum_scatter(carried["w_out"], ("section", "dp"), scatter_dimension=0, tiled=True),
        lax.psum_scatter(carried["patch"], ("section", "dp"), scatter_dimension=0, tiled=True),
    )
    var_grads, gain_grads, shift_grads = lax.psum(
        (carried["var"], carried["gains"], carried["shifts"]), ("section", "dp")
    )
    pixel_half = pixel_width // 2
    moved = from_behind(shortened(carried["pixels"][:, :, pixel_half:]), "section", 1)
    input_grads = jnp.where(on_front, carried["pixels"][:, :, :pixel_half], moved)
    activations = carried["outputs"][None]
    return (
        activations,
        input_grads,
        patch_grads,
        var_grads,
        attn_grads,
        vec_grads,
        gain_grads,
        shift_grads,
        win_grads,
        bin_grads,
        wout_grads,
    )


F32 = jnp.float32
BF = jnp.bfloat16
I32 = jnp.int32
MESH = pl.DeviceIdType.MESH
CELLS = 256
SLOT = 64
WIDE = 1152
LANES = 128
SCALE = 0.125
ROOT_HALF = 0.7071067811865476
ROOT_TAU = 0.3989422804014327


def nn(a, b):
    return jnp.dot(a, b, preferred_element_type=F32)


def nt(a, b):
    return lax.dot_general(a, b, (((1,), (1,)), ((), ())), preferred_element_type=F32)


def tn(a, b):
    return lax.dot_general(a, b, (((0,), (0,)), ((), ())), preferred_element_type=F32)


def at(start, size):
    if isinstance(start, int):
        return pl.ds(start, size)
    return pl.ds(pl.multiple_of(start, size), size)


def each(count, body, unroll=1):
    def step(index, carry):
        body(index)
        return carry

    lax.fori_loop(0, count, step, 0, unroll=unroll)


def iota(shape, dim):
    return lax.broadcasted_iota(I32, shape, dim)


def halves(value):
    high = value.astype(BF)
    return high, (value - high.astype(F32)).astype(BF)


def pixel_column(slot):
    return ((slot & (SLOT - 1)) << 4) + (slot >> 6)


def slot_tile(index, rows, columns):
    match = pixel_column(iota((rows, 1), 0) + index * rows)
    return jnp.where(iota((rows, columns), 1) == match, 1.0, 0.0).astype(BF)


def spread(tile):
    return jnp.concatenate([tile] * (WIDE // LANES), axis=1)


def front_tables(r):
    def place(index):
        tile = slot_tile(index, 256, V * PIX)
        r.table[at(index * 256, 256), :] = nn(tile, r.raw[...]).astype(BF)
        r.pat[:, at(index * 256, 256)] = nt(r.pix[...], tile).astype(BF)

    each(4, place, 4)
    r.table[1024:1072, :] = r.embed[...]
    r.table[1072:WIDE, :] = jnp.zeros((WIDE - 1072, D), BF)
    lane = iota((CELLS, LANES), 1)
    r.pat[:, 1024:WIDE] = jnp.where(lane < V, 1.0, 0.0).astype(BF)
    twice = jnp.where(iota((V, LANES), 1) & (SLOT - 1) == iota((V, LANES), 0), 1.0, 0.0).astype(BF)
    for sample in range(2):
        present = tn(r.masks[sample].astype(F32).astype(BF), twice)
        r.keep[sample * 128 : sample * 128 + 128, :] = present


def front_query(r):
    first = jnp.broadcast_to(r.vecs[0:1, :], (16, D))
    query = nn(first, r.attn[0])[0:1, :] + r.vecs[1:2, :].astype(F32)
    own = iota((HEADS, D), 1) >> 6 == iota((HEADS, D), 0)
    high, low = halves(jnp.where(own, jnp.broadcast_to(query, (HEADS, D)), 0.0))
    r.qhead[0:HEADS, :] = high
    r.qhead[HEADS : 2 * HEADS, :] = low
    both = nt(r.qhead[...], r.attn[1])
    folded = (both[0:HEADS] + both[HEADS : 2 * HEADS]).astype(BF)
    r.fold[...] = folded
    r.score[...] = nt(folded, r.table[...]) * SCALE


def front_values(r):
    def tile(index):
        lanes = at(index * 256, 256)
        r.mid[:, lanes] = nn(r.table[...], r.attn[2, :, lanes]).astype(BF)

    each(4, tile, 4)


def front_scores(r, head, rows):
    row = r.score[pl.ds(head, 1), :]
    total = None
    for k in range(WIDE // LANES):
        cols = slice(k * LANES, (k + 1) * LANES)
        part = r.pat[rows, cols].astype(F32) * row[:, cols]
        total = part if total is None else total + part
    total = total + pltpu.roll(total, SLOT, 1)
    total = jnp.where(r.keep[rows, :] > 0.5, total, MASKED)
    top = jnp.max(total, axis=1, keepdims=True)
    grown = jnp.exp(total - top)
    return grown / (0.5 * jnp.sum(grown, axis=1, keepdims=True))


def front_forward(r, out, sample):
    rows = slice(sample * 128, sample * 128 + 128)
    first_half = iota((128, LANES), 1) < HEAD

    def pair(index):
        lanes = at(index * LANES, LANES)
        pooled = []
        for part in range(2):
            head = index * 2 + part
            weights = front_scores(r, head, rows)
            r.probs[head * 2 + sample] = weights
            pooled.append(r.pat[rows, :] * spread(weights.astype(BF)))
        found = nn(jnp.concatenate(pooled, axis=0), r.mid[:, lanes])
        values = jnp.where(first_half, found[0:128], found[128:256]) + r.vecs[2:3, lanes].astype(F32)
        r.agg[rows, lanes] = values.astype(BF)

    each(HEADS // 2, pair, 2)

    def tile(index):
        lanes = at(index * 256, 256)
        found = nn(r.agg[rows, :], r.attn[3, :, lanes]) + r.vecs[3:4, lanes].astype(F32)
        out[rows, lanes] = found.astype(BF)

    each(4, tile, 4)


def front_back_values(r, d_out, sample):
    cells = slice(sample * 128, sample * 128 + 128)

    def tile(index):
        rows = at(index * 256, 256)
        grad = nt(d_out[cells, :], r.attn[3, rows, :])
        sums = (jnp.sum(grad, axis=0, keepdims=True), jnp.sum(d_out[cells, rows].astype(F32), axis=0, keepdims=True))
        for row, value in zip((16, 17), sums):
            r.small[row : row + 1, rows] = value if sample == 0 else r.small[row : row + 1, rows] + value
        r.dlow[cells, rows] = grad.astype(BF)

    each(4, tile, 4)
    r.turn_a[:, cells] = r.dlow[cells, :].T


def front_back_heads(r, sample):
    rows = slice(sample * 128, sample * 128 + 128)
    first_half = iota((128, LANES), 1) < HEAD
    r.input_sum[rows, :] = jnp.zeros((128, D), F32)

    def pair(index):
        lanes = at(index * LANES, LANES)
        grads = r.dlow[rows, lanes]
        none = jnp.zeros_like(grads)
        own = jnp.concatenate([jnp.where(first_half, grads, none), jnp.where(first_half, none, grads)], axis=0)
        mid = r.mid[:, lanes]
        weights = [r.probs[(index * 2 + part) * 2 + sample] for part in range(2)]
        lows = [weight.astype(BF) for weight in weights]
        totals = [None, None]
        for k in range(WIDE // 384):
            wide = nt(own, mid[k * 384 : (k + 1) * 384, :])
            for j in range(3):
                n = k * 3 + j
                cols = slice(n * LANES, (n + 1) * LANES)
                pixels = r.pat[rows, cols].astype(F32)
                pieces = [wide[part * 128 : part * 128 + 128, j * LANES : (j + 1) * LANES] for part in range(2)]
                for part in range(2):
                    term = pieces[part] * pixels
                    totals[part] = term if totals[part] is None else totals[part] + term
                if n < 8:
                    sums = lows[0].astype(F32) * pieces[0] + lows[1].astype(F32) * pieces[1]
                    r.input_sum[rows, cols] = r.input_sum[rows, cols] + sums
        scores = []
        for part in range(2):
            total = totals[part] + pltpu.roll(totals[part], SLOT, 1)
            inner = 0.5 * jnp.sum(weights[part] * total, axis=1, keepdims=True)
            scores.append((weights[part] * (total - inner)).astype(BF).astype(F32))
        along = [r.score[pl.ds(index * 2 + part, 1), :] for part in range(2)]
        for n in range(9):
            cols = slice(n * LANES, (n + 1) * LANES)
            if n < 8:
                sums = scores[0] * along[0][:, cols] + scores[1] * along[1][:, cols]
                r.input_sum[rows, cols] = r.input_sum[rows, cols] + sums
            pixels = r.pat[rows, cols].astype(F32)
            for part in range(2):
                head = index * 2 + part
                use = SCALE * jnp.sum(scores[part] * pixels, axis=0, keepdims=True)
                r.uses[head, :, cols] = use if sample == 0 else r.uses[head, :, cols] + use
        for part in range(2):
            spot = at((index * 2 + part) * HEAD, HEAD)
            pooled = r.pat[rows, :] * spread(lows[part])
            found = nn(r.turn_a[spot, rows], pooled)
            if sample == 1:
                found = found + r.turned[spot, :].astype(F32)
            r.turned[spot, :] = found.astype(BF)

    each(HEADS // 2, pair, 2)


def put_rows(sums, quarter, value):
    y, c = quarter // 2, quarter % 2
    for j in range(2):
        sums[at(j * 512 + (c * 2 + y) * 128, 128), :] = value[j * 128 : (j + 1) * 128].astype(BF)


def front_back_out(r, d_out):
    r.turn_b[...] = r.agg[...].T

    def tile(index):
        put_rows(r.sums[3], index, nn(r.turn_b[at(index * 256, 256), :], d_out[...]))

    each(4, tile, 4)


def front_back_table(r):
    uses = jnp.concatenate([r.uses[h] for h in range(HEADS)], axis=0).astype(BF)
    r.small[0:16, :] = nn(uses, r.table[...])
    r.mid[...] = r.turned[...].T


def front_back_projection(r):
    def values(index):
        rows = at(index * 256, 256)
        put_rows(r.sums[2], index, tn(r.table[:, rows], r.mid[...]))

    each(4, values, 4)


def front_back_pixels(r):
    uses = jnp.concatenate([r.uses[h] for h in range(HEADS)], axis=0).astype(BF)

    def pixels(index):
        lanes = at(index * 256, 256)
        full = nt(r.mid[...], r.attn[2, lanes, :]) + tn(uses, r.fold[:, lanes])
        r.turned[:, lanes] = full[0:1024].astype(BF)
        r.var_sum[:, lanes] = full[1024:1072].astype(BF)

    each(4, pixels, 4)


def front_back_order(r):
    def order(index):
        row = iota((256, 1), 0) + index * 256
        piece, k = row // 48, row % 48
        owner = ((piece & 1) * 2 + ((piece >> 1) & 1)) * 4 + ((piece >> 2) & 1) * 2 + (piece >> 3)
        natural = owner * 24 + jnp.where(k < 24, k, k + 360)
        slot = (natural & (PIX - 1)) * SLOT + (natural >> 4)
        pick = jnp.where(iota((256, D), 1) == slot, 1.0, 0.0).astype(BF)
        r.patch_sum[at(index * 256, 256), :] = nn(pick, r.turned[:, 0:1024]).astype(BF)

    each(3, order, 3)


def front_back_inputs(r, own_half, other_half):
    low = r.input_sum[...].astype(BF)
    r.dlow[...] = low
    for half, out in ((0, own_half), (1, other_half)):
        column = pixel_column(iota((D, 1), 0)) - half * 384
        pick = jnp.where(iota((D, 384), 1) == column, 1.0, 0.0).astype(BF)
        out[...] = nn(r.dlow[...], pick).astype(out.dtype)


def row_mean(x):
    return jnp.mean(x, axis=1, keepdims=True)


def col_sum(x):
    return jnp.sum(x, axis=0, keepdims=True)


def trunk_ahead(r):
    def tile(index):
        n, k = index // 4, index % 4
        found = nt(r.cot[...], r.bufs[at(4096 + index * 256, 256), :])
        r.grads_flat[at(n * 512, 256), at(k * 256, 256)] = found.astype(BF)

    each(16, tile, 4)
    r.small[3:4, :] = col_sum(r.cot[...].astype(F32))


def normalise(r, source, spread_rows, unit, gain, shift, out):
    def rows_of(index):
        rows = at(index * 64, 64)
        x = source[rows, :]
        centred = x - row_mean(x)
        rstd = lax.rsqrt(row_mean(centred * centred) + EPSILON)
        scaled = centred * rstd
        unit[rows, :] = scaled
        spread_rows[rows, :] = jnp.broadcast_to(rstd, (64, LANES))
        out[rows, :] = (scaled * gain + shift).astype(BF)

    each(4, rows_of, 4)


def trunk_attention(r, front):
    shift_rows = r.shifts[...].astype(F32)
    gain_rows = r.gains[...].astype(F32)

    def enter(index):
        rows = at(index * 128, 128)
        lead = r.leads[index].astype(F32) / 100.0
        r.resid[rows, :] = front[rows, :].astype(F32) + lead * shift_rows[2:3]

    each(2, enter)
    normalise(r, r.resid, r.rstd_one, r.unit_one, gain_rows[0:1], shift_rows[0:1], r.normed)

    def project(index):
        lanes = at(index * 256, 256)
        x = r.normed[...]
        r.q[:, lanes] = (nn(x, r.attn[0, :, lanes]) + r.vecs[0:1, lanes].astype(F32)).astype(BF)
        r.k[:, lanes] = nn(x, r.attn[1, :, lanes]).astype(BF)
        r.v[:, lanes] = (nn(x, r.attn[2, :, lanes]) + r.vecs[1:2, lanes].astype(F32)).astype(BF)

    each(4, project, 4)
    first = iota((128, LANES), 1) < HEAD

    def pair(index):
        sample, hp = index // 8, index % 8
        rows, lanes = at(sample * 128, 128), at(hp * LANES, LANES)
        q, k, v = r.q[rows, lanes], r.k[rows, lanes], r.v[rows, lanes]
        none = jnp.zeros_like(q)
        mixed = None
        for part in range(2):
            mine = first if part == 0 else jnp.logical_not(first)
            scores = nt(jnp.where(mine, q, none), k) * SCALE
            grown = jnp.exp(scores - jnp.max(scores, axis=1, keepdims=True))
            probs = grown / jnp.sum(grown, axis=1, keepdims=True)
            r.probs[index * 2 + part] = probs
            term = nn(probs.astype(BF), jnp.where(mine, v, none))
            mixed = term if mixed is None else mixed + term
        r.mixed[rows, lanes] = mixed.astype(BF)

    each(16, pair, 4)

    def leave(index):
        lanes = at(index * 256, 256)
        grown = nn(r.mixed[...], r.attn[3, :, lanes]) + r.vecs[2:3, lanes].astype(F32)
        r.resid[:, lanes] = r.resid[:, lanes] + grown

    each(4, leave, 4)
    normalise(r, r.resid, r.rstd_two, r.unit_two, gain_rows[1:2], shift_rows[1:2], r.x_own)


def bias_row(r, start, count):
    return r.bias_in[at(start, count)].astype(F32).reshape(1, count)


def curve(x):
    area = 0.5 + 0.5 * lax.erf(x * ROOT_HALF)
    return x * area, area + x * (ROOT_TAU * jnp.exp(-0.5 * x * x))


def trunk_hidden(r):
    def tile(index):
        n, k = index // 4, index % 4
        lanes = at(k * 256, 256)
        pre = nn(r.x_own[...], r.bufs[at(n * 1024, 1024), lanes]) + bias_row(r, index * 256, 256)
        value, slope = curve(pre)
        r.grads_flat[at(n * 512 + 256, 256), lanes] = value.astype(BF)
        r.grads_flat[at(n * 512, 256), lanes] = (r.grads_flat[at(n * 512, 256), lanes].astype(F32) * slope).astype(BF)

    each(16, tile, 4)

    def back(index):
        rows = at(index * 256, 256)
        total = None
        for n in range(4):
            term = nt(r.grads_flat[n * 512 : n * 512 + 256, :], r.bufs[at(n * 1024 + index * 256, 256), :])
            total = term if total is None else total + term
        r.d_mid[:, rows] = total

    each(4, back, 4)


def norm_back(grad, unit, rstd, gain):
    scaled = grad * gain
    along = row_mean(scaled * unit)
    return rstd * (scaled - row_mean(scaled) - unit * along)


def trunk_back(r):
    gain_rows = r.gains[...].astype(F32)
    r.small[2:3, :] = jnp.zeros((1, D), F32)
    r.small[4:9, :] = jnp.zeros((5, D), F32)

    def second(index):
        rows = at(index * 64, 64)
        grad, unit = r.d_mid[rows, :], r.unit_two[rows, :]
        mid = r.cot[rows, :].astype(F32) + norm_back(grad, unit, r.rstd_two[rows, 0:1], gain_rows[1:2])
        r.d_mid[rows, :] = mid
        r.d_low[rows, :] = mid.astype(BF)
        r.small[2:3, :] += col_sum(mid)
        r.small[5:6, :] += col_sum(grad * unit)
        r.small[7:8, :] += col_sum(grad)

    each(4, second, 4)


def trunk_mix(r):
    def mix(index):
        rows = at(index * 256, 256)
        r.second[:, rows] = nt(r.d_low[...], r.attn[3, rows, :]).astype(BF)

    each(4, mix, 4)
    r.small[0:2, :] = jnp.zeros((2, D), F32)


def trunk_back_heads(r, sample):
    first = iota((128, LANES), 1) < HEAD
    rows = slice(sample * 128, sample * 128 + 128)

    def pair(hp):
        index = sample * 8 + hp
        lanes = at(hp * LANES, LANES)
        q, k, v = r.q[rows, lanes], r.k[rows, lanes], r.v[rows, lanes]
        d_mixed = r.second[rows, lanes]
        none = jnp.zeros_like(q)
        d_q = d_k = d_v = None
        for part in range(2):
            mine = first if part == 0 else jnp.logical_not(first)
            own = jnp.where(mine, d_mixed, none)
            probs = r.probs[index * 2 + part]
            d_probs = nt(own, v)
            inner = jnp.sum(probs * d_probs, axis=1, keepdims=True)
            d_scores = (probs * (d_probs - inner)).astype(BF)
            terms = (
                nn(d_scores, jnp.where(mine, k, none)),
                tn(d_scores, jnp.where(mine, q, none)),
                tn(probs.astype(BF), own),
            )
            d_q = terms[0] if d_q is None else d_q + terms[0]
            d_k = terms[1] if d_k is None else d_k + terms[1]
            d_v = terms[2] if d_v is None else d_v + terms[2]
        d_q = d_q * SCALE
        r.q[rows, lanes] = d_q.astype(BF)
        r.k[rows, lanes] = (d_k * SCALE).astype(BF)
        r.v[rows, lanes] = d_v.astype(BF)
        r.small[0:1, lanes] += col_sum(d_q)
        r.small[1:2, lanes] += col_sum(d_v)

    each(8, pair, 4)


def trunk_back_in(r, d_in, sample):
    gain_rows = r.gains[...].astype(F32)
    cells = slice(sample * 128, sample * 128 + 128)

    def inward(index):
        rows = at(index * 256, 256)
        total = nt(r.q[cells, :], r.attn[0, rows, :]) + nt(r.k[cells, :], r.attn[1, rows, :])
        r.unit_two[cells, rows] = total + nt(r.v[cells, :], r.attn[2, rows, :])

    each(4, inward, 4)

    def start(index):
        rows = at(sample * 128 + index * 64, 64)
        grad, unit = r.unit_two[rows, :], r.unit_one[rows, :]
        whole = r.d_mid[rows, :] + norm_back(grad, unit, r.rstd_one[rows, 0:1], gain_rows[0:1])
        d_in[rows, :] = whole.astype(BF)
        lead = r.leads[sample].astype(F32) / 100.0
        r.small[4:5, :] += col_sum(grad * unit)
        r.small[6:7, :] += col_sum(grad)
        r.small[8:9, :] += lead * col_sum(whole)

    each(2, start, 2)


def trunk_out(r, out):
    def tile(index):
        lanes = at(index * 256, 256)
        total = r.resid[:, lanes] + r.vecs[3:4, lanes].astype(F32)
        for n in range(4):
            total = total + nn(r.grads_flat[n * 512 + 256 : n * 512 + 512, :], r.bufs[4096 + n * 1024 : 5120 + n * 1024, lanes])
        out[:, lanes] = total.astype(BF)

    each(4, tile, 4)


def trunk_weight_out(r):
    r.turn_b[...] = r.mixed[...].T

    def quarter(index):
        put_rows(r.sums[3], index, nn(r.turn_b[at(index * 256, 256), :], r.d_low[...]))

    each(4, quarter, 4)


def trunk_weights(r, which):
    right = (r.q, r.k, r.v)[which]

    def quarter(index):
        put_rows(r.sums[which], index, nn(r.turn_a[at(index * 256, 256), :], right[...]))

    each(4, quarter, 4)


def trunk_turn(r):
    r.turn_a[...] = r.normed[...].T


def hidden_loads(r, place, load):
    loads = []
    for part, owner in enumerate((place.me, place.me + 2 - 4 * place.y)):
        units = at((place.section * 16 + owner) * 128, 128)
        side = slice(part * 128, part * 128 + 128)
        loads.append(load(15 + part * 2, r.mlp_in.at[:, units], r.win.at[:, side]))
        loads.append(load(16 + part * 2, r.mlp_out.at[units, :], r.wout.at[side]))
    return loads


def hidden_tables(r, place):
    r.win_t[...] = r.win[...].T
    for part, owner in enumerate((place.me, place.me + 2 - 4 * place.y)):
        both = bias_row(r, (place.section * 16 + owner - place.c) * 128, 256)
        first = jnp.broadcast_to(place.c == 0, (1, 128))
        row = jnp.where(first, both[:, 0:128], both[:, 128:256])
        r.units[part * 128 : part * 128 + 128, :] = jnp.broadcast_to(row, (256, 128)).T
    r.unit_two[...] = jnp.zeros((256, D), F32)
    r.d_mid[...] = jnp.zeros((256, D), F32)
    r.bias_sum[...] = jnp.zeros((256, 256), F32)


def hidden_plane(r, plane):
    def tile(index):
        x, cot = r.gather[plane, at(index * 256, 256), :], r.gather[plane, at(512 + index * 256, 256), :]
        value, slope = curve(nt(r.win_t[...], x) + r.units[...])
        grad = nt(r.wout[...], cot) * slope
        r.bias_sum[...] += grad
        r.unit_two[...] += nn(grad.astype(BF), x)
        r.d_mid[...] += nn(value.astype(BF), cot)

    each(2, tile, 2)


def hidden_gifts(r, place):
    return [
        remote(r.gift, r.gift_in, r.gift_sent.at[0], r.gift_come.at[0], place.beside),
        remote(r.gift_bias, r.gift_bias_in, r.gift_sent.at[1], r.gift_come.at[1], place.beside),
    ]


def hidden_exchange(r, gifts):
    r.gift[0] = r.unit_two[128:256, :].astype(BF)
    r.gift[1] = r.d_mid[128:256, :].astype(BF)
    r.gift_bias[...] = jnp.broadcast_to(col_sum(r.bias_sum[...].T), (8, 256))
    for one in gifts:
        one.start()


def hidden_finish(r, gifts):
    for one in gifts:
        one.wait()
    r.win_out[...] = (r.unit_two[0:128, :] + r.gift_in[0].astype(F32)).T
    r.wout_out[...] = r.d_mid[0:128, :] + r.gift_in[1].astype(F32)
    r.bias_out[...] = r.gift_bias[0:1, 0:128] + r.gift_bias_in[0:1, 128:256]


def remote(source, target, sent, arrived, device):
    return pltpu.make_async_remote_copy(
        src_ref=source,
        dst_ref=target,
        send_sem=sent,
        recv_sem=arrived,
        device_id=device,
        device_id_type=MESH,
    )


class Place:
    def __init__(self):
        self.section = lax.axis_index("section")
        self.me = lax.axis_index("dp")
        self.c = self.me % 2
        self.y = (self.me // 2) % 2
        self.low = (self.me // 4) % 2
        self.high = self.me // 8
        self.across = {"section": 1 - self.section}
        self.core = {"dp": self.me + 1 - 2 * self.c}
        self.beside = {"dp": self.me + 2 - 4 * self.y}
        self.near = {"dp": self.me + 4 - 8 * self.low}
        self.far = {"dp": self.me + 8 - 16 * self.high}
        self.both = {"dp": self.me + 12 - 8 * self.low - 16 * self.high}

    def plane(self, step):
        low = (self.low + step % 2) % 2
        high = (self.high + step // 2) % 2
        return high * 2 + low

    def levels(self):
        return (self.core, self.beside, self.near, self.far)


class Share:
    def __init__(self, r, place, base, sent, arrived):
        self.place, self.base, self.sent, self.arrived = place, base, sent, arrived
        self.buf = r.gather
        self.mine = place.high * 2 + place.low

    def block(self, plane, c):
        return self.buf.at[plane, at(self.base + c * 256, 256)]

    def copy(self, plane, c, number, device):
        block = self.block(plane, c)
        return remote(block, block, self.sent.at[number], self.arrived.at[plane * 2 + c], device)

    def wait(self, plane, c):
        self.copy(plane, c, 0, self.place.core).wait_recv()

    def along(self, plane, number, to_upper):
        device = {"dp": self.place.me + (4 if to_upper else -4)}
        pl.when(self.mine < 3 if to_upper else self.mine > 0)(
            lambda: self.copy(plane, self.place.c, number, device).start()
        )

    def open(self):
        self.along(self.mine, 0, True)
        self.along(self.mine, 1, False)
        self.copy(self.mine, self.place.c, 2 + self.mine, self.place.core).start()

    def pass_on(self, distance):
        for below in (True, False):
            plane = self.mine - distance if below else self.mine + distance

            @pl.when(plane >= 0 if below else plane < 4)
            def _():
                self.wait(plane, self.place.c)
                self.along(plane, 6 + plane, below)
                self.copy(plane, self.place.c, 2 + plane, self.place.core).start()

    def settle(self, plane):
        self.wait(plane, 1 - self.place.c)

    def close(self):
        def done(number):
            self.copy(0, 0, number, self.place.core).wait_send()

        pl.when(self.mine < 3)(lambda: done(0))
        pl.when(self.mine > 0)(lambda: done(1))
        for number in range(2, 6):
            done(number)
        for plane in range(4):
            gone = ((plane < self.mine) & (self.mine < 3)) | ((plane > self.mine) & (self.mine > 0))
            pl.when(gone)(functools.partial(done, 6 + plane))


class Halving:
    def __init__(self, place, source, room, sizes, sent, arrived, done, target=None):
        self.place, self.source, self.room, self.sizes = place, source, room, sizes
        self.sent, self.arrived, self.done, self.target = sent, arrived, done, target
        self.bits = (place.c, place.y, place.low, place.high)

    def takes(self, level):
        if self.target is None or level < 2:
            return None
        on_low = self.place.low == self.target[0]
        return on_low if level == 2 else on_low & (self.place.high == self.target[1])

    def gives(self, level):
        if self.target is None or level < 2:
            return None
        on_low = self.place.low == self.target[0]
        return jnp.logical_not(on_low) if level == 2 else on_low & (self.place.high != self.target[1])

    def when(self, condition, action):
        if condition is None:
            action()
        else:
            pl.when(condition)(action)

    def part(self, j, level, side):
        rows = self.sizes[level]
        start = 0 if self.target is not None and level >= 2 else side * rows
        return self.source(j, start, rows) if level == 0 else self.room(j, level - 1, start, rows)

    def copy(self, j, level):
        give = self.part(j, level, 1 - self.bits[level])
        target = self.room(j, level, 0, self.sizes[level])
        device = self.place.levels()[level]
        return remote(give, target, self.sent.at[j, level], self.arrived.at[j, level], device)

    def begin(self, j, level):
        self.when(self.gives(level), lambda: self.copy(j, level).start())

    def finish(self, j, level):
        self.when(self.takes(level), lambda: self.take(j, level))
        if level < 3:
            self.begin(j, level + 1)

    def take(self, j, level):
        self.copy(j, level).wait_recv()
        mine = self.part(j, level, self.bits[level])
        room = self.room(j, level, 0, self.sizes[level])
        step = 64 if self.sizes[level] % 64 == 0 else 48

        def add(index):
            rows = at(index * step, step)
            total = mine[rows, :].astype(F32) + room[rows, :].astype(F32)
            if level == 3:
                self.done(j, index * step, total)
            else:
                room[rows, :] = total.astype(BF)

        each(self.sizes[level] // step, add)

    def close(self, j):
        for level in range(4):
            self.when(self.gives(level), lambda: self.copy(j, level).wait_send())


class Doubling:
    def __init__(self, place, rows, own, come, sent, arrived):
        self.place, self.rows, self.own, self.come = place, rows, own, come
        self.sent, self.arrived = sent, arrived

    def before(self, level):
        return self.own.at[0 : self.rows] if level == 0 else self.come.at[level - 1, 0 : self.rows]

    def copy(self, level):
        target = self.come.at[level, 0 : self.rows]
        device = self.place.levels()[level]
        return remote(self.before(level), target, self.sent.at[level], self.arrived.at[level], device)

    def begin(self):
        self.copy(0).start()

    def finish(self, level):
        self.copy(level).wait_recv()
        room = self.come.at[level, 0 : self.rows]
        total = self.before(level)[...].astype(F32) + room[...].astype(F32)
        room[...] = total.astype(room.dtype)
        if level < 3:
            self.copy(level + 1).start()

    def close(self):
        for level in range(4):
            self.copy(level).wait_send()


def matrix_sums(r, place, which):
    sums, rooms = r.sums[which], r.matrix_rooms[which]
    starts = (0, 256, 384)

    def room(j, level, start, rows):
        if level == 3:
            return r.last_room.at[at(j * 128 + start, rows)]
        return rooms.at[at(j * 512 + starts[level] + start, rows)]

    def done(j, start, value):
        r.attn_out[at(j * 128 + start, 64), :] = value

    return Halving(
        place,
        lambda j, start, rows: sums.at[at(j * 512 + start, rows)],
        room,
        (256, 128, 128, 128),
        r.sum_sent.at[:, at(which * 4, 4)],
        r.sum_come.at[:, at(which * 4, 4)],
        done,
        (which % 2, which // 2),
    )


def greet(place):
    barrier = pltpu.get_barrier_semaphore()
    devices = (place.across, place.core, place.beside, place.near, place.far, place.both)
    for device in devices:
        pl.semaphore_signal(barrier, inc=1, device_id=device, device_id_type=MESH)
    return lambda: pl.semaphore_wait(barrier, len(devices))


def across(r, place, number, source, target):
    return remote(source, target, r.over_sent.at[number], r.over_come.at[number], place.across)


def front_tail(r, place):
    own = at((place.y * 2 + place.c) * 256, 256)
    high, low = halves(r.small_in[3, 0:16])
    r.fold_sum[0:16, :] = high
    r.fold_sum[16:32, :] = low
    both = nn(r.fold_sum[...], r.attn[1])
    mine = iota((HEADS, D), 1) >> 6 == iota((HEADS, D), 0)
    query = col_sum(jnp.where(mine, both[0:HEADS] + both[HEADS : 2 * HEADS], 0.0))
    r.query_row[0:1, :] = query
    high, low = halves(query)
    row = iota((16, D), 0)
    pair = jnp.where(row == 0, high.astype(F32), jnp.where(row == 1, low.astype(F32), 0.0))
    r.query_pair[...] = pair.astype(BF)

    @pl.when(place.high + place.low == 0)
    def _():
        first = jnp.broadcast_to(r.vecs[0:1, own].astype(F32), (16, 256))
        first = jnp.where(iota((16, 256), 0) < 2, first, 0.0).astype(BF)
        r.attn_out[...] = tn(first, r.query_pair[...])
        r.vec_out[...] = col_sum(nt(r.query_pair[...], r.attn[0, own, :]))

    @pl.when((place.high == 0) & (place.low == 1))
    def _():
        left = jnp.concatenate([r.fold_sum[0:16, own], r.fold_sum[16:32, own], r.fold_sum[0:16, own]], axis=0)
        right = jnp.concatenate([r.qhead[0:16, :], r.qhead[0:16, :], r.qhead[16:32, :]], axis=0)
        r.attn_out[...] = tn(left, right)
        r.vec_out[...] = r.query_row[0:1, own]

    @pl.when(place.high == 1)
    def _():
        r.vec_out[...] = r.small_in[3, pl.ds(16 + place.low, 1), own]


def front_section(r, place):
    def load(number, source, target):
        return pltpu.make_async_copy(source, target, r.loads.at[number])

    cots = Share(r, place, 512, r.cot_sent, r.cot_come)
    hiddens = Share(r, place, 0, r.x_sent, r.x_come)
    mine = hiddens.mine
    loads = [
        load(0, r.patches_in.at[0], r.pix.at[0:128]),
        load(1, r.patches_in.at[1], r.pix.at[128:256]),
        load(2, r.weight_in, r.raw),
        load(7, r.cot_in.at[0], cots.block(mine, place.c).at[0:128]),
        load(8, r.cot_in.at[1], cots.block(mine, place.c).at[128:256]),
        load(3, r.attn_in.at[0, 0], r.attn.at[0]),
        load(4, r.attn_in.at[0, 1], r.attn.at[1]),
        load(5, r.attn_in.at[0, 2], r.attn.at[2]),
        load(6, r.attn_in.at[0, 3], r.attn.at[3]),
    ]
    units = hidden_loads(r, place, load)
    met = greet(place)
    for one in loads + units:
        one.start()
    r.small[16:24, :] = jnp.zeros((8, D), F32)
    for one in loads[0:3]:
        one.wait()
    front_tables(r)
    loads[3].wait()
    loads[4].wait()
    met()
    cots.open()
    loads[5].wait()
    loads[6].wait()
    front_query(r)
    loads[7].wait()
    front_values(r)
    loads[8].wait()
    send_front = []
    for sample in range(2):
        front_forward(r, r.act_out, sample)
        rows = slice(sample * 128, sample * 128 + 128)
        send_front.append(across(r, place, (0, 3)[sample], r.act_out.at[rows], r.arrive.at[rows]))
        send_front[sample].start()
    for one in units:
        one.wait()
    hidden_tables(r, place)
    for distance in range(1, 4):
        cots.pass_on(distance)
    for plane in range(4):
        cots.settle(plane)
    near = mine + 1 - 2 * place.low
    far = mine + 2 - 4 * place.high
    both = 3 - mine

    def patch_done(j, start, value):
        r.patch_out[...] = value[0:24]
        r.gift_patch[...] = value[24:48]

    values, outs = matrix_sums(r, place, 2), matrix_sums(r, place, 3)
    patch_starts = (0, 384, 576, 672)
    pixels = Halving(
        place,
        lambda j, start, rows: r.patch_sum.at[at(start, rows)],
        lambda j, level, start, rows: r.patch_rooms.at[at(patch_starts[level] + start, rows)],
        (384, 192, 96, 48),
        r.patch_sent,
        r.patch_come,
        patch_done,
    )
    smalls = Doubling(place, 24, r.small, r.small_in, r.small_sent, r.small_come)
    embeds = Doubling(place, 48, r.var_sum, r.var_in, r.var_sent, r.var_come)
    gifts = hidden_gifts(r, place)
    give_half = across(r, place, 2, r.gift_half, r.gift_half)
    give_patch = across(r, place, 6, r.gift_patch, r.gift_patch)
    give_var = across(r, place, 5, r.var_in.at[3], r.gift_var)

    def cells():
        hiddens.wait(mine, place.c)
        hiddens.open()

    def plane(which):
        hiddens.settle(which)
        hidden_plane(r, which)

    def come(sample):
        rows = slice(sample * 128, sample * 128 + 128)
        across(r, place, (1, 4)[sample], r.leave.at[rows], r.arrive.at[rows]).wait_recv()

    def back_out():
        front_back_out(r, r.arrive)
        outs.begin(0, 0)
        outs.begin(1, 0)

    def projection():
        front_back_projection(r)
        values.begin(0, 0)
        values.begin(1, 0)

    def table():
        front_back_table(r)
        smalls.begin()

    def pixel_rows():
        front_back_pixels(r)
        embeds.begin()

    def order():
        front_back_order(r)
        pixels.begin(0, 0)

    def inputs():
        front_back_inputs(r, r.input_out, r.gift_half)
        give_half.start()

    def patch_last():
        pixels.finish(0, 3)
        give_patch.start()

    def var_last():
        embeds.finish(3)
        give_var.start()

    t = types.SimpleNamespace(
        cells=cells,
        own=lambda: plane(mine),
        pass1=lambda: hiddens.pass_on(1),
        near=lambda: plane(near),
        come0=lambda: come(0),
        come1=lambda: come(1),
        back_out=back_out,
        back_values0=lambda: front_back_values(r, r.arrive, 0),
        back_values1=lambda: front_back_values(r, r.arrive, 1),
        pass2=lambda: hiddens.pass_on(2),
        heads0=lambda: front_back_heads(r, 0),
        heads1=lambda: front_back_heads(r, 1),
        table=table,
        projection=projection,
        pass3=lambda: hiddens.pass_on(3),
        pixel_rows=pixel_rows,
        order=order,
        inputs=inputs,
        far=lambda: plane(far),
        both=lambda: plane(both),
        exchange=lambda: hidden_exchange(r, gifts),
        small0=lambda: smalls.finish(0),
        small1=lambda: smalls.finish(1),
        small2=lambda: smalls.finish(2),
        small3=lambda: smalls.finish(3),
        tail=lambda: front_tail(r, place),
        embed0=lambda: embeds.finish(0),
        embed1=lambda: embeds.finish(1),
        embed2=lambda: embeds.finish(2),
        embed3=var_last,
        patch0=lambda: pixels.finish(0, 0),
        patch1=lambda: pixels.finish(0, 1),
        patch2=lambda: pixels.finish(0, 2),
        patch3=patch_last,
        a00=lambda: outs.finish(0, 0),
        a01=lambda: outs.finish(0, 1),
        a02=lambda: outs.finish(0, 2),
        a03=lambda: outs.finish(0, 3),
        a10=lambda: outs.finish(1, 0),
        a11=lambda: outs.finish(1, 1),
        a12=lambda: outs.finish(1, 2),
        a13=lambda: outs.finish(1, 3),
        v00=lambda: values.finish(0, 0),
        v01=lambda: values.finish(0, 1),
        v02=lambda: values.finish(0, 2),
        v03=lambda: values.finish(0, 3),
        v10=lambda: values.finish(1, 0),
        v11=lambda: values.finish(1, 1),
        v12=lambda: values.finish(1, 2),
        v13=lambda: values.finish(1, 3),
    )
    t.cells()
    t.come0()
    t.back_values0()
    t.pass1()
    t.heads0()
    t.come1()
    t.back_out()
    t.back_values1()
    t.a10()
    t.a00()
    t.pass2()
    t.heads1()
    t.table()
    t.projection()
    t.a01()
    t.small0()
    t.pixel_rows()
    t.pass3()
    t.v00()
    t.small1()
    t.a02()
    t.order()
    t.embed0()
    t.inputs()
    t.patch0()
    t.a11()
    t.small2()
    t.embed1()
    t.near()
    t.a12()
    t.v01()
    t.small3()
    t.own()
    t.far()
    t.v10()
    t.patch1()
    t.both()
    t.v02()
    t.exchange()
    t.v11()
    t.patch2()
    t.a03()
    t.embed2()
    t.tail()
    t.patch3()
    t.v03()
    t.v12()
    t.embed3()
    t.v13()
    t.a13()
    give_attn = load(13, r.attn_out, r.attn_final)
    give_attn.start()
    r.var_out[...] = r.var_in[3].astype(F32)
    hidden_finish(r, gifts)
    across(r, place, 7, r.small_in.at[3, 0:16], r.gift_small).wait_recv()
    r.gain_out[...] = r.gift_small[4:6, :]
    r.shift_out[...] = r.gift_small[6:9, :]
    cots.close()
    hiddens.close()
    for j in range(2):
        values.close(j)
        outs.close(j)
    pixels.close(0)
    smalls.close()
    embeds.close()
    for one in (*send_front, give_half, give_var, give_patch):
        one.wait_send()
    give_attn.wait()


def trunk_section(r, place):
    def load(number, source, target):
        return pltpu.make_async_copy(source, target, r.loads.at[number])

    cots = Share(r, place, 512, r.cot_sent, r.cot_come)
    hiddens = Share(r, place, 0, r.x_sent, r.x_come)
    mine = hiddens.mine
    r.cot = cots.block(mine, place.c)
    r.x_own = hiddens.block(mine, place.c)
    given = [load(4 + n, r.cot_in.at[n], r.cot.at[n * 128 : (n + 1) * 128]) for n in range(2)]
    outs = [load(n, r.mlp_out.at[n * 1024 : (n + 1) * 1024], r.bufs.at[4096 + n * 1024 : 5120 + n * 1024]) for n in range(4)]
    attns = [load(6 + n, r.attn_in.at[0, n], r.attn.at[n]) for n in range(4)]
    ins = [load(10 + n, r.mlp_in.at[:, n * 1024 : (n + 1) * 1024], r.bufs.at[n * 1024 : (n + 1) * 1024]) for n in range(4)]
    met = greet(place)
    for one in (*given, *outs, *attns, *ins):
        one.start()
    met()
    r.small[...] = jnp.zeros((24, D), F32)
    for one in given:
        one.wait()
    cots.open()
    for one in outs:
        one.wait()
    trunk_ahead(r)
    for one in (*attns, *ins):
        one.wait()
    cots.pass_on(1)
    for sample in range(2):
        rows = slice(sample * 128, sample * 128 + 128)
        across(r, place, (0, 3)[sample], r.act_out.at[rows], r.arrive.at[rows]).wait_recv()
    send_x = remote(r.x_own, r.x_own, r.over_sent.at[0], r.x_come.at[mine * 2 + place.c], place.across)
    halves_of = [slice(sample * 128, sample * 128 + 128) for sample in range(2)]
    send_in = [
        across(r, place, number, r.leave.at[rows], r.arrive.at[rows]) for number, rows in zip((1, 4), halves_of)
    ]
    send_small = across(r, place, 7, r.small_in.at[3, 0:16], r.gift_small)
    near = mine + 1 - 2 * place.low
    far = mine + 2 - 4 * place.high
    both = 3 - mine
    sums = [matrix_sums(r, place, which) for which in range(4)]
    queries, keys, values, outs_sum = sums
    smalls = Doubling(place, 24, r.small, r.small_in, r.small_sent, r.small_come)
    gifts = hidden_gifts(r, place)
    units = hidden_loads(r, place, load)

    def tell(ready):
        for level, device in enumerate(place.levels()):
            pl.semaphore_signal(ready.at[level], inc=1, device_id=device, device_id_type=MESH)

    def heed(ready):
        for level in range(4):
            pl.semaphore_wait(ready.at[level], 1)

    def attention():
        trunk_attention(r, r.arrive)
        send_x.start()
        hiddens.open()

    def hidden():
        trunk_hidden(r)
        tell(r.ready)

    def weight_out():
        trunk_weight_out(r)
        heed(r.ready)
        outs_sum.begin(0, 0)
        outs_sum.begin(1, 0)

    def back_in(sample):
        trunk_back_in(r, r.leave, sample)
        send_in[sample].start()
        if sample == 1:
            smalls.begin()

    def out():
        trunk_out(r, r.act_out)
        tell(r.ready_two)

    def weights(which):
        trunk_weights(r, which)
        if which == 2:
            heed(r.ready_two)
        sums[which].begin(0, 0)
        sums[which].begin(1, 0)

    def tables():
        for one in units:
            one.start()
        for one in units:
            one.wait()
        hidden_tables(r, place)

    def plane(which):
        cots.settle(which)
        hiddens.settle(which)
        hidden_plane(r, which)

    def small_last():
        smalls.finish(3)
        send_small.start()

    t = types.SimpleNamespace(
        attention=attention,
        cot2=lambda: cots.pass_on(2),
        hidden=hidden,
        cot3=lambda: cots.pass_on(3),
        back=lambda: trunk_back(r),
        weight_out=weight_out,
        pass1=lambda: hiddens.pass_on(1),
        mix=lambda: trunk_mix(r),
        back_heads0=lambda: trunk_back_heads(r, 0),
        back_heads1=lambda: trunk_back_heads(r, 1),
        back_in0=lambda: back_in(0),
        back_in1=lambda: back_in(1),
        pass2=lambda: hiddens.pass_on(2),
        out=out,
        turn=lambda: trunk_turn(r),
        weight_v=lambda: weights(2),
        weight_k=lambda: weights(1),
        weight_q=lambda: weights(0),
        tables=tables,
        own=lambda: plane(mine),
        near=lambda: plane(near),
        pass3=lambda: hiddens.pass_on(3),
        far=lambda: plane(far),
        both=lambda: plane(both),
        exchange=lambda: hidden_exchange(r, gifts),
        small0=lambda: smalls.finish(0),
        small1=lambda: smalls.finish(1),
        small2=lambda: smalls.finish(2),
        small3=small_last,
        a00=lambda: outs_sum.finish(0, 0),
        a01=lambda: outs_sum.finish(0, 1),
        a02=lambda: outs_sum.finish(0, 2),
        a03=lambda: outs_sum.finish(0, 3),
        a10=lambda: outs_sum.finish(1, 0),
        a11=lambda: outs_sum.finish(1, 1),
        a12=lambda: outs_sum.finish(1, 2),
        a13=lambda: outs_sum.finish(1, 3),
        v00=lambda: values.finish(0, 0),
        v01=lambda: values.finish(0, 1),
        v02=lambda: values.finish(0, 2),
        v03=lambda: values.finish(0, 3),
        v10=lambda: values.finish(1, 0),
        v11=lambda: values.finish(1, 1),
        v12=lambda: values.finish(1, 2),
        v13=lambda: values.finish(1, 3),
        k00=lambda: keys.finish(0, 0),
        k01=lambda: keys.finish(0, 1),
        k02=lambda: keys.finish(0, 2),
        k03=lambda: keys.finish(0, 3),
        k10=lambda: keys.finish(1, 0),
        k11=lambda: keys.finish(1, 1),
        k12=lambda: keys.finish(1, 2),
        k13=lambda: keys.finish(1, 3),
        q00=lambda: queries.finish(0, 0),
        q01=lambda: queries.finish(0, 1),
        q02=lambda: queries.finish(0, 2),
        q03=lambda: queries.finish(0, 3),
        q10=lambda: queries.finish(1, 0),
        q11=lambda: queries.finish(1, 1),
        q12=lambda: queries.finish(1, 2),
        q13=lambda: queries.finish(1, 3),
    )
    t.attention()
    t.turn()
    t.cot2()
    t.hidden()
    t.back()
    t.mix()
    t.back_heads0()
    t.back_in0()
    t.weight_out()
    t.back_heads1()
    t.pass1()
    t.back_in1()
    t.a00()
    t.out()
    t.a10()
    t.a01()
    t.weight_v()
    t.cot3()
    t.weight_q()
    t.q00()
    t.pass2()
    t.v10()
    t.weight_k()
    t.tables()
    t.a11()
    t.far()
    t.pass3()
    t.q01()
    t.k10()
    t.small0()
    t.v00()
    t.k00()
    t.both()
    t.a02()
    t.k11()
    t.v11()
    t.own()
    t.small1()
    t.q02()
    t.near()
    t.q10()
    t.v01()
    t.a03()
    t.small2()
    t.k01()
    t.q11()
    t.a12()
    t.exchange()
    t.small3()
    t.k02()
    t.v12()
    t.v02()
    t.a13()
    t.q12()
    t.k12()
    t.v13()
    t.k03()
    t.v03()
    t.k13()
    t.q03()
    t.q13()
    own = at((place.y * 2 + place.c) * 256, 256)
    r.vec_out[...] = r.small_in[3, pl.ds(mine, 1), own]
    r.gain_out[...] = r.small_in[3, 4:6]
    r.shift_out[...] = r.small_in[3, 6:9]
    give_attn = load(14, r.attn_out, r.attn_final)
    give_attn.start()
    hidden_finish(r, gifts)
    across(r, place, 2, r.gift_half, r.gift_half).wait_recv()
    r.input_out[...] = r.gift_half[...].astype(F32)
    across(r, place, 5, r.var_in.at[3], r.gift_var).wait_recv()
    r.var_out[...] = r.gift_var[...].astype(F32)
    across(r, place, 6, r.gift_patch, r.gift_patch).wait_recv()
    r.patch_out[...] = r.gift_patch[...]
    cots.close()
    hiddens.close()
    for one in sums:
        for j in range(2):
            one.close(j)
    smalls.close()
    for one in (send_x, *send_in, send_small):
        one.wait_send()
    give_attn.wait()


CELL_ROWS = (CELLS, D)
SCRATCH = dict(
    attn=((4, D, D), BF),
    bufs=((8 * D, D), BF),
    gather=((4, D, D), BF),
    last_room=((256, D), BF),
    grads_flat=((2 * D, D), BF),
    turned=((D, WIDE), BF),
    pat=((CELLS, WIDE), BF),
    qhead=((32, D), BF),
    fold=((16, D), BF),
    fold_sum=((32, D), BF),
    query_pair=((16, D), BF),
    query_row=((8, D), F32),
    score=((16, WIDE), F32),
    uses=((16, 1, WIDE), F32),
    probs=((32, 128, 128), F32),
    resid=(CELL_ROWS, F32),
    unit_one=(CELL_ROWS, F32),
    unit_two=(CELL_ROWS, F32),
    d_mid=(CELL_ROWS, F32),
    rstd_one=((CELLS, LANES), F32),
    rstd_two=((CELLS, LANES), F32),
    normed=(CELL_ROWS, BF),
    k=(CELL_ROWS, BF),
    v=(CELL_ROWS, BF),
    mixed=(CELL_ROWS, BF),
    d_low=(CELL_ROWS, BF),
    arrive=(CELL_ROWS, BF),
    turn_a=((D, CELLS), BF),
    turn_b=((D, CELLS), BF),
    small=((24, D), F32),
    small_in=((4, 24, D), F32),
    var_sum=((48, D), BF),
    var_in=((4, 48, D), BF),
    gift=((2, 128, D), BF),
    gift_in=((2, 128, D), BF),
    gift_bias=((8, 256), F32),
    gift_bias_in=((8, 256), F32),
    gift_var=((48, D), BF),
    gift_small=((16, D), F32),
    gift_patch=((24, D), F32),
    gift_half=((CELLS, 384), BF),
)
SEMAPHORES = dict(
    loads=(19,),
    over_sent=(8,),
    over_come=(8,),
    cot_sent=(10,),
    cot_come=(8,),
    x_sent=(10,),
    x_come=(8,),
    var_sent=(4,),
    var_come=(4,),
    gift_sent=(2,),
    gift_come=(2,),
    sum_sent=(2, 16),
    sum_come=(2, 16),
    patch_sent=(1, 4),
    patch_come=(1, 4),
    small_sent=(4,),
    small_come=(4,),
)
INPUTS = dict(
    patches_in=pl.ANY,
    masks=pltpu.VMEM,
    leads=pltpu.SMEM,
    cot_in=pl.ANY,
    weight_in=pl.ANY,
    embed=pltpu.VMEM,
    attn_in=pl.ANY,
    vecs=pltpu.VMEM,
    gains=pltpu.VMEM,
    shifts=pltpu.VMEM,
    mlp_in=pl.ANY,
    bias_in=pltpu.VMEM,
    mlp_out=pl.ANY,
)
OUTPUTS = dict(
    act_out=(CELL_ROWS, BF),
    input_out=((CELLS, 384), F32),
    patch_out=((24, D), F32),
    var_out=((48, D), F32),
    attn_final=(CELL_ROWS, F32),
    vec_out=((1, 256), F32),
    gain_out=((2, D), F32),
    shift_out=((3, D), F32),
    win_out=((D, 128), F32),
    bias_out=((1, 128), F32),
    wout_out=((128, D), F32),
)


class Refs:
    pass


def fused_kernel(*refs):
    r = Refs()
    names = list(INPUTS) + list(OUTPUTS) + list(SCRATCH) + list(SEMAPHORES) + ["ready", "ready_two"]
    for name, ref in zip(names, refs, strict=True):
        setattr(r, name, ref)
    r.table = r.bufs.at[0:WIDE]
    r.mid = r.bufs.at[WIDE : 2 * WIDE]
    r.patch_rooms = r.bufs.at[4352:5072]
    r.patch_sum = r.table.at[0:768]
    r.raw = r.turned.at[0:768, 0:D]
    for number, name in enumerate(("q", "second", "leave")):
        setattr(r, name, r.turned.at[number * 256 : number * 256 + 256, 0:D])
    r.pix = r.normed.at[:, 0 : V * PIX]
    r.input_sum = r.resid
    r.attn_out = r.resid
    r.agg = r.mixed
    r.dlow = r.d_low
    r.wout = r.k
    r.win_t = r.v
    r.win = r.turn_a
    r.keep = r.rstd_one
    r.units = r.unit_one.at[:, 0:256]
    r.bias_sum = r.unit_one.at[:, 256:512]
    place = Place()

    @pl.when(place.section == 0)
    def _():
        r.sums = (None, None, r.grads_flat.at[0:D], r.grads_flat.at[D : 2 * D])
        r.matrix_rooms = (None, None, r.bufs.at[2304:3328], r.bufs.at[3328:4352])
        front_section(r, place)

    @pl.when(place.section == 1)
    def _():
        r.sums = tuple(r.bufs.at[at(start, D)] for start in (2 * D, 3 * D, 4 * D, 0))
        r.matrix_rooms = tuple(r.bufs.at[at(start, D)] for start in (5 * D, 6 * D, 7 * D, D))
        trunk_section(r, place)


def hand_on(*refs):
    count = len(OUTPUTS)
    given, taken, rooms = (refs[count * part : count * (part + 1)] for part in range(3))
    sems = refs[3 * count]
    ins = [pltpu.make_async_copy(given[n], rooms[n], sems.at[0, n]) for n in range(count)]
    outs = [pltpu.make_async_copy(rooms[n], taken[n], sems.at[1, n]) for n in range(count)]
    for one in ins:
        one.start()
    for first, then in zip(ins, outs):
        first.wait()
        then.start()
    for one in outs:
        one.wait()


def fused_shards(
    patches,
    masks,
    lead_times,
    cotangent,
    patch_weight,
    var_embed,
    attention,
    attn_vectors,
    norm_gains,
    trunk_shifts,
    mlp_in,
    mlp_in_bias,
    mlp_out,
):
    outs = pl.pallas_call(
        fused_kernel,
        in_specs=[pl.BlockSpec(memory_space=space) for space in INPUTS.values()],
        out_specs=[
            pl.BlockSpec(memory_space=pl.ANY if one == (CELL_ROWS, F32) else pltpu.VMEM)
            for one in OUTPUTS.values()
        ],
        out_shape=[jax.ShapeDtypeStruct(*one) for one in OUTPUTS.values()],
        scratch_shapes=[pltpu.VMEM(*one) for one in SCRATCH.values()]
        + [pltpu.SemaphoreType.DMA(one) for one in SEMAPHORES.values()]
        + [pltpu.SemaphoreType.REGULAR((4,))] * 2,
        compiler_params=pltpu.CompilerParams(
            collective_id=0, has_side_effects=True, vmem_limit_bytes=60 * 2**20
        ),
    )(
        patches,
        masks,
        lead_times,
        cotangent,
        patch_weight,
        var_embed,
        attention,
        attn_vectors[0],
        norm_gains,
        trunk_shifts,
        mlp_in,
        mlp_in_bias,
        mlp_out,
    )
    outs = pl.pallas_call(
        hand_on,
        in_specs=[pl.BlockSpec(memory_space=pl.ANY)] * len(outs),
        out_specs=[pl.BlockSpec(memory_space=pl.ANY)] * len(outs),
        out_shape=[jax.ShapeDtypeStruct(*one) for one in OUTPUTS.values()],
        scratch_shapes=[pltpu.VMEM(*one) for one in OUTPUTS.values()]
        + [pltpu.SemaphoreType.DMA((2, len(outs)))],
    )(*outs)
    act, inputs, patch, var, attn, vec, gain, shift, win, bias, wout = outs
    return (
        act.reshape(1, 2, 128, D),
        inputs.reshape(2, 128, 384),
        patch,
        var,
        attn[None],
        vec,
        gain,
        shift,
        win,
        bias.reshape(128),
        wout,
    )


def solution(mesh):
    in_specs = (
        P("dp", None, None),
        P("dp", None, None),
        P("dp"),
        P("dp", None, None),
        P(),
        P(),
        P("section", None, None, None),
        P("section", None, None),
        P(),
        P(),
        P(),
        P(),
        P(),
    )
    out_specs = (
        P("section", "dp", None, None),
        P("dp", None, "section"),
        P(("section", "dp"), None),
        P(),
        P("section", "dp", None),
        P("section", "dp"),
        P(),
        P(),
        P(None, ("section", "dp")),
        P(("section", "dp")),
        P(("section", "dp"), None),
    )
    small = mesh.shape["section"] == 2 and mesh.shape["dp"] == 16
    body = fused_shards if small else shards
    return jax.shard_map(body, mesh=mesh, in_specs=in_specs, out_specs=out_specs, check_vma=False)
```

```python
import functools
import types

import jax
import jax.numpy as jnp
from jax import lax
from jax.experimental import pallas as pl
from jax.experimental.pallas import tpu as pltpu
from jax.sharding import PartitionSpec as P

D = 1024
HEADS = 16
HEAD = 64
FF = 4096
V = 48
PIX = 16


EPSILON = 1e-05
MASKED = -1e30
HIGHEST = lax.Precision.HIGHEST


def shortened(array):
    return jax.tree.map(lambda a: a.astype(jnp.bfloat16) if a.dtype == jnp.float32 else a, array)


def from_behind(value, axis, steps):
    count = lax.axis_size(axis)
    leading, last = (max(0, -steps), min(count, count - steps))
    return lax.ppermute(value, axis, [(source, source + steps) for source in range(leading, last)])


def layer_norm(features, gain_row, shift_row):
    row_mean = jnp.mean(features, axis=-1, keepdims=True)
    centred = features - row_mean
    spread = jnp.mean(centred * centred, axis=-1, keepdims=True)
    return centred * lax.rsqrt(spread + EPSILON) * gain_row + shift_row


def exact_gelu(inputs):
    return jax.nn.gelu(inputs, approximate=False)


def matmul(left_side, right_side):
    return jnp.dot(left_side, right_side, preferred_element_type=jnp.float32)


def matmul_tn(left_side, right_side):
    return lax.dot_general(
        left_side, right_side, (((0,), (0,)), ((), ())), preferred_element_type=jnp.float32
    )


def matmul_nt(left_side, right_side):
    return lax.dot_general(
        left_side, right_side, (((1,), (1,)), ((), ())), preferred_element_type=jnp.float32
    )


def updated(carried, changes):
    merged = dict(carried)
    merged.update(changes)
    return merged


def query_terms(layer_weights, layer_vectors):
    query_vec = matmul(layer_vectors[0][None, :], layer_weights[0])[0] + layer_vectors[1].astype(
        jnp.float32
    )
    key_wide = layer_weights[1].astype(jnp.float32).reshape(D, HEADS, HEAD)
    folded = jnp.einsum("dhk,hk->dh", key_wide, query_vec.reshape(HEADS, HEAD), precision=HIGHEST)
    return (query_vec, key_wide, folded)


def embed_block(pixel_rows, valid_cells, patch_weight, var_embed, folded_low, score_scale):
    cell_count = pixel_rows.shape[0]
    shaped = pixel_rows.reshape(cell_count, V, PIX)
    pieces = jnp.einsum(
        "tvp,vpd->tvd", shaped, patch_weight.reshape(V, PIX, D), preferred_element_type=jnp.float32
    )
    embedded = (pieces + var_embed.astype(jnp.float32)[None]).astype(jnp.bfloat16)
    scores = (
        jnp.einsum("tvd,dh->tvh", embedded, folded_low, preferred_element_type=jnp.float32)
        * score_scale
    )
    scores = jnp.where(valid_cells[:, :, None] > 0, scores, MASKED)
    weights = jax.nn.softmax(scores, axis=1)
    weights_low = weights.astype(jnp.bfloat16)
    pooled = jnp.einsum(
        "tvh,tvd->thd", weights_low, embedded, preferred_element_type=jnp.float32
    ).astype(jnp.bfloat16)
    return (shaped, embedded, weights, weights_low, pooled)


def pool_values(pooled, layer_weights, layer_vectors):
    cell_count = pooled.shape[0]
    projected = jnp.einsum(
        "thd,dhk->thk",
        pooled,
        layer_weights[2].reshape(D, HEADS, HEAD),
        preferred_element_type=jnp.float32,
    )
    return (projected.reshape(cell_count, D) + layer_vectors[2].astype(jnp.float32)).astype(
        jnp.bfloat16
    )


def front_block_back(
    pixel_rows,
    valid_cells,
    d_out,
    patch_weight,
    var_embed,
    layer_weights,
    layer_vectors,
    folded_low,
    score_scale,
):
    shaped, embedded, weights, weights_low, pooled = embed_block(
        pixel_rows, valid_cells, patch_weight, var_embed, folded_low, score_scale
    )
    values_low = pool_values(pooled, layer_weights, layer_vectors)
    cell_count = pixel_rows.shape[0]
    g_bo = jnp.sum(d_out.astype(jnp.float32), axis=0)
    g_wo = matmul_tn(values_low, d_out)
    d_values = matmul_nt(d_out, layer_weights[3])
    g_bv = jnp.sum(d_values, axis=0)
    d_values_low = d_values.astype(jnp.bfloat16).reshape(cell_count, HEADS, HEAD)
    g_wv = jnp.einsum(
        "thd,thk->dhk", pooled, d_values_low, preferred_element_type=jnp.float32
    ).reshape(D, D)
    d_pooled = jnp.einsum(
        "thk,dhk->thd",
        d_values_low,
        layer_weights[2].reshape(D, HEADS, HEAD),
        preferred_element_type=jnp.float32,
    ).astype(jnp.bfloat16)
    d_weights = jnp.einsum("thd,tvd->tvh", d_pooled, embedded, preferred_element_type=jnp.float32)
    d_embedded = jnp.einsum(
        "tvh,thd->tvd", weights_low, d_pooled, preferred_element_type=jnp.float32
    )
    d_scores = (weights * (d_weights - jnp.sum(weights * d_weights, axis=1, keepdims=True))).astype(
        jnp.bfloat16
    )
    g_folded = (
        jnp.einsum("tvd,tvh->dh", embedded, d_scores, preferred_element_type=jnp.float32)
        * score_scale
    )
    d_embedded = (
        d_embedded
        + jnp.einsum("tvh,dh->tvd", d_scores, folded_low, preferred_element_type=jnp.float32)
        * score_scale
    )
    g_var = jnp.sum(d_embedded, axis=0)
    d_embedded_low = d_embedded.astype(jnp.bfloat16)
    g_patch = jnp.einsum(
        "tvp,tvd->vpd", shaped, d_embedded_low, preferred_element_type=jnp.float32
    ).reshape(V * PIX, D)
    d_pixels = jnp.einsum(
        "tvd,vpd->tvp",
        d_embedded_low,
        patch_weight.reshape(V, PIX, D),
        preferred_element_type=jnp.float32,
    ).reshape(cell_count, V * PIX)
    return (g_wv, g_wo, g_bv, g_bo, g_folded, g_var, g_patch, d_pixels)


def layer_two(
    x_in,
    lead_hours,
    d_out,
    layer_weights,
    layer_vectors,
    norm_gains,
    trunk_shifts,
    mlp_in,
    mlp_in_bias,
    mlp_out,
):
    seq_len = x_in.shape[0]
    score_scale = HEAD ** (-0.5)
    gain_rows = norm_gains.astype(jnp.float32)
    shift_rows = trunk_shifts.astype(jnp.float32)
    vec_rows = layer_vectors.astype(jnp.float32)
    lead_scale = lead_hours.astype(jnp.float32) / 100.0
    resid_in = x_in.astype(jnp.float32) + lead_scale * shift_rows[2]
    normed, first_back = jax.vjp(layer_norm, resid_in, gain_rows[0], shift_rows[0])
    normed_low = normed.astype(jnp.bfloat16)
    queries = (
        (matmul(normed_low, layer_weights[0]) + vec_rows[0])
        .astype(jnp.bfloat16)
        .reshape(seq_len, HEADS, HEAD)
    )
    key_rows = (
        matmul(normed_low, layer_weights[1]).astype(jnp.bfloat16).reshape(seq_len, HEADS, HEAD)
    )
    value_rows = (
        (matmul(normed_low, layer_weights[2]) + vec_rows[1])
        .astype(jnp.bfloat16)
        .reshape(seq_len, HEADS, HEAD)
    )
    scores = (
        jnp.einsum("qhd,khd->hqk", queries, key_rows, preferred_element_type=jnp.float32)
        * score_scale
    )
    attn_probs = jax.nn.softmax(scores, axis=-1)
    probs_low = attn_probs.astype(jnp.bfloat16)
    mixed_heads = (
        jnp.einsum("hqk,khd->qhd", probs_low, value_rows, preferred_element_type=jnp.float32)
        .reshape(seq_len, D)
        .astype(jnp.bfloat16)
    )
    resid_mid = resid_in + matmul(mixed_heads, layer_weights[3]) + vec_rows[2]
    normed_two, second_back = jax.vjp(layer_norm, resid_mid, gain_rows[1], shift_rows[1])
    normed_two_low = normed_two.astype(jnp.bfloat16)
    hidden_pre = matmul(normed_two_low, mlp_in) + mlp_in_bias.astype(jnp.float32)
    hidden, gelu_back = jax.vjp(exact_gelu, hidden_pre)
    hidden_low = hidden.astype(jnp.bfloat16)
    produced = (resid_mid + matmul(hidden_low, mlp_out) + vec_rows[3]).astype(jnp.bfloat16)
    d_final = d_out.astype(jnp.float32)
    g_b2 = jnp.sum(d_final, axis=0)
    g_wout = matmul_tn(hidden_low, d_out)
    d_hidden = matmul_nt(d_out, mlp_out)
    d_pre = gelu_back(d_hidden)[0]
    g_bin = jnp.sum(d_pre, axis=0)
    d_pre_low = d_pre.astype(jnp.bfloat16)
    g_win = matmul_tn(normed_two_low, d_pre_low)
    d_mid_norm, g_gain_two, g_shift_two = second_back(matmul_nt(d_pre_low, mlp_in))
    d_mid = d_final + d_mid_norm
    g_bo = jnp.sum(d_mid, axis=0)
    d_mid_low = d_mid.astype(jnp.bfloat16)
    g_wo = matmul_tn(mixed_heads, d_mid_low)
    d_mixed = (
        matmul_nt(d_mid_low, layer_weights[3]).astype(jnp.bfloat16).reshape(seq_len, HEADS, HEAD)
    )
    d_probs = jnp.einsum("qhd,khd->hqk", d_mixed, value_rows, preferred_element_type=jnp.float32)
    d_values = jnp.einsum(
        "hqk,qhd->khd", probs_low, d_mixed, preferred_element_type=jnp.float32
    ).reshape(seq_len, D)
    d_scores = (
        attn_probs * (d_probs - jnp.sum(attn_probs * d_probs, axis=-1, keepdims=True))
    ).astype(jnp.bfloat16)
    d_queries = (
        jnp.einsum("hqk,khd->qhd", d_scores, key_rows, preferred_element_type=jnp.float32).reshape(
            seq_len, D
        )
        * score_scale
    )
    d_keys = (
        jnp.einsum("hqk,qhd->khd", d_scores, queries, preferred_element_type=jnp.float32).reshape(
            seq_len, D
        )
        * score_scale
    )
    g_bq = jnp.sum(d_queries, axis=0)
    g_bv = jnp.sum(d_values, axis=0)
    d_queries_low = d_queries.astype(jnp.bfloat16)
    d_keys_low = d_keys.astype(jnp.bfloat16)
    d_values_low = d_values.astype(jnp.bfloat16)
    g_wq = matmul_tn(normed_low, d_queries_low)
    g_wk = matmul_tn(normed_low, d_keys_low)
    g_wv = matmul_tn(normed_low, d_values_low)
    d_normed = (
        matmul_nt(d_queries_low, layer_weights[0])
        + matmul_nt(d_keys_low, layer_weights[1])
        + matmul_nt(d_values_low, layer_weights[2])
    )
    d_in_norm, g_gain_one, g_shift_one = first_back(d_normed)
    d_in = d_mid + d_in_norm
    g_lead = lead_scale * jnp.sum(d_in, axis=0)
    return (
        produced,
        d_in.astype(jnp.bfloat16),
        jnp.stack([g_wq, g_wk, g_wv, g_wo]),
        jnp.stack([g_bq, g_bv, g_bo, g_b2]),
        jnp.stack([g_gain_one, g_gain_two]),
        jnp.stack([g_shift_one, g_shift_two, g_lead]),
        g_win,
        g_bin,
        g_wout,
    )


def send_forward(sent_rows):
    return from_behind(shortened(sent_rows), "section", 1).astype(sent_rows.dtype)


def shards(
    patches,
    masks,
    lead_times,
    cotangent,
    patch_weight,
    var_embed,
    attention,
    attn_vectors,
    norm_gains,
    trunk_shifts,
    mlp_in,
    mlp_in_bias,
    mlp_out,
):
    micro_count, seq_len, pixel_width = patches.shape
    block_rows = min(128, seq_len)
    score_scale = HEAD ** (-0.5)
    layer_weights = attention[0]
    layer_vectors = attn_vectors[0]
    on_front = lax.axis_index("section") == 0
    empty_rows = jnp.zeros((seq_len, D), jnp.bfloat16)
    carried = {
        "attn": jnp.zeros((4, D, D), jnp.float32),
        "vec": jnp.zeros((4, D), jnp.float32),
        "u_sum": jnp.zeros((D, HEADS), jnp.float32),
        "patch": jnp.zeros((V * PIX, D), jnp.float32),
        "var": jnp.zeros((V, D), jnp.float32),
        "gains": jnp.zeros((2, D), jnp.float32),
        "shifts": jnp.zeros((3, D), jnp.float32),
        "w_in": jnp.zeros((D, FF), jnp.float32),
        "b_in": jnp.zeros((FF,), jnp.float32),
        "w_out": jnp.zeros((FF, D), jnp.float32),
        "outputs": jnp.zeros((micro_count, seq_len, D), jnp.bfloat16),
        "pixels": jnp.zeros((micro_count, seq_len, pixel_width), jnp.float32),
        "returned": jnp.zeros((micro_count, seq_len, D), jnp.bfloat16),
    }

    def front_forward(carried, mb_index):
        query_vec, key_wide, folded = query_terms(layer_weights, layer_vectors)
        folded_low = folded.astype(jnp.bfloat16)
        valid_cells = masks[mb_index, :, 0:block_rows].T
        block_parts = embed_block(
            patches[mb_index, 0:block_rows],
            valid_cells,
            patch_weight,
            var_embed,
            folded_low,
            score_scale,
        )
        values_low = pool_values(block_parts[4], layer_weights, layer_vectors)
        pieces = [
            (matmul(values_low, layer_weights[3]) + layer_vectors[3].astype(jnp.float32)).astype(
                jnp.bfloat16
            )
        ]
        produced = jnp.concatenate(pieces, axis=0)
        return (
            updated(carried, {"outputs": carried["outputs"].at[mb_index].set(produced)}),
            produced,
        )

    def front_backward(carried, mb_index, d_front):
        query_vec, key_wide, folded = query_terms(layer_weights, layer_vectors)
        folded_low = folded.astype(jnp.bfloat16)
        attn_sum = carried["attn"]
        vec_sum = carried["vec"]
        u_total = carried["u_sum"]
        var_total = carried["var"]
        patch_total = carried["patch"]
        valid_cells = masks[mb_index, :, 0:block_rows].T
        block_grads = front_block_back(
            patches[mb_index, 0:block_rows],
            valid_cells,
            d_front[0:block_rows],
            patch_weight,
            var_embed,
            layer_weights,
            layer_vectors,
            folded_low,
            score_scale,
        )
        attn_sum = attn_sum.at[2].add(block_grads[0]).at[3].add(block_grads[1])
        vec_sum = vec_sum.at[2].add(block_grads[2]).at[3].add(block_grads[3])
        u_total = u_total + block_grads[4]
        var_total = var_total + block_grads[5]
        patch_total = patch_total + block_grads[6]
        pixel_pieces = [block_grads[7]]
        pixel_grads = carried["pixels"].at[mb_index].set(jnp.concatenate(pixel_pieces, axis=0))
        return updated(
            carried,
            {
                "attn": attn_sum,
                "vec": vec_sum,
                "u_sum": u_total,
                "var": var_total,
                "patch": patch_total,
                "pixels": pixel_grads,
            },
        )

    def back_step(carried, mb_index, arriving):
        produced, d_front, attn_part, vec_part, gain_part, shift_part, g_win, g_bin, g_wout = (
            layer_two(
                arriving,
                lead_times[mb_index],
                cotangent[mb_index],
                layer_weights,
                layer_vectors,
                norm_gains,
                trunk_shifts,
                mlp_in,
                mlp_in_bias,
                mlp_out,
            )
        )
        changes = {
            "attn": carried["attn"] + attn_part,
            "vec": carried["vec"] + vec_part,
            "gains": carried["gains"] + gain_part,
            "shifts": carried["shifts"] + shift_part,
            "w_in": carried["w_in"] + g_win,
            "b_in": carried["b_in"] + g_bin,
            "w_out": carried["w_out"] + g_wout,
            "outputs": carried["outputs"].at[mb_index].set(produced),
            "returned": carried["returned"].at[mb_index].set(d_front),
        }
        return (updated(carried, changes), d_front)

    def finish_front(carried):
        query_vec, key_wide, folded = query_terms(layer_weights, layer_vectors)
        u_total = carried["u_sum"]
        d_key = (u_total[:, :, None] * query_vec.reshape(HEADS, HEAD)[None]).reshape(D, D)
        d_query_vec = jnp.einsum("dh,dhk->hk", u_total, key_wide, precision=HIGHEST).reshape(D)
        d_query_weight = layer_vectors[0].astype(jnp.float32)[:, None] * d_query_vec[None, :]
        d_query = jnp.dot(layer_weights[0].astype(jnp.float32), d_query_vec, precision=HIGHEST)
        attn_sum = carried["attn"].at[0].set(d_query_weight).at[1].set(d_key)
        vec_sum = carried["vec"].at[0].set(d_query).at[1].set(d_query_vec)
        return updated(carried, {"attn": attn_sum, "vec": vec_sum})

    arriving_act = empty_rows
    for step_number in range(micro_count + 1):

        def front_turn(inputs, step_number=step_number):
            carried, act_in = inputs
            sent_rows = empty_rows
            if step_number < micro_count:
                carried, sent_rows = front_forward(carried, step_number)
            return (carried, sent_rows)

        def back_turn(inputs, step_number=step_number):
            carried, act_in = inputs
            if step_number >= 1:
                carried, returned_rows = back_step(carried, step_number - 1, act_in)
            return (carried, empty_rows)

        carried, sent_act = lax.cond(on_front, front_turn, back_turn, (carried, arriving_act))
        if step_number < micro_count:
            arriving_act = send_forward(sent_act)
    gradients_back = from_behind(shortened(carried["returned"]), "section", -1)

    def front_all(kept_state):
        for mb_index in range(micro_count):
            kept_state = front_backward(kept_state, mb_index, gradients_back[mb_index])
        return kept_state

    carried = lax.cond(on_front, front_all, lambda kept_state: kept_state, carried)
    carried = lax.cond(on_front, finish_front, lambda kept_state: kept_state, carried)
    attn_grads, vec_grads = (
        lax.psum_scatter(
            carried["attn"].reshape(1, 4 * D, D), "dp", scatter_dimension=1, tiled=True
        ),
        lax.psum_scatter(carried["vec"].reshape(1, 4 * D), "dp", scatter_dimension=1, tiled=True),
    )
    win_grads, bin_grads, wout_grads, patch_grads = (
        lax.psum_scatter(carried["w_in"], ("section", "dp"), scatter_dimension=1, tiled=True),
        lax.psum_scatter(carried["b_in"], ("section", "dp"), scatter_dimension=0, tiled=True),
        lax.psum_scatter(carried["w_out"], ("section", "dp"), scatter_dimension=0, tiled=True),
        lax.psum_scatter(carried["patch"], ("section", "dp"), scatter_dimension=0, tiled=True),
    )
    var_grads, gain_grads, shift_grads = lax.psum(
        (carried["var"], carried["gains"], carried["shifts"]), ("section", "dp")
    )
    pixel_half = pixel_width // 2
    moved = from_behind(shortened(carried["pixels"][:, :, pixel_half:]), "section", 1)
    input_grads = jnp.where(on_front, carried["pixels"][:, :, :pixel_half], moved)
    activations = carried["outputs"][None]
    return (
        activations,
        input_grads,
        patch_grads,
        var_grads,
        attn_grads,
        vec_grads,
        gain_grads,
        shift_grads,
        win_grads,
        bin_grads,
        wout_grads,
    )


F32 = jnp.float32
BF = jnp.bfloat16
I32 = jnp.int32
MESH = pl.DeviceIdType.MESH
CELLS = 256
SLOT = 64
WIDE = 1152
LANES = 128
SCALE = 0.125
ROOT_HALF = 0.7071067811865476
ROOT_TAU = 0.3989422804014327


def nn(a, b):
    return jnp.dot(a, b, preferred_element_type=F32)


def nt(a, b):
    return lax.dot_general(a, b, (((1,), (1,)), ((), ())), preferred_element_type=F32)


def tn(a, b):
    return lax.dot_general(a, b, (((0,), (0,)), ((), ())), preferred_element_type=F32)


def at(start, size):
    if isinstance(start, int):
        return pl.ds(start, size)
    return pl.ds(pl.multiple_of(start, size), size)


def each(count, body, unroll=1):
    def step(index, carry):
        body(index)
        return carry

    lax.fori_loop(0, count, step, 0, unroll=unroll)


def iota(shape, dim):
    return lax.broadcasted_iota(I32, shape, dim)


def halves(value):
    high = value.astype(BF)
    return high, (value - high.astype(F32)).astype(BF)


def pixel_column(slot):
    return ((slot & (SLOT - 1)) << 4) + (slot >> 6)


def slot_tile(index, rows, columns):
    match = pixel_column(iota((rows, 1), 0) + index * rows)
    return jnp.where(iota((rows, columns), 1) == match, 1.0, 0.0).astype(BF)


def spread(tile):
    return jnp.concatenate([tile] * (WIDE // LANES), axis=1)


def front_tables(r):
    def place(index):
        tile = slot_tile(index, 256, V * PIX)
        r.table[at(index * 256, 256), :] = nn(tile, r.raw[...]).astype(BF)
        r.pat[:, at(index * 256, 256)] = nt(r.pix[...], tile).astype(BF)

    each(4, place, 4)
    r.table[1024:1072, :] = r.embed[...]
    r.table[1072:WIDE, :] = jnp.zeros((WIDE - 1072, D), BF)
    lane = iota((CELLS, LANES), 1)
    r.pat[:, 1024:WIDE] = jnp.where(lane < V, 1.0, 0.0).astype(BF)
    twice = jnp.where(iota((V, LANES), 1) & (SLOT - 1) == iota((V, LANES), 0), 1.0, 0.0).astype(BF)
    for sample in range(2):
        present = tn(r.masks[sample].astype(F32).astype(BF), twice)
        r.keep[sample * 128 : sample * 128 + 128, :] = present


def front_query(r):
    first = jnp.broadcast_to(r.vecs[0:1, :], (16, D))
    query = nn(first, r.attn[0])[0:1, :] + r.vecs[1:2, :].astype(F32)
    own = iota((HEADS, D), 1) >> 6 == iota((HEADS, D), 0)
    high, low = halves(jnp.where(own, jnp.broadcast_to(query, (HEADS, D)), 0.0))
    r.qhead[0:HEADS, :] = high
    r.qhead[HEADS : 2 * HEADS, :] = low
    both = nt(r.qhead[...], r.attn[1])
    folded = (both[0:HEADS] + both[HEADS : 2 * HEADS]).astype(BF)
    r.fold[...] = folded
    r.score[...] = nt(folded, r.table[...]) * SCALE


def front_values(r):
    def tile(index):
        lanes = at(index * 256, 256)
        r.mid[:, lanes] = nn(r.table[...], r.attn[2, :, lanes]).astype(BF)

    each(4, tile, 4)


def front_scores(r, head, rows):
    row = r.score[pl.ds(head, 1), :]
    total = None
    for k in range(WIDE // LANES):
        cols = slice(k * LANES, (k + 1) * LANES)
        part = r.pat[rows, cols].astype(F32) * row[:, cols]
        total = part if total is None else total + part
    total = total + pltpu.roll(total, SLOT, 1)
    total = jnp.where(r.keep[rows, :] > 0.5, total, MASKED)
    top = jnp.max(total, axis=1, keepdims=True)
    grown = jnp.exp(total - top)
    return grown / (0.5 * jnp.sum(grown, axis=1, keepdims=True))


def front_forward(r, out, sample):
    rows = slice(sample * 128, sample * 128 + 128)
    first_half = iota((128, LANES), 1) < HEAD

    def pair(index):
        lanes = at(index * LANES, LANES)
        pooled = []
        for part in range(2):
            head = index * 2 + part
            weights = front_scores(r, head, rows)
            r.probs[head * 2 + sample] = weights
            pooled.append(r.pat[rows, :] * spread(weights.astype(BF)))
        found = nn(jnp.concatenate(pooled, axis=0), r.mid[:, lanes])
        values = jnp.where(first_half, found[0:128], found[128:256]) + r.vecs[2:3, lanes].astype(F32)
        r.agg[rows, lanes] = values.astype(BF)

    each(HEADS // 2, pair, 2)

    def tile(index):
        lanes = at(index * 256, 256)
        found = nn(r.agg[rows, :], r.attn[3, :, lanes]) + r.vecs[3:4, lanes].astype(F32)
        out[rows, lanes] = found.astype(BF)

    each(4, tile, 4)


def front_back_values(r, d_out, sample):
    cells = slice(sample * 128, sample * 128 + 128)

    def tile(index):
        rows = at(index * 256, 256)
        grad = nt(d_out[cells, :], r.attn[3, rows, :])
        sums = (jnp.sum(grad, axis=0, keepdims=True), jnp.sum(d_out[cells, rows].astype(F32), axis=0, keepdims=True))
        for row, value in zip((16, 17), sums):
            r.small[row : row + 1, rows] = value if sample == 0 else r.small[row : row + 1, rows] + value
        r.dlow[cells, rows] = grad.astype(BF)

    each(4, tile, 4)
    r.turn_a[:, cells] = r.dlow[cells, :].T


def front_back_heads(r, sample):
    rows = slice(sample * 128, sample * 128 + 128)
    first_half = iota((128, LANES), 1) < HEAD
    r.input_sum[rows, :] = jnp.zeros((128, D), F32)

    def pair(index):
        lanes = at(index * LANES, LANES)
        grads = r.dlow[rows, lanes]
        none = jnp.zeros_like(grads)
        own = jnp.concatenate([jnp.where(first_half, grads, none), jnp.where(first_half, none, grads)], axis=0)
        mid = r.mid[:, lanes]
        weights = [r.probs[(index * 2 + part) * 2 + sample] for part in range(2)]
        lows = [weight.astype(BF) for weight in weights]
        totals = [None, None]
        for k in range(WIDE // 384):
            wide = nt(own, mid[k * 384 : (k + 1) * 384, :])
            for j in range(3):
                n = k * 3 + j
                cols = slice(n * LANES, (n + 1) * LANES)
                pixels = r.pat[rows, cols].astype(F32)
                pieces = [wide[part * 128 : part * 128 + 128, j * LANES : (j + 1) * LANES] for part in range(2)]
                for part in range(2):
                    term = pieces[part] * pixels
                    totals[part] = term if totals[part] is None else totals[part] + term
                if n < 8:
                    sums = lows[0].astype(F32) * pieces[0] + lows[1].astype(F32) * pieces[1]
                    r.input_sum[rows, cols] = r.input_sum[rows, cols] + sums
        scores = []
        for part in range(2):
            total = totals[part] + pltpu.roll(totals[part], SLOT, 1)
            inner = 0.5 * jnp.sum(weights[part] * total, axis=1, keepdims=True)
            scores.append((weights[part] * (total - inner)).astype(BF).astype(F32))
        along = [r.score[pl.ds(index * 2 + part, 1), :] for part in range(2)]
        for n in range(9):
            cols = slice(n * LANES, (n + 1) * LANES)
            if n < 8:
                sums = scores[0] * along[0][:, cols] + scores[1] * along[1][:, cols]
                r.input_sum[rows, cols] = r.input_sum[rows, cols] + sums
            pixels = r.pat[rows, cols].astype(F32)
            for part in range(2):
                head = index * 2 + part
                use = SCALE * jnp.sum(scores[part] * pixels, axis=0, keepdims=True)
                r.uses[head, :, cols] = use if sample == 0 else r.uses[head, :, cols] + use
        for part in range(2):
            spot = at((index * 2 + part) * HEAD, HEAD)
            pooled = r.pat[rows, :] * spread(lows[part])
            found = nn(r.turn_a[spot, rows], pooled)
            if sample == 1:
                found = found + r.turned[spot, :].astype(F32)
            r.turned[spot, :] = found.astype(BF)

    each(HEADS // 2, pair, 2)


def put_rows(sums, quarter, value):
    y, c = quarter // 2, quarter % 2
    for j in range(2):
        sums[at(j * 512 + (c * 2 + y) * 128, 128), :] = value[j * 128 : (j + 1) * 128].astype(BF)


def front_back_out(r, d_out):
    r.turn_b[...] = r.agg[...].T

    def tile(index):
        put_rows(r.sums[3], index, nn(r.turn_b[at(index * 256, 256), :], d_out[...]))

    each(4, tile, 4)


def front_back_table(r):
    uses = jnp.concatenate([r.uses[h] for h in range(HEADS)], axis=0).astype(BF)
    r.small[0:16, :] = nn(uses, r.table[...])
    r.mid[...] = r.turned[...].T


def front_back_projection(r):
    def values(index):
        rows = at(index * 256, 256)
        put_rows(r.sums[2], index, tn(r.table[:, rows], r.mid[...]))

    each(4, values, 4)


def front_back_pixels(r):
    uses = jnp.concatenate([r.uses[h] for h in range(HEADS)], axis=0).astype(BF)

    def pixels(index):
        lanes = at(index * 256, 256)
        full = nt(r.mid[...], r.attn[2, lanes, :]) + tn(uses, r.fold[:, lanes])
        r.turned[:, lanes] = full[0:1024].astype(BF)
        r.var_sum[:, lanes] = full[1024:1072].astype(BF)

    each(4, pixels, 4)


def front_back_order(r):
    def order(index):
        row = iota((256, 1), 0) + index * 256
        piece, k = row // 48, row % 48
        owner = ((piece & 1) * 2 + ((piece >> 1) & 1)) * 4 + ((piece >> 2) & 1) * 2 + (piece >> 3)
        natural = owner * 24 + jnp.where(k < 24, k, k + 360)
        slot = (natural & (PIX - 1)) * SLOT + (natural >> 4)
        pick = jnp.where(iota((256, D), 1) == slot, 1.0, 0.0).astype(BF)
        r.patch_sum[at(index * 256, 256), :] = nn(pick, r.turned[:, 0:1024]).astype(BF)

    each(3, order, 3)


def front_back_inputs(r, own_half, other_half):
    low = r.input_sum[...].astype(BF)
    r.dlow[...] = low
    for half, out in ((0, own_half), (1, other_half)):
        column = pixel_column(iota((D, 1), 0)) - half * 384
        pick = jnp.where(iota((D, 384), 1) == column, 1.0, 0.0).astype(BF)
        out[...] = nn(r.dlow[...], pick).astype(out.dtype)


def row_mean(x):
    return jnp.mean(x, axis=1, keepdims=True)


def col_sum(x):
    return jnp.sum(x, axis=0, keepdims=True)


def trunk_ahead(r):
    def tile(index):
        n, k = index // 4, index % 4
        found = nt(r.cot[...], r.bufs[at(4096 + index * 256, 256), :])
        r.grads_flat[at(n * 512, 256), at(k * 256, 256)] = found.astype(BF)

    each(16, tile, 4)
    r.small[3:4, :] = col_sum(r.cot[...].astype(F32))


def normalise(r, source, spread_rows, unit, gain, shift, out):
    def rows_of(index):
        rows = at(index * 64, 64)
        x = source[rows, :]
        centred = x - row_mean(x)
        rstd = lax.rsqrt(row_mean(centred * centred) + EPSILON)
        scaled = centred * rstd
        unit[rows, :] = scaled
        spread_rows[rows, :] = jnp.broadcast_to(rstd, (64, LANES))
        out[rows, :] = (scaled * gain + shift).astype(BF)

    each(4, rows_of, 4)


def trunk_attention(r, front):
    shift_rows = r.shifts[...].astype(F32)
    gain_rows = r.gains[...].astype(F32)

    def enter(index):
        rows = at(index * 128, 128)
        lead = r.leads[index].astype(F32) / 100.0
        r.resid[rows, :] = front[rows, :].astype(F32) + lead * shift_rows[2:3]

    each(2, enter)
    normalise(r, r.resid, r.rstd_one, r.unit_one, gain_rows[0:1], shift_rows[0:1], r.normed)

    def project(index):
        lanes = at(index * 256, 256)
        x = r.normed[...]
        r.q[:, lanes] = (nn(x, r.attn[0, :, lanes]) + r.vecs[0:1, lanes].astype(F32)).astype(BF)
        r.k[:, lanes] = nn(x, r.attn[1, :, lanes]).astype(BF)
        r.v[:, lanes] = (nn(x, r.attn[2, :, lanes]) + r.vecs[1:2, lanes].astype(F32)).astype(BF)

    each(4, project, 4)
    first = iota((128, LANES), 1) < HEAD

    def pair(index):
        sample, hp = index // 8, index % 8
        rows, lanes = at(sample * 128, 128), at(hp * LANES, LANES)
        q, k, v = r.q[rows, lanes], r.k[rows, lanes], r.v[rows, lanes]
        none = jnp.zeros_like(q)
        mixed = None
        for part in range(2):
            mine = first if part == 0 else jnp.logical_not(first)
            scores = nt(jnp.where(mine, q, none), k) * SCALE
            grown = jnp.exp(scores - jnp.max(scores, axis=1, keepdims=True))
            probs = grown / jnp.sum(grown, axis=1, keepdims=True)
            r.probs[index * 2 + part] = probs
            term = nn(probs.astype(BF), jnp.where(mine, v, none))
            mixed = term if mixed is None else mixed + term
        r.mixed[rows, lanes] = mixed.astype(BF)

    each(16, pair, 4)

    def leave(index):
        lanes = at(index * 256, 256)
        grown = nn(r.mixed[...], r.attn[3, :, lanes]) + r.vecs[2:3, lanes].astype(F32)
        r.resid[:, lanes] = r.resid[:, lanes] + grown

    each(4, leave, 4)
    normalise(r, r.resid, r.rstd_two, r.unit_two, gain_rows[1:2], shift_rows[1:2], r.x_own)


def bias_row(r, start, count):
    return r.bias_in[at(start, count)].astype(F32).reshape(1, count)


def curve(x):
    area = 0.5 + 0.5 * lax.erf(x * ROOT_HALF)
    return x * area, area + x * (ROOT_TAU * jnp.exp(-0.5 * x * x))


def trunk_hidden(r):
    def tile(index):
        n, k = index // 4, index % 4
        lanes = at(k * 256, 256)
        pre = nn(r.x_own[...], r.bufs[at(n * 1024, 1024), lanes]) + bias_row(r, index * 256, 256)
        value, slope = curve(pre)
        r.grads_flat[at(n * 512 + 256, 256), lanes] = value.astype(BF)
        r.grads_flat[at(n * 512, 256), lanes] = (r.grads_flat[at(n * 512, 256), lanes].astype(F32) * slope).astype(BF)

    each(16, tile, 4)

    def back(index):
        rows = at(index * 256, 256)
        total = None
        for n in range(4):
            term = nt(r.grads_flat[n * 512 : n * 512 + 256, :], r.bufs[at(n * 1024 + index * 256, 256), :])
            total = term if total is None else total + term
        r.d_mid[:, rows] = total

    each(4, back, 4)


def norm_back(grad, unit, rstd, gain):
    scaled = grad * gain
    along = row_mean(scaled * unit)
    return rstd * (scaled - row_mean(scaled) - unit * along)


def trunk_back(r):
    gain_rows = r.gains[...].astype(F32)
    r.small[2:3, :] = jnp.zeros((1, D), F32)
    r.small[4:9, :] = jnp.zeros((5, D), F32)

    def second(index):
        rows = at(index * 64, 64)
        grad, unit = r.d_mid[rows, :], r.unit_two[rows, :]
        mid = r.cot[rows, :].astype(F32) + norm_back(grad, unit, r.rstd_two[rows, 0:1], gain_rows[1:2])
        r.d_mid[rows, :] = mid
        r.d_low[rows, :] = mid.astype(BF)
        r.small[2:3, :] += col_sum(mid)
        r.small[5:6, :] += col_sum(grad * unit)
        r.small[7:8, :] += col_sum(grad)

    each(4, second, 4)


def trunk_mix(r):
    def mix(index):
        rows = at(index * 256, 256)
        r.second[:, rows] = nt(r.d_low[...], r.attn[3, rows, :]).astype(BF)

    each(4, mix, 4)
    r.small[0:2, :] = jnp.zeros((2, D), F32)


def trunk_back_heads(r, sample):
    first = iota((128, LANES), 1) < HEAD
    rows = slice(sample * 128, sample * 128 + 128)

    def pair(hp):
        index = sample * 8 + hp
        lanes = at(hp * LANES, LANES)
        q, k, v = r.q[rows, lanes], r.k[rows, lanes], r.v[rows, lanes]
        d_mixed = r.second[rows, lanes]
        none = jnp.zeros_like(q)
        d_q = d_k = d_v = None
        for part in range(2):
            mine = first if part == 0 else jnp.logical_not(first)
            own = jnp.where(mine, d_mixed, none)
            probs = r.probs[index * 2 + part]
            d_probs = nt(own, v)
            inner = jnp.sum(probs * d_probs, axis=1, keepdims=True)
            d_scores = (probs * (d_probs - inner)).astype(BF)
            terms = (
                nn(d_scores, jnp.where(mine, k, none)),
                tn(d_scores, jnp.where(mine, q, none)),
                tn(probs.astype(BF), own),
            )
            d_q = terms[0] if d_q is None else d_q + terms[0]
            d_k = terms[1] if d_k is None else d_k + terms[1]
            d_v = terms[2] if d_v is None else d_v + terms[2]
        d_q = d_q * SCALE
        r.q[rows, lanes] = d_q.astype(BF)
        r.k[rows, lanes] = (d_k * SCALE).astype(BF)
        r.v[rows, lanes] = d_v.astype(BF)
        r.small[0:1, lanes] += col_sum(d_q)
        r.small[1:2, lanes] += col_sum(d_v)

    each(8, pair, 4)


def trunk_back_in(r, d_in, sample):
    gain_rows = r.gains[...].astype(F32)
    cells = slice(sample * 128, sample * 128 + 128)

    def inward(index):
        rows = at(index * 256, 256)
        total = nt(r.q[cells, :], r.attn[0, rows, :]) + nt(r.k[cells, :], r.attn[1, rows, :])
        r.unit_two[cells, rows] = total + nt(r.v[cells, :], r.attn[2, rows, :])

    each(4, inward, 4)

    def start(index):
        rows = at(sample * 128 + index * 64, 64)
        grad, unit = r.unit_two[rows, :], r.unit_one[rows, :]
        whole = r.d_mid[rows, :] + norm_back(grad, unit, r.rstd_one[rows, 0:1], gain_rows[0:1])
        d_in[rows, :] = whole.astype(BF)
        lead = r.leads[sample].astype(F32) / 100.0
        r.small[4:5, :] += col_sum(grad * unit)
        r.small[6:7, :] += col_sum(grad)
        r.small[8:9, :] += lead * col_sum(whole)

    each(2, start, 2)


def trunk_out(r, out):
    def tile(index):
        lanes = at(index * 256, 256)
        total = r.resid[:, lanes] + r.vecs[3:4, lanes].astype(F32)
        for n in range(4):
            total = total + nn(r.grads_flat[n * 512 + 256 : n * 512 + 512, :], r.bufs[4096 + n * 1024 : 5120 + n * 1024, lanes])
        out[:, lanes] = total.astype(BF)

    each(4, tile, 4)


def trunk_weight_out(r):
    r.turn_b[...] = r.mixed[...].T

    def quarter(index):
        put_rows(r.sums[3], index, nn(r.turn_b[at(index * 256, 256), :], r.d_low[...]))

    each(4, quarter, 4)


def trunk_weights(r, which):
    right = (r.q, r.k, r.v)[which]

    def quarter(index):
        put_rows(r.sums[which], index, nn(r.turn_a[at(index * 256, 256), :], right[...]))

    each(4, quarter, 4)


def trunk_turn(r):
    r.turn_a[...] = r.normed[...].T


def hidden_loads(r, place, load):
    loads = []
    for part, owner in enumerate((place.me, place.me + 2 - 4 * place.y)):
        units = at((place.section * 16 + owner) * 128, 128)
        side = slice(part * 128, part * 128 + 128)
        loads.append(load(15 + part * 2, r.mlp_in.at[:, units], r.win.at[:, side]))
        loads.append(load(16 + part * 2, r.mlp_out.at[units, :], r.wout.at[side]))
    return loads


def hidden_tables(r, place):
    r.win_t[...] = r.win[...].T
    for part, owner in enumerate((place.me, place.me + 2 - 4 * place.y)):
        both = bias_row(r, (place.section * 16 + owner - place.c) * 128, 256)
        first = jnp.broadcast_to(place.c == 0, (1, 128))
        row = jnp.where(first, both[:, 0:128], both[:, 128:256])
        r.units[part * 128 : part * 128 + 128, :] = jnp.broadcast_to(row, (256, 128)).T
    r.unit_two[...] = jnp.zeros((256, D), F32)
    r.d_mid[...] = jnp.zeros((256, D), F32)
    r.bias_sum[...] = jnp.zeros((256, 256), F32)


def hidden_plane(r, plane):
    def tile(index):
        x, cot = r.gather[plane, at(index * 256, 256), :], r.gather[plane, at(512 + index * 256, 256), :]
        value, slope = curve(nt(r.win_t[...], x) + r.units[...])
        grad = nt(r.wout[...], cot) * slope
        r.bias_sum[...] += grad
        r.unit_two[...] += nn(grad.astype(BF), x)
        r.d_mid[...] += nn(value.astype(BF), cot)

    each(2, tile, 2)


def hidden_gifts(r, place):
    return [
        remote(r.gift, r.gift_in, r.gift_sent.at[0], r.gift_come.at[0], place.beside),
        remote(r.gift_bias, r.gift_bias_in, r.gift_sent.at[1], r.gift_come.at[1], place.beside),
    ]


def hidden_exchange(r, gifts):
    r.gift[0] = r.unit_two[128:256, :].astype(BF)
    r.gift[1] = r.d_mid[128:256, :].astype(BF)
    r.gift_bias[...] = jnp.broadcast_to(col_sum(r.bias_sum[...].T), (8, 256))
    for one in gifts:
        one.start()


def hidden_finish(r, gifts):
    for one in gifts:
        one.wait()
    r.win_out[...] = (r.unit_two[0:128, :] + r.gift_in[0].astype(F32)).T
    r.wout_out[...] = r.d_mid[0:128, :] + r.gift_in[1].astype(F32)
    r.bias_out[...] = r.gift_bias[0:1, 0:128] + r.gift_bias_in[0:1, 128:256]


def remote(source, target, sent, arrived, device):
    return pltpu.make_async_remote_copy(
        src_ref=source,
        dst_ref=target,
        send_sem=sent,
        recv_sem=arrived,
        device_id=device,
        device_id_type=MESH,
    )


class Place:
    def __init__(self):
        self.section = lax.axis_index("section")
        self.me = lax.axis_index("dp")
        self.c = self.me % 2
        self.y = (self.me // 2) % 2
        self.low = (self.me // 4) % 2
        self.high = self.me // 8
        self.across = {"section": 1 - self.section}
        self.core = {"dp": self.me + 1 - 2 * self.c}
        self.beside = {"dp": self.me + 2 - 4 * self.y}
        self.near = {"dp": self.me + 4 - 8 * self.low}
        self.far = {"dp": self.me + 8 - 16 * self.high}
        self.both = {"dp": self.me + 12 - 8 * self.low - 16 * self.high}

    def plane(self, step):
        low = (self.low + step % 2) % 2
        high = (self.high + step // 2) % 2
        return high * 2 + low

    def levels(self):
        return (self.core, self.beside, self.near, self.far)


class Share:
    def __init__(self, r, place, base, sent, arrived):
        self.place, self.base, self.sent, self.arrived = place, base, sent, arrived
        self.buf = r.gather
        self.mine = place.high * 2 + place.low

    def block(self, plane, c):
        return self.buf.at[plane, at(self.base + c * 256, 256)]

    def copy(self, plane, c, number, device):
        block = self.block(plane, c)
        return remote(block, block, self.sent.at[number], self.arrived.at[plane * 2 + c], device)

    def wait(self, plane, c):
        self.copy(plane, c, 0, self.place.core).wait_recv()

    def along(self, plane, number, to_upper):
        device = {"dp": self.place.me + (4 if to_upper else -4)}
        pl.when(self.mine < 3 if to_upper else self.mine > 0)(
            lambda: self.copy(plane, self.place.c, number, device).start()
        )

    def open(self):
        self.along(self.mine, 0, True)
        self.along(self.mine, 1, False)
        self.copy(self.mine, self.place.c, 2 + self.mine, self.place.core).start()

    def pass_on(self, distance):
        for below in (True, False):
            plane = self.mine - distance if below else self.mine + distance

            @pl.when(plane >= 0 if below else plane < 4)
            def _():
                self.wait(plane, self.place.c)
                self.along(plane, 6 + plane, below)
                self.copy(plane, self.place.c, 2 + plane, self.place.core).start()

    def settle(self, plane):
        self.wait(plane, 1 - self.place.c)

    def close(self):
        def done(number):
            self.copy(0, 0, number, self.place.core).wait_send()

        pl.when(self.mine < 3)(lambda: done(0))
        pl.when(self.mine > 0)(lambda: done(1))
        for number in range(2, 6):
            done(number)
        for plane in range(4):
            gone = ((plane < self.mine) & (self.mine < 3)) | ((plane > self.mine) & (self.mine > 0))
            pl.when(gone)(functools.partial(done, 6 + plane))


class Halving:
    def __init__(self, place, source, room, sizes, sent, arrived, done, target=None):
        self.place, self.source, self.room, self.sizes = place, source, room, sizes
        self.sent, self.arrived, self.done, self.target = sent, arrived, done, target
        self.bits = (place.c, place.y, place.low, place.high)

    def takes(self, level):
        if self.target is None or level < 2:
            return None
        on_low = self.place.low == self.target[0]
        return on_low if level == 2 else on_low & (self.place.high == self.target[1])

    def gives(self, level):
        if self.target is None or level < 2:
            return None
        on_low = self.place.low == self.target[0]
        return jnp.logical_not(on_low) if level == 2 else on_low & (self.place.high != self.target[1])

    def when(self, condition, action):
        if condition is None:
            action()
        else:
            pl.when(condition)(action)

    def part(self, j, level, side):
        rows = self.sizes[level]
        start = 0 if self.target is not None and level >= 2 else side * rows
        return self.source(j, start, rows) if level == 0 else self.room(j, level - 1, start, rows)

    def copy(self, j, level):
        give = self.part(j, level, 1 - self.bits[level])
        target = self.room(j, level, 0, self.sizes[level])
        device = self.place.levels()[level]
        return remote(give, target, self.sent.at[j, level], self.arrived.at[j, level], device)

    def begin(self, j, level):
        self.when(self.gives(level), lambda: self.copy(j, level).start())

    def finish(self, j, level):
        self.when(self.takes(level), lambda: self.take(j, level))
        if level < 3:
            self.begin(j, level + 1)

    def take(self, j, level):
        self.copy(j, level).wait_recv()
        mine = self.part(j, level, self.bits[level])
        room = self.room(j, level, 0, self.sizes[level])
        step = 64 if self.sizes[level] % 64 == 0 else 48

        def add(index):
            rows = at(index * step, step)
            total = mine[rows, :].astype(F32) + room[rows, :].astype(F32)
            if level == 3:
                self.done(j, index * step, total)
            else:
                room[rows, :] = total.astype(BF)

        each(self.sizes[level] // step, add)

    def close(self, j):
        for level in range(4):
            self.when(self.gives(level), lambda: self.copy(j, level).wait_send())


class Doubling:
    def __init__(self, place, rows, own, come, sent, arrived):
        self.place, self.rows, self.own, self.come = place, rows, own, come
        self.sent, self.arrived = sent, arrived

    def before(self, level):
        return self.own.at[0 : self.rows] if level == 0 else self.come.at[level - 1, 0 : self.rows]

    def copy(self, level):
        target = self.come.at[level, 0 : self.rows]
        device = self.place.levels()[level]
        return remote(self.before(level), target, self.sent.at[level], self.arrived.at[level], device)

    def begin(self):
        self.copy(0).start()

    def finish(self, level):
        self.copy(level).wait_recv()
        room = self.come.at[level, 0 : self.rows]
        total = self.before(level)[...].astype(F32) + room[...].astype(F32)
        room[...] = total.astype(room.dtype)
        if level < 3:
            self.copy(level + 1).start()

    def close(self):
        for level in range(4):
            self.copy(level).wait_send()


def matrix_sums(r, place, which):
    sums, rooms = r.sums[which], r.matrix_rooms[which]
    starts = (0, 256, 384)

    def room(j, level, start, rows):
        if level == 3:
            return r.last_room.at[at(j * 128 + start, rows)]
        return rooms.at[at(j * 512 + starts[level] + start, rows)]

    def done(j, start, value):
        r.attn_out[at(j * 128 + start, 64), :] = value

    return Halving(
        place,
        lambda j, start, rows: sums.at[at(j * 512 + start, rows)],
        room,
        (256, 128, 128, 128),
        r.sum_sent.at[:, at(which * 4, 4)],
        r.sum_come.at[:, at(which * 4, 4)],
        done,
        (which % 2, which // 2),
    )


def greet(place):
    barrier = pltpu.get_barrier_semaphore()
    devices = (place.across, place.core, place.beside, place.near, place.far, place.both)
    for device in devices:
        pl.semaphore_signal(barrier, inc=1, device_id=device, device_id_type=MESH)
    return lambda: pl.semaphore_wait(barrier, len(devices))


def across(r, place, number, source, target):
    return remote(source, target, r.over_sent.at[number], r.over_come.at[number], place.across)


def front_tail(r, place):
    own = at((place.y * 2 + place.c) * 256, 256)
    high, low = halves(r.small_in[3, 0:16])
    r.fold_sum[0:16, :] = high
    r.fold_sum[16:32, :] = low
    both = nn(r.fold_sum[...], r.attn[1])
    mine = iota((HEADS, D), 1) >> 6 == iota((HEADS, D), 0)
    query = col_sum(jnp.where(mine, both[0:HEADS] + both[HEADS : 2 * HEADS], 0.0))
    r.query_row[0:1, :] = query
    high, low = halves(query)
    row = iota((16, D), 0)
    pair = jnp.where(row == 0, high.astype(F32), jnp.where(row == 1, low.astype(F32), 0.0))
    r.query_pair[...] = pair.astype(BF)

    @pl.when(place.high + place.low == 0)
    def _():
        first = jnp.broadcast_to(r.vecs[0:1, own].astype(F32), (16, 256))
        first = jnp.where(iota((16, 256), 0) < 2, first, 0.0).astype(BF)
        r.attn_out[...] = tn(first, r.query_pair[...])
        r.vec_out[...] = col_sum(nt(r.query_pair[...], r.attn[0, own, :]))

    @pl.when((place.high == 0) & (place.low == 1))
    def _():
        left = jnp.concatenate([r.fold_sum[0:16, own], r.fold_sum[16:32, own], r.fold_sum[0:16, own]], axis=0)
        right = jnp.concatenate([r.qhead[0:16, :], r.qhead[0:16, :], r.qhead[16:32, :]], axis=0)
        r.attn_out[...] = tn(left, right)
        r.vec_out[...] = r.query_row[0:1, own]

    @pl.when(place.high == 1)
    def _():
        r.vec_out[...] = r.small_in[3, pl.ds(16 + place.low, 1), own]


def front_section(r, place):
    def load(number, source, target):
        return pltpu.make_async_copy(source, target, r.loads.at[number])

    cots = Share(r, place, 512, r.cot_sent, r.cot_come)
    hiddens = Share(r, place, 0, r.x_sent, r.x_come)
    mine = hiddens.mine
    loads = [
        load(0, r.patches_in.at[0], r.pix.at[0:128]),
        load(1, r.patches_in.at[1], r.pix.at[128:256]),
        load(2, r.weight_in, r.raw),
        load(7, r.cot_in.at[0], cots.block(mine, place.c).at[0:128]),
        load(8, r.cot_in.at[1], cots.block(mine, place.c).at[128:256]),
        load(3, r.attn_in.at[0, 0], r.attn.at[0]),
        load(4, r.attn_in.at[0, 1], r.attn.at[1]),
        load(5, r.attn_in.at[0, 2], r.attn.at[2]),
        load(6, r.attn_in.at[0, 3], r.attn.at[3]),
    ]
    units = hidden_loads(r, place, load)
    met = greet(place)
    for one in loads + units:
        one.start()
    r.small[16:24, :] = jnp.zeros((8, D), F32)
    for one in loads[0:3]:
        one.wait()
    front_tables(r)
    loads[3].wait()
    loads[4].wait()
    met()
    cots.open()
    loads[5].wait()
    loads[6].wait()
    front_query(r)
    loads[7].wait()
    front_values(r)
    loads[8].wait()
    send_front = []
    for sample in range(2):
        front_forward(r, r.act_out, sample)
        rows = slice(sample * 128, sample * 128 + 128)
        send_front.append(across(r, place, (0, 3)[sample], r.act_out.at[rows], r.arrive.at[rows]))
        send_front[sample].start()
    cots.pass_on(1)
    for one in units:
        one.wait()
    hidden_tables(r, place)
    for distance in range(2, 4):
        cots.pass_on(distance)
    for plane in range(4):
        cots.settle(plane)
    near = mine + 1 - 2 * place.low
    far = mine + 2 - 4 * place.high
    both = 3 - mine

    def patch_done(j, start, value):
        r.patch_out[...] = value[0:24]
        r.gift_patch[...] = value[24:48]

    values, outs = matrix_sums(r, place, 2), matrix_sums(r, place, 3)
    patch_starts = (0, 384, 576, 672)
    pixels = Halving(
        place,
        lambda j, start, rows: r.patch_sum.at[at(start, rows)],
        lambda j, level, start, rows: r.patch_rooms.at[at(patch_starts[level] + start, rows)],
        (384, 192, 96, 48),
        r.patch_sent,
        r.patch_come,
        patch_done,
    )
    smalls = Doubling(place, 24, r.small, r.small_in, r.small_sent, r.small_come)
    embeds = Doubling(place, 48, r.var_sum, r.var_in, r.var_sent, r.var_come)
    gifts = hidden_gifts(r, place)
    give_half = across(r, place, 2, r.gift_half, r.gift_half)
    give_patch = across(r, place, 6, r.gift_patch, r.gift_patch)
    give_var = across(r, place, 5, r.var_in.at[3], r.gift_var)

    def cells():
        hiddens.wait(mine, place.c)
        hiddens.open()

    def plane(which):
        hiddens.settle(which)
        hidden_plane(r, which)

    def come(sample):
        rows = slice(sample * 128, sample * 128 + 128)
        across(r, place, (1, 4)[sample], r.leave.at[rows], r.arrive.at[rows]).wait_recv()

    def back_out():
        front_back_out(r, r.arrive)
        outs.begin(0, 0)
        outs.begin(1, 0)

    def projection():
        front_back_projection(r)
        values.begin(0, 0)
        values.begin(1, 0)

    def table():
        front_back_table(r)
        smalls.begin()

    def pixel_rows():
        front_back_pixels(r)
        embeds.begin()

    def order():
        front_back_order(r)
        pixels.begin(0, 0)

    def inputs():
        front_back_inputs(r, r.input_out, r.gift_half)
        give_half.start()

    def patch_last():
        pixels.finish(0, 3)
        give_patch.start()

    def var_last():
        embeds.finish(3)
        give_var.start()

    t = types.SimpleNamespace(
        cells=cells,
        own=lambda: plane(mine),
        pass1=lambda: hiddens.pass_on(1),
        near=lambda: plane(near),
        come0=lambda: come(0),
        come1=lambda: come(1),
        back_out=back_out,
        back_values0=lambda: front_back_values(r, r.arrive, 0),
        back_values1=lambda: front_back_values(r, r.arrive, 1),
        pass2=lambda: hiddens.pass_on(2),
        heads0=lambda: front_back_heads(r, 0),
        heads1=lambda: front_back_heads(r, 1),
        table=table,
        projection=projection,
        pass3=lambda: hiddens.pass_on(3),
        pixel_rows=pixel_rows,
        order=order,
        inputs=inputs,
        far=lambda: plane(far),
        both=lambda: plane(both),
        exchange=lambda: hidden_exchange(r, gifts),
        small0=lambda: smalls.finish(0),
        small1=lambda: smalls.finish(1),
        small2=lambda: smalls.finish(2),
        small3=lambda: smalls.finish(3),
        tail=lambda: front_tail(r, place),
        embed0=lambda: embeds.finish(0),
        embed1=lambda: embeds.finish(1),
        embed2=lambda: embeds.finish(2),
        embed3=var_last,
        patch0=lambda: pixels.finish(0, 0),
        patch1=lambda: pixels.finish(0, 1),
        patch2=lambda: pixels.finish(0, 2),
        patch3=patch_last,
        a00=lambda: outs.finish(0, 0),
        a01=lambda: outs.finish(0, 1),
        a02=lambda: outs.finish(0, 2),
        a03=lambda: outs.finish(0, 3),
        a10=lambda: outs.finish(1, 0),
        a11=lambda: outs.finish(1, 1),
        a12=lambda: outs.finish(1, 2),
        a13=lambda: outs.finish(1, 3),
        v00=lambda: values.finish(0, 0),
        v01=lambda: values.finish(0, 1),
        v02=lambda: values.finish(0, 2),
        v03=lambda: values.finish(0, 3),
        v10=lambda: values.finish(1, 0),
        v11=lambda: values.finish(1, 1),
        v12=lambda: values.finish(1, 2),
        v13=lambda: values.finish(1, 3),
    )
    t.cells()
    t.come0()
    t.back_values0()
    t.pass1()
    t.heads0()
    t.come1()
    t.back_out()
    t.back_values1()
    t.a10()
    t.a00()
    t.pass2()
    t.heads1()
    t.table()
    t.projection()
    t.a01()
    t.small0()
    t.pixel_rows()
    t.pass3()
    t.v00()
    t.small1()
    t.a02()
    t.order()
    t.embed0()
    t.inputs()
    t.patch0()
    t.a11()
    t.small2()
    t.embed1()
    t.near()
    t.a12()
    t.v01()
    t.small3()
    t.own()
    t.far()
    t.v10()
    t.patch1()
    t.both()
    t.v02()
    t.exchange()
    t.v11()
    t.patch2()
    t.a03()
    t.embed2()
    t.tail()
    t.patch3()
    t.v03()
    t.v12()
    t.embed3()
    t.v13()
    t.a13()
    give_attn = load(13, r.attn_out, r.attn_final)
    give_attn.start()
    r.var_out[...] = r.var_in[3].astype(F32)
    hidden_finish(r, gifts)
    across(r, place, 7, r.small_in.at[3, 0:16], r.gift_small).wait_recv()
    r.gain_out[...] = r.gift_small[4:6, :]
    r.shift_out[...] = r.gift_small[6:9, :]
    cots.close()
    hiddens.close()
    for j in range(2):
        values.close(j)
        outs.close(j)
    pixels.close(0)
    smalls.close()
    embeds.close()
    for one in (*send_front, give_half, give_var, give_patch):
        one.wait_send()
    give_attn.wait()


def trunk_section(r, place):
    def load(number, source, target):
        return pltpu.make_async_copy(source, target, r.loads.at[number])

    cots = Share(r, place, 512, r.cot_sent, r.cot_come)
    hiddens = Share(r, place, 0, r.x_sent, r.x_come)
    mine = hiddens.mine
    r.cot = cots.block(mine, place.c)
    r.x_own = hiddens.block(mine, place.c)
    given = [load(4 + n, r.cot_in.at[n], r.cot.at[n * 128 : (n + 1) * 128]) for n in range(2)]
    outs = [load(n, r.mlp_out.at[n * 1024 : (n + 1) * 1024], r.bufs.at[4096 + n * 1024 : 5120 + n * 1024]) for n in range(4)]
    attns = [load(6 + n, r.attn_in.at[0, n], r.attn.at[n]) for n in range(4)]
    ins = [load(10 + n, r.mlp_in.at[:, n * 1024 : (n + 1) * 1024], r.bufs.at[n * 1024 : (n + 1) * 1024]) for n in range(4)]
    met = greet(place)
    for one in (*given, *outs, *attns, *ins):
        one.start()
    met()
    r.small[...] = jnp.zeros((24, D), F32)
    for one in given:
        one.wait()
    cots.open()
    for one in outs:
        one.wait()
    trunk_ahead(r)
    for one in (*attns, *ins):
        one.wait()
    cots.pass_on(1)
    for sample in range(2):
        rows = slice(sample * 128, sample * 128 + 128)
        across(r, place, (0, 3)[sample], r.act_out.at[rows], r.arrive.at[rows]).wait_recv()
    send_x = remote(r.x_own, r.x_own, r.over_sent.at[0], r.x_come.at[mine * 2 + place.c], place.across)
    halves_of = [slice(sample * 128, sample * 128 + 128) for sample in range(2)]
    send_in = [
        across(r, place, number, r.leave.at[rows], r.arrive.at[rows]) for number, rows in zip((1, 4), halves_of)
    ]
    send_small = across(r, place, 7, r.small_in.at[3, 0:16], r.gift_small)
    near = mine + 1 - 2 * place.low
    far = mine + 2 - 4 * place.high
    both = 3 - mine
    sums = [matrix_sums(r, place, which) for which in range(4)]
    queries, keys, values, outs_sum = sums
    smalls = Doubling(place, 24, r.small, r.small_in, r.small_sent, r.small_come)
    gifts = hidden_gifts(r, place)
    units = hidden_loads(r, place, load)

    def tell(ready):
        for level, device in enumerate(place.levels()):
            pl.semaphore_signal(ready.at[level], inc=1, device_id=device, device_id_type=MESH)

    def heed(ready):
        for level in range(4):
            pl.semaphore_wait(ready.at[level], 1)

    def attention():
        trunk_attention(r, r.arrive)
        send_x.start()
        hiddens.open()

    def hidden():
        trunk_hidden(r)
        tell(r.ready)

    def weight_out():
        trunk_weight_out(r)
        heed(r.ready)
        outs_sum.begin(0, 0)
        outs_sum.begin(1, 0)

    def back_in(sample):
        trunk_back_in(r, r.leave, sample)
        send_in[sample].start()
        if sample == 1:
            smalls.begin()

    def out():
        trunk_out(r, r.act_out)
        tell(r.ready_two)

    def weights(which):
        trunk_weights(r, which)
        if which == 2:
            heed(r.ready_two)
        sums[which].begin(0, 0)
        sums[which].begin(1, 0)

    def tables():
        for one in units:
            one.start()
        for one in units:
            one.wait()
        hidden_tables(r, place)

    def plane(which):
        cots.settle(which)
        hiddens.settle(which)
        hidden_plane(r, which)

    def small_last():
        smalls.finish(3)
        send_small.start()

    t = types.SimpleNamespace(
        attention=attention,
        cot2=lambda: cots.pass_on(2),
        hidden=hidden,
        cot3=lambda: cots.pass_on(3),
        back=lambda: trunk_back(r),
        weight_out=weight_out,
        pass1=lambda: hiddens.pass_on(1),
        mix=lambda: trunk_mix(r),
        back_heads0=lambda: trunk_back_heads(r, 0),
        back_heads1=lambda: trunk_back_heads(r, 1),
        back_in0=lambda: back_in(0),
        back_in1=lambda: back_in(1),
        pass2=lambda: hiddens.pass_on(2),
        out=out,
        turn=lambda: trunk_turn(r),
        weight_v=lambda: weights(2),
        weight_k=lambda: weights(1),
        weight_q=lambda: weights(0),
        tables=tables,
        own=lambda: plane(mine),
        near=lambda: plane(near),
        pass3=lambda: hiddens.pass_on(3),
        far=lambda: plane(far),
        both=lambda: plane(both),
        exchange=lambda: hidden_exchange(r, gifts),
        small0=lambda: smalls.finish(0),
        small1=lambda: smalls.finish(1),
        small2=lambda: smalls.finish(2),
        small3=small_last,
        a00=lambda: outs_sum.finish(0, 0),
        a01=lambda: outs_sum.finish(0, 1),
        a02=lambda: outs_sum.finish(0, 2),
        a03=lambda: outs_sum.finish(0, 3),
        a10=lambda: outs_sum.finish(1, 0),
        a11=lambda: outs_sum.finish(1, 1),
        a12=lambda: outs_sum.finish(1, 2),
        a13=lambda: outs_sum.finish(1, 3),
        v00=lambda: values.finish(0, 0),
        v01=lambda: values.finish(0, 1),
        v02=lambda: values.finish(0, 2),
        v03=lambda: values.finish(0, 3),
        v10=lambda: values.finish(1, 0),
        v11=lambda: values.finish(1, 1),
        v12=lambda: values.finish(1, 2),
        v13=lambda: values.finish(1, 3),
        k00=lambda: keys.finish(0, 0),
        k01=lambda: keys.finish(0, 1),
        k02=lambda: keys.finish(0, 2),
        k03=lambda: keys.finish(0, 3),
        k10=lambda: keys.finish(1, 0),
        k11=lambda: keys.finish(1, 1),
        k12=lambda: keys.finish(1, 2),
        k13=lambda: keys.finish(1, 3),
        q00=lambda: queries.finish(0, 0),
        q01=lambda: queries.finish(0, 1),
        q02=lambda: queries.finish(0, 2),
        q03=lambda: queries.finish(0, 3),
        q10=lambda: queries.finish(1, 0),
        q11=lambda: queries.finish(1, 1),
        q12=lambda: queries.finish(1, 2),
        q13=lambda: queries.finish(1, 3),
    )
    t.attention()
    t.turn()
    t.cot2()
    t.hidden()
    t.back()
    t.mix()
    t.back_heads0()
    t.back_in0()
    t.weight_out()
    t.back_heads1()
    t.pass1()
    t.back_in1()
    t.a00()
    t.out()
    t.a10()
    t.a01()
    t.weight_v()
    t.cot3()
    t.weight_q()
    t.q00()
    t.pass2()
    t.v10()
    t.weight_k()
    t.tables()
    t.a11()
    t.far()
    t.pass3()
    t.q01()
    t.k10()
    t.small0()
    t.v00()
    t.k00()
    t.both()
    t.a02()
    t.k11()
    t.v11()
    t.own()
    t.small1()
    t.q02()
    t.near()
    t.q10()
    t.v01()
    t.a03()
    t.small2()
    t.k01()
    t.q11()
    t.a12()
    t.exchange()
    t.small3()
    t.k02()
    t.v12()
    t.v02()
    t.a13()
    t.q12()
    t.k12()
    t.v13()
    t.k03()
    t.v03()
    t.k13()
    t.q03()
    t.q13()
    own = at((place.y * 2 + place.c) * 256, 256)
    r.vec_out[...] = r.small_in[3, pl.ds(mine, 1), own]
    r.gain_out[...] = r.small_in[3, 4:6]
    r.shift_out[...] = r.small_in[3, 6:9]
    give_attn = load(14, r.attn_out, r.attn_final)
    give_attn.start()
    hidden_finish(r, gifts)
    across(r, place, 2, r.gift_half, r.gift_half).wait_recv()
    r.input_out[...] = r.gift_half[...].astype(F32)
    across(r, place, 5, r.var_in.at[3], r.gift_var).wait_recv()
    r.var_out[...] = r.gift_var[...].astype(F32)
    across(r, place, 6, r.gift_patch, r.gift_patch).wait_recv()
    r.patch_out[...] = r.gift_patch[...]
    cots.close()
    hiddens.close()
    for one in sums:
        for j in range(2):
            one.close(j)
    smalls.close()
    for one in (send_x, *send_in, send_small):
        one.wait_send()
    give_attn.wait()


CELL_ROWS = (CELLS, D)
SCRATCH = dict(
    attn=((4, D, D), BF),
    bufs=((8 * D, D), BF),
    gather=((4, D, D), BF),
    last_room=((256, D), BF),
    grads_flat=((2 * D, D), BF),
    turned=((D, WIDE), BF),
    pat=((CELLS, WIDE), BF),
    qhead=((32, D), BF),
    fold=((16, D), BF),
    fold_sum=((32, D), BF),
    query_pair=((16, D), BF),
    query_row=((8, D), F32),
    score=((16, WIDE), F32),
    uses=((16, 1, WIDE), F32),
    probs=((32, 128, 128), F32),
    resid=(CELL_ROWS, F32),
    unit_one=(CELL_ROWS, F32),
    unit_two=(CELL_ROWS, F32),
    d_mid=(CELL_ROWS, F32),
    rstd_one=((CELLS, LANES), F32),
    rstd_two=((CELLS, LANES), F32),
    normed=(CELL_ROWS, BF),
    k=(CELL_ROWS, BF),
    v=(CELL_ROWS, BF),
    mixed=(CELL_ROWS, BF),
    d_low=(CELL_ROWS, BF),
    arrive=(CELL_ROWS, BF),
    turn_a=((D, CELLS), BF),
    turn_b=((D, CELLS), BF),
    small=((24, D), F32),
    small_in=((4, 24, D), F32),
    var_sum=((48, D), BF),
    var_in=((4, 48, D), BF),
    gift=((2, 128, D), BF),
    gift_in=((2, 128, D), BF),
    gift_bias=((8, 256), F32),
    gift_bias_in=((8, 256), F32),
    gift_var=((48, D), BF),
    gift_small=((16, D), F32),
    gift_patch=((24, D), F32),
    gift_half=((CELLS, 384), BF),
)
SEMAPHORES = dict(
    loads=(19,),
    over_sent=(8,),
    over_come=(8,),
    cot_sent=(10,),
    cot_come=(8,),
    x_sent=(10,),
    x_come=(8,),
    var_sent=(4,),
    var_come=(4,),
    gift_sent=(2,),
    gift_come=(2,),
    sum_sent=(2, 16),
    sum_come=(2, 16),
    patch_sent=(1, 4),
    patch_come=(1, 4),
    small_sent=(4,),
    small_come=(4,),
)
INPUTS = dict(
    patches_in=pl.ANY,
    masks=pltpu.VMEM,
    leads=pltpu.SMEM,
    cot_in=pl.ANY,
    weight_in=pl.ANY,
    embed=pltpu.VMEM,
    attn_in=pl.ANY,
    vecs=pltpu.VMEM,
    gains=pltpu.VMEM,
    shifts=pltpu.VMEM,
    mlp_in=pl.ANY,
    bias_in=pltpu.VMEM,
    mlp_out=pl.ANY,
)
OUTPUTS = dict(
    act_out=(CELL_ROWS, BF),
    input_out=((CELLS, 384), F32),
    patch_out=((24, D), F32),
    var_out=((48, D), F32),
    attn_final=(CELL_ROWS, F32),
    vec_out=((1, 256), F32),
    gain_out=((2, D), F32),
    shift_out=((3, D), F32),
    win_out=((D, 128), F32),
    bias_out=((1, 128), F32),
    wout_out=((128, D), F32),
)


class Refs:
    pass


def fused_kernel(*refs):
    r = Refs()
    names = list(INPUTS) + list(OUTPUTS) + list(SCRATCH) + list(SEMAPHORES) + ["ready", "ready_two"]
    for name, ref in zip(names, refs, strict=True):
        setattr(r, name, ref)
    r.table = r.bufs.at[0:WIDE]
    r.mid = r.bufs.at[WIDE : 2 * WIDE]
    r.patch_rooms = r.bufs.at[4352:5072]
    r.patch_sum = r.table.at[0:768]
    r.raw = r.turned.at[0:768, 0:D]
    for number, name in enumerate(("q", "second", "leave")):
        setattr(r, name, r.turned.at[number * 256 : number * 256 + 256, 0:D])
    r.pix = r.normed.at[:, 0 : V * PIX]
    r.input_sum = r.resid
    r.attn_out = r.resid
    r.agg = r.mixed
    r.dlow = r.d_low
    r.wout = r.k
    r.win_t = r.v
    r.win = r.turn_a
    r.keep = r.rstd_one
    r.units = r.unit_one.at[:, 0:256]
    r.bias_sum = r.unit_one.at[:, 256:512]
    place = Place()

    @pl.when(place.section == 0)
    def _():
        r.sums = (None, None, r.grads_flat.at[0:D], r.grads_flat.at[D : 2 * D])
        r.matrix_rooms = (None, None, r.bufs.at[2304:3328], r.bufs.at[3328:4352])
        front_section(r, place)

    @pl.when(place.section == 1)
    def _():
        r.sums = tuple(r.bufs.at[at(start, D)] for start in (2 * D, 3 * D, 4 * D, 0))
        r.matrix_rooms = tuple(r.bufs.at[at(start, D)] for start in (5 * D, 6 * D, 7 * D, D))
        trunk_section(r, place)


def hand_on(*refs):
    count = len(OUTPUTS)
    given, taken, rooms = (refs[count * part : count * (part + 1)] for part in range(3))
    sems = refs[3 * count]
    ins = [pltpu.make_async_copy(given[n], rooms[n], sems.at[0, n]) for n in range(count)]
    outs = [pltpu.make_async_copy(rooms[n], taken[n], sems.at[1, n]) for n in range(count)]
    for one in ins:
        one.start()
    for first, then in zip(ins, outs):
        first.wait()
        then.start()
    for one in outs:
        one.wait()


def fused_shards(
    patches,
    masks,
    lead_times,
    cotangent,
    patch_weight,
    var_embed,
    attention,
    attn_vectors,
    norm_gains,
    trunk_shifts,
    mlp_in,
    mlp_in_bias,
    mlp_out,
):
    outs = pl.pallas_call(
        fused_kernel,
        in_specs=[pl.BlockSpec(memory_space=space) for space in INPUTS.values()],
        out_specs=[
            pl.BlockSpec(memory_space=pl.ANY if one == (CELL_ROWS, F32) else pltpu.VMEM)
            for one in OUTPUTS.values()
        ],
        out_shape=[jax.ShapeDtypeStruct(*one) for one in OUTPUTS.values()],
        scratch_shapes=[pltpu.VMEM(*one) for one in SCRATCH.values()]
        + [pltpu.SemaphoreType.DMA(one) for one in SEMAPHORES.values()]
        + [pltpu.SemaphoreType.REGULAR((4,))] * 2,
        compiler_params=pltpu.CompilerParams(
            collective_id=0, has_side_effects=True, vmem_limit_bytes=60 * 2**20
        ),
    )(
        patches,
        masks,
        lead_times,
        cotangent,
        patch_weight,
        var_embed,
        attention,
        attn_vectors[0],
        norm_gains,
        trunk_shifts,
        mlp_in,
        mlp_in_bias,
        mlp_out,
    )
    outs = pl.pallas_call(
        hand_on,
        in_specs=[pl.BlockSpec(memory_space=pl.ANY)] * len(outs),
        out_specs=[pl.BlockSpec(memory_space=pl.ANY)] * len(outs),
        out_shape=[jax.ShapeDtypeStruct(*one) for one in OUTPUTS.values()],
        scratch_shapes=[pltpu.VMEM(*one) for one in OUTPUTS.values()]
        + [pltpu.SemaphoreType.DMA((2, len(outs)))],
    )(*outs)
    act, inputs, patch, var, attn, vec, gain, shift, win, bias, wout = outs
    return (
        act.reshape(1, 2, 128, D),
        inputs.reshape(2, 128, 384),
        patch,
        var,
        attn[None],
        vec,
        gain,
        shift,
        win,
        bias.reshape(128),
        wout,
    )


def solution(mesh):
    in_specs = (
        P("dp", None, None),
        P("dp", None, None),
        P("dp"),
        P("dp", None, None),
        P(),
        P(),
        P("section", None, None, None),
        P("section", None, None),
        P(),
        P(),
        P(),
        P(),
        P(),
    )
    out_specs = (
        P("section", "dp", None, None),
        P("dp", None, "section"),
        P(("section", "dp"), None),
        P(),
        P("section", "dp", None),
        P("section", "dp"),
        P(),
        P(),
        P(None, ("section", "dp")),
        P(("section", "dp")),
        P(("section", "dp"), None),
    )
    small = mesh.shape["section"] == 2 and mesh.shape["dp"] == 16
    body = fused_shards if small else shards
    return jax.shard_map(body, mesh=mesh, in_specs=in_specs, out_specs=out_specs, check_vma=False)
```
